32 devices in a mesh: dp: 8 (over y, x, core), mp: 4 (over z).
Axes of the slice: x: 2, y: 2, z: 4, core: 2. Of those that a mesh axis runs over, the one named last changes fastest.
Arguments:
- inputs: bfloat16 [8, 1024, 1536], P('dp'), may hold values from -6 to 6
- lengths: int32 [8, 4], P('dp'), may hold values from 0 to 1024, as said below
- q_weight: bfloat16 [1536, 1536], P(None, 'mp'), may hold values from -0.3125 to 0.3125
- k_weight: bfloat16 [1536, 768], P(None, 'mp'), may hold values from -0.15625 to 0.15625
- v_weight: bfloat16 [1536, 768], P(None, 'mp'), may hold values from -0.15625 to 0.15625
- o_weight: bfloat16 [1536, 1536], P('mp'), may hold values from -0.625 to 0.625
- gate_weight: bfloat16 [1536, 4096], P(None, 'mp'), may hold values from -0.15625 to 0.15625
- up_weight: bfloat16 [1536, 4096], P(None, 'mp'), may hold values from -0.15625 to 0.15625
- down_weight: bfloat16 [4096, 1536], P('mp'), may hold values from -0.09375 to 0.09375
- attn_gain: bfloat16 [1536], replicated, may hold values from 0.5 to 1.5
- mlp_gain: bfloat16 [1536], replicated, may hold values from 0.5 to 1.5
- cotangent: bfloat16 [8, 1024, 1536], P('dp'), may hold values from -6 to 6
Outputs:
- output: bfloat16 [8, 1024, 1536], P('dp')
- input_grad: bfloat16 [8, 1024, 1536], P('dp')
- q_grad: float32 [1536, 1536], P('dp', 'mp')
- k_grad: float32 [1536, 768], P('dp', 'mp')
- v_grad: float32 [1536, 768], P('dp', 'mp')
- o_grad: float32 [1536, 1536], P('mp', 'dp')
- gate_grad: float32 [1536, 4096], P('dp', 'mp')
- up_grad: float32 [1536, 4096], P('dp', 'mp')
- down_grad: float32 [4096, 1536], P('mp', 'dp')
- attn_gain_grad: float32 [1536], P('dp')
- mlp_gain_grad: float32 [1536], P('dp')
The draws below stay inside these ranges and needn't reach their ends.
Inputs may be any that keep to these rules, and one draw needn't show every extreme that they name: Each row's 4 lengths sum to 1024 (a length may be 0); in every draw at least a quarter of the rows hold a single sequence of 1024 tokens.
All inputs are finite; a program needn't handle non-finite values.
Results may differ from the reference program's by a relative error of at most 0.023.
Values may be sent and summed in bfloat16 or wider, within the bound.
A program may use at most 192 MiB of HBM per device.

```python
import jax
import jax.numpy as jnp
from jax import lax

D = 1536
HQ = 16
HK = 8
HD = 96
FF = 4096
ROW = 1024
SEGS = 4
BATCH = 8
N_MP = 4


def draw_lengths(key, part):
    key = jax.random.fold_in(key, 7)
    cut_key, shift_key = jax.random.split(key)
    cuts = jnp.sort(jax.random.randint(cut_key, (BATCH, SEGS - 1), 0, ROW + 1), axis=1)
    edges = jnp.concatenate([jnp.zeros((BATCH, 1), jnp.int32), cuts.astype(jnp.int32), jnp.full((BATCH, 1), ROW, jnp.int32)], axis=1)
    pieces = edges[:, 1:] - edges[:, :-1]
    shift = jax.random.randint(shift_key, (), 0, 4)
    single = (jnp.arange(BATCH, dtype=jnp.int32) + shift) % 4 == 0
    whole = jnp.where(jnp.arange(SEGS, dtype=jnp.int32) == 0, ROW, 0).astype(jnp.int32)
    return jnp.where(single[:, None], whole[None, :], pieces).astype(jnp.int32)


def spiked(values, stream_key, source, target, parts, factor):
    def block_of(dim):
        return (jnp.arange(values.shape[dim]) // (values.shape[dim] // parts)).reshape((-1,) + (1,) * (values.ndim - 1 - dim))

    one_side = jax.random.permutation(stream_key, parts)[block_of(target)]
    second = (block_of(target) + parts // 2) % parts
    return jnp.where((block_of(source) == one_side) | (block_of(source) == second), factor * values, values)


def levels(own_key, extent, shards, low, largest):
    level, own = 1.0, jax.random.fold_in(own_key, 6)
    for position, shards_of in shards:
        steps = jnp.exp(jax.random.uniform(jax.random.fold_in(own, position), (shards_of,), jnp.float32, low / len(shards), largest / len(shards)))
        level = level * jnp.repeat(steps, extent[position] // shards_of).reshape([-1 if axis == position else 1 for axis in range(len(extent))])
    return level


def gaussian(own_key, shape, spread, reach, cuts=(), kind=jnp.bfloat16):
    loudness = levels(own_key, shape, cuts, -0.22, 0.18) if cuts else 1.0
    entries = jax.random.normal(own_key, shape, jnp.float32) * spread * loudness
    return jnp.minimum(jnp.maximum(entries, -reach), reach).astype(kind)


def heavy_noise(own_key, shape, spread, limit, cuts, heavy, kind=jnp.bfloat16):
    values = spread * jax.random.normal(own_key, shape, jnp.float32)
    if cuts:
        values = values * levels(own_key, shape, cuts, -0.22, 0.18)
    return jnp.clip(spiked(values, jax.random.fold_in(own_key, 3), *heavy), -limit, limit).astype(kind)


def setup_inputs(seed: int = 0) -> dict:
    seeds = jax.random.split(jax.random.key(seed), 13)
    inputs = gaussian(seeds[0], (BATCH, ROW, D), 1.0, 6.0, ((0, 8),))
    lengths = draw_lengths(jax.random.fold_in(seeds[12], 71), 0)
    q_weight = gaussian(seeds[2], (D, HQ * HD), (D // 4) ** -0.5, 0.3125, ((1, 4),))
    k_weight = gaussian(seeds[3], (D, HK * HD), D ** -0.5, 0.15625, ((1, 4),))
    v_weight = gaussian(seeds[4], (D, HK * HD), D ** -0.5, 0.15625, ((1, 4),))
    o_weight = gaussian(seeds[5], (HQ * HD, D), (HQ * HD // 16) ** -0.5, 0.625, ((0, 4),))
    gate_weight = gaussian(seeds[6], (D, FF), D ** -0.5, 0.15625, ((1, 4),))
    up_weight = gaussian(seeds[7], (D, FF), D ** -0.5, 0.15625, ((1, 4),))
    down_weight = gaussian(seeds[8], (FF, D), FF ** -0.5, 0.09375, ((0, 4),))
    attn_gain = jnp.clip(1.0 + 0.1 * jax.random.normal(seeds[9], (D,), jnp.float32), 0.5, 1.5).astype(jnp.bfloat16)
    mlp_gain = jnp.clip(1.0 + 0.1 * jax.random.normal(seeds[10], (D,), jnp.float32), 0.5, 1.5).astype(jnp.bfloat16)
    cotangent = heavy_noise(seeds[11], (BATCH, ROW, D), 1.0, 6.0, ((0, 8),), (0, 2, 8, 2.0))
    return dict(inputs=inputs, lengths=lengths, q_weight=q_weight, k_weight=k_weight, v_weight=v_weight, o_weight=o_weight, gate_weight=gate_weight, up_weight=up_weight, down_weight=down_weight, attn_gain=attn_gain, mlp_gain=mlp_gain, cotangent=cotangent)


eps = 1e-05
rope_base = 100000.0
highest = lax.Precision.HIGHEST

@jax.custom_vjp
def low(v):
    return lax.optimization_barrier(v.astype(jnp.bfloat16)).astype(jnp.float32)

@jax.custom_vjp
def low_back(v):
    return v

def low_keep(v):
    return (low(v), None)

def low_pass(kept, grad):
    return (grad,)

def back_keep(v):
    return (v, None)

def back_low(kept, grad):
    return (low(grad),)
low.defvjp(low_keep, low_pass)
low_back.defvjp(back_keep, back_low)

def layout(lengths):
    finish = jnp.cumsum(lengths, axis=1)
    starts = finish - lengths
    places = jnp.arange(ROW, dtype=jnp.int32)
    segment = lax.optimization_barrier(jnp.sum((places[None, :, None] >= finish[:, None, :]).astype(jnp.int32), axis=2))
    chosen = segment[:, :, None] == jnp.arange(SEGS, dtype=jnp.int32)[None, None, :]
    offsets = lax.optimization_barrier(jnp.sum(jnp.where(chosen, starts[:, None, :], 0), axis=2))
    return (segment, places[None, :] - offsets)

def angles_of(positions):
    freqs = rope_base ** (-(jnp.arange(HD // 2, dtype=jnp.float32) * 2.0) / HD)
    angles = positions.astype(jnp.float32)[..., None] * freqs
    return (jnp.cos(angles), jnp.sin(angles))

def rotate(tensor, cosine, sine):
    middle = tensor.shape[-1] // 2
    leading = tensor[..., :middle]
    trailing = tensor[..., middle:]
    cos_wide = cosine[..., None, :]
    sin_wide = sine[..., None, :]
    return jnp.concatenate([leading * cos_wide - trailing * sin_wide, trailing * cos_wide + leading * sin_wide], axis=-1)

def normalize(tensor, gain):
    factor = lax.rsqrt(lax.optimization_barrier(jnp.mean(tensor * tensor, axis=-1, keepdims=True)) + eps)
    return tensor * factor * gain

def attend_row(pieces):
    queries, keys, values, segment = pieces
    block = min(512, ROW)
    outputs = []
    for begin in range(0, ROW, block):
        stop = begin + block
        key_rows = jnp.repeat(keys[:stop], HQ // HK, axis=1)
        value_rows = jnp.repeat(values[:stop], HQ // HK, axis=1)
        scores = jnp.einsum('qhe,khe->hqk', queries[begin:stop], key_rows, precision=highest) * HD ** (-0.5)
        scores = low_back(scores)
        rows_here = begin + jnp.arange(block, dtype=jnp.int32)
        columns = jnp.arange(stop, dtype=jnp.int32)
        allowed = (segment[begin:stop][:, None] == segment[:stop][None, :]) & (columns[None, :] <= rows_here[:, None])
        masked = jnp.where(allowed[None], scores, -1e+30)
        top = lax.optimization_barrier(jnp.max(masked, axis=-1, keepdims=True))
        weights = jnp.exp(masked - top)
        probs = low(weights / lax.optimization_barrier(jnp.sum(weights, axis=-1, keepdims=True)))
        outputs.append(jnp.einsum('hqk,khe->qhe', probs, value_rows, precision=highest))
    return jnp.concatenate(outputs, axis=0)

def forward(inputs, q_weight, k_weight, v_weight, o_weight, gate_weight, up_weight, down_weight, attn_gain, mlp_gain, segment, cosine, sine):
    batch = inputs.shape[0]
    q_cols = HQ * HD // N_MP
    kv_cols = HK * HD // N_MP
    ff_cols = FF // N_MP
    hidden = low(normalize(inputs, attn_gain))
    q_parts = []
    k_parts = []
    v_parts = []
    for group in range(N_MP):
        local = low_back(hidden)
        q_parts.append(low_back(jnp.dot(local, q_weight[:, group * q_cols:(group + 1) * q_cols], precision=highest)))
        k_parts.append(low_back(jnp.dot(local, k_weight[:, group * kv_cols:(group + 1) * kv_cols], precision=highest)))
        v_parts.append(low_back(jnp.dot(local, v_weight[:, group * kv_cols:(group + 1) * kv_cols], precision=highest)))
    queries = low(rotate(jnp.concatenate(q_parts, axis=-1).reshape(batch, ROW, HQ, HD), cosine, sine))
    keys = low(rotate(jnp.concatenate(k_parts, axis=-1).reshape(batch, ROW, HK, HD), cosine, sine))
    values = low(jnp.concatenate(v_parts, axis=-1).reshape(batch, ROW, HK, HD))
    heads_out = lax.map(jax.checkpoint(attend_row), (queries, keys, values, segment))
    heads_out = low(low_back(heads_out.reshape(batch, ROW, HQ * HD)))
    attn_out = jnp.zeros_like(inputs)
    for group in range(N_MP):
        term = jnp.dot(heads_out[..., group * q_cols:(group + 1) * q_cols], o_weight[group * q_cols:(group + 1) * q_cols], precision=highest)
        attn_out = attn_out + low(low_back(term))
    mid = inputs + attn_out
    hidden2 = low(normalize(mid, mlp_gain))
    mlp_out = jnp.zeros_like(inputs)
    for group in range(N_MP):
        local = low_back(hidden2)
        gate = low_back(jnp.dot(local, gate_weight[:, group * ff_cols:(group + 1) * ff_cols], precision=highest))
        upper = low_back(jnp.dot(local, up_weight[:, group * ff_cols:(group + 1) * ff_cols], precision=highest))
        act = low(jax.nn.silu(gate) * upper)
        term = jnp.dot(act, down_weight[group * ff_cols:(group + 1) * ff_cols], precision=highest)
        mlp_out = mlp_out + low(low_back(term))
    return mid + mlp_out

def reference(inputs, lengths, q_weight, k_weight, v_weight, o_weight, gate_weight, up_weight, down_weight, attn_gain, mlp_gain, cotangent):
    segment, positions = layout(lengths)
    cosine, sine = angles_of(positions)
    params = tuple((item.astype(jnp.float32) for item in (inputs, q_weight, k_weight, v_weight, o_weight, gate_weight, up_weight, down_weight, attn_gain, mlp_gain)))

    def run(*params_in):
        return forward(*params_in, segment, cosine, sine)
    result, pullback = jax.vjp(run, *params)
    grads = pullback(cotangent.astype(jnp.float32))
    return (result.astype(jnp.bfloat16), grads[0].astype(jnp.bfloat16), grads[1], grads[2], grads[3], grads[4], grads[5], grads[6], grads[7], grads[8], grads[9])
```

```python
import functools

import jax
import jax.numpy as jnp
from jax import lax
from jax.experimental import pallas as pl
from jax.experimental.pallas import tpu as pltpu
from jax.sharding import PartitionSpec as P

D = 1536
HD = 96
ROW = 1024
SEGS = 4
NZ = 4
CH = 256
TB = 128
HQ_OWN = 4
KV_OWN = 2
QR = HQ_OWN * HD
KR = KV_OWN * HD
QKV = QR + 2 * KR
WR = QKV + QR
SCALE = HD ** -0.5
C2 = SCALE * 1.4426950408889634
NEG = -1e30
eps = 1e-05
rope_base = 100000.0
f32 = jnp.float32
bf16 = jnp.bfloat16
MESH = pl.DeviceIdType.MESH
ANY = pl.BlockSpec(memory_space=pl.ANY)
VM = pl.BlockSpec(memory_space=pltpu.VMEM)
DMA = pltpu.SemaphoreType.DMA
sds = jax.ShapeDtypeStruct


def nt(a, b):
    return lax.dot_general(a, b, (((1,), (1,)), ((), ())), preferred_element_type=f32)


def nn(a, b):
    return lax.dot_general(a, b, (((1,), (0,)), ((), ())), preferred_element_type=f32)


def tn(a, b):
    return lax.dot_general(a, b, (((0,), (0,)), ((), ())), preferred_element_type=f32)


def chunk(c, size=CH):
    return pl.ds(pl.multiple_of(c * size, size), size)


def places():
    dp = lax.axis_index("dp")
    z = lax.axis_index("mp")
    low = lax.rem(dp, 8)
    return dp, z, low


def partner(low, dp, bit):
    on = lax.rem(low // bit, 2)
    return dp + bit - 2 * bit * on


def greet(dp, z, low):
    barrier = pltpu.get_barrier_semaphore()
    for bit in (1, 2, 4):
        pl.semaphore_signal(barrier, inc=1, device_id={"dp": partner(low, dp, bit)}, device_id_type=MESH)
    for other in (1, 2, 3):
        pl.semaphore_signal(barrier, inc=1, device_id={"mp": lax.rem(z + other, NZ)}, device_id_type=MESH)
    pl.semaphore_wait(barrier, 6)


def put(src, dst, ssem, rsem, dev):
    return pltpu.make_async_remote_copy(
        src_ref=src, dst_ref=dst, send_sem=ssem, recv_sem=rsem, device_id=dev, device_id_type=MESH)


def split3(v):
    hi = v.astype(bf16).astype(f32)
    rest = v - hi
    mid = rest.astype(bf16).astype(f32)
    return hi, mid, rest - mid


def extra_rows(base, v, first):
    row = lax.broadcasted_iota(jnp.int32, base.shape, 0)
    out = base
    for i, part in enumerate(split3(v)):
        out = jnp.where(row == first + i, part, out)
    return out.astype(bf16)


def project(w, hid, qt, kt, kk, vt, vv, cos, sin, qaug, kaug, s, c):
    cols = chunk(c)
    t = nt(w[s, 0:QKV], hid[cols])
    co = cos[:, cols]
    si = sin[:, cols]

    def rot(u):
        a = u[0:HD // 2]
        b = u[HD // 2:HD]
        return jnp.concatenate([a * co - b * si, b * co + a * si], axis=0).astype(bf16)

    for h in range(HQ_OWN):
        qt[HQ_OWN * s + h, 0:HD, cols] = rot(t[HD * h:HD * h + HD])
        qt[HQ_OWN * s + h, HD:128, cols] = qaug[:, cols]
    for h in range(KV_OWN):
        g = KV_OWN * s + h
        k = jnp.concatenate([rot(t[QR + HD * h:QR + HD * h + HD]), kaug[:, cols]], axis=0)
        kt[g, :, cols] = k
        kk[g, cols, :] = k.T
        v = t[QR + KR + HD * h:QR + KR + HD * h + HD].astype(bf16)
        v = jnp.concatenate([v, jnp.ones((128 - HD, CH), bf16)], axis=0)
        vt[g, :, cols] = v
        vv[g, cols, :] = v.T


def attend(qt, kk, vt, ho, qaug, g):
    for qb in range(ROW // CH):
        lo = qb * CH
        nk = lo + CH
        q = jnp.concatenate([qt[2 * g, :, lo:nk], qt[2 * g + 1, :, lo:nk]], axis=1)
        st = nn(kk[g, 0:nk, :], q)
        ki = lax.broadcasted_iota(jnp.int32, (CH, CH), 0)
        qi = lax.broadcasted_iota(jnp.int32, (CH, CH), 1)
        keep = jnp.concatenate([ki <= qi, ki <= qi], axis=1)
        dg = jnp.where(keep, st[lo:nk], NEG)
        m = jnp.max(dg, axis=0, keepdims=True)
        if qb:
            m = jnp.maximum(m, jnp.max(st[0:lo], axis=0, keepdims=True))
        mc = m * C2
        o = nn(vt[g, :, lo:nk], jnp.exp2(dg * C2 - mc).astype(bf16))
        if qb:
            o = o + nn(vt[g, :, 0:lo], jnp.exp2(st[0:lo] * C2 - mc).astype(bf16))
        total = o[HD:HD + 1]
        r = (o[0:HD] / total).astype(bf16)
        back = (mc + jnp.log2(total)) * (-1.0 / C2)
        for h in range(2):
            part = slice(h * CH, (h + 1) * CH)
            ho[pl.ds(pl.multiple_of(g * 2 * HD + h * HD, 32), HD), lo:nk] = r[:, part]
            base = qaug[:, lo:nk].astype(f32)
            qt[2 * g + h, HD:128, lo:nk] = extra_rows(base, back[:, part], SEGS)


def order(z, j):
    right = (0, 1, 2, 3), (1, 0, 2, 3), (2, 3, 1, 0), (3, 2, 1, 0)
    s = jnp.int32(0)
    for i in range(NZ):
        s = s + jnp.where(z == i, right[i][j], 0)
    return s


GPARTS = ((0, QKV // 8, 48), (QKV, QR // 8, 32))


def forward_kernel(x, gain, gain2, cos, sin, qaug, kaug, own,
                   mid_o, hid2_o, ho_o, qt_o, kt_o, kk_o, vv_o, w_o, hid_o,
                   w, hid, ho, qt, kt, kk, vt, vv, midb, hidb,
                   zsend, zrecv, xsend, xrecv, ysend, yrecv, csend, crecv, osem, wsem, msem):
    dp, z, low = places()
    pc, px, py = (partner(low, dp, bit) for bit in (1, 2, 4))
    lx = px - dp + low
    ly = py - dp + low
    lxy = ly + lx - low
    load = pltpu.make_async_copy(own, w.at[z], wsem.at[0])
    load.start()
    greet(dp, z, low)
    load.wait()

    def rows(part, where, lo, hi):
        base, size, _ = GPARTS[part]
        return pl.ds(pl.multiple_of(base + where * size + lo, 16), hi - lo)

    def zcopy(part, d, s):
        r = rows(part, low, 0, GPARTS[part][1])
        to = lax.rem(z + d, NZ)
        return put(w.at[s, r], w.at[s, r], zsend.at[part, d - 1], zrecv.at[part, s], {"mp": to})

    for part in range(2):
        for hop in (1, 2, 3):
            for sign in (1, -1):
                to = z + sign * hop

                @pl.when((to >= 0) & (to < NZ))
                def _(part=part, hop=hop, sign=sign):
                    zcopy(part, (sign * hop) % NZ, z).start()

    def copies(part, j, kind):
        s = order(z, j)
        base, size, cut = GPARTS[part]
        a, b, both = (0, cut), (cut, size), (0, size)
        if part == 1:
            a, b = (0, size - 32), (size - 32, size)

        def c(where, half, sems, semr, i, dev):
            r = rows(part, where, *half)
            return put(w.at[s, r], w.at[s, r], sems.at[part, j - 1, i], semr.at[part, j - 1, i], {"dp": dev})

        if kind == 1:
            return [c(low, a, xsend, xrecv, 0, px), c(low, b, ysend, yrecv, 0, py)]
        if kind == 2:
            return [c(low, a, ysend, yrecv, 1, py), c(lx, a, ysend, yrecv, 2, py),
                    c(low, b, xsend, xrecv, 1, px), c(ly, b, xsend, xrecv, 2, px)]
        return [c(at, both, csend, crecv, i, pc) for i, at in enumerate((low, lx, ly, lxy))]

    def stage(part, j, k):
        if k == 1:
            zcopy(part, 1, order(z, j)).wait_recv()
        else:
            for c in copies(part, j, k - 1):
                c.wait_recv()
        if k < 4:
            for c in copies(part, j, k):
                c.start()

    def norm(c, _):
        r = chunk(c)
        xx = x[r].astype(f32)
        f = lax.rsqrt(jnp.mean(xx * xx, axis=1, keepdims=True) + eps)
        hid[r] = (xx * f * gain[...].astype(f32)).astype(bf16)
        return 0

    lax.fori_loop(0, ROW // CH, norm, 0)

    def projections(s):
        def one(c, _):
            project(w, hid, qt, kt, kk, vt, vv, cos, sin, qaug, kaug, s, c)
            return 0

        lax.fori_loop(0, ROW // CH, one, 0)

    def attends(s):
        def one(g, _):
            attend(qt, kk, vt, ho, qaug, KV_OWN * s + g)
            return 0

        lax.fori_loop(0, KV_OWN, one, 0)

    events = {
        "0a": ((0, 1, 1),),
        "0b": ((0, 1, 2), (0, 2, 1), (0, 1, 3), (0, 2, 2), (0, 3, 1), (0, 1, 4)),
        "1a": ((0, 2, 3), (0, 3, 2), (1, 1, 1)),
        "1b": ((0, 2, 4), (0, 3, 3), (1, 1, 2), (1, 2, 1)),
        "2a": ((0, 3, 4), (1, 1, 3), (1, 2, 2), (1, 3, 1)),
        "2b": ((1, 1, 4), (1, 2, 3), (1, 3, 2)),
        "3a": ((1, 2, 4), (1, 3, 3)),
        "3b": ((1, 3, 4),),
    }
    for j in range(NZ):
        s = order(z, j)
        projections(s)
        for e in events[f"{j}a"]:
            stage(*e)
        attends(s)
        for e in events[f"{j}b"]:
            stage(*e)
    outs = [(w, w_o), (qt, qt_o), (kt, kt_o), (kk, kk_o), (vv, vv_o), (ho, ho_o), (hid, hid_o)]
    writes = [pltpu.make_async_copy(a, b, osem.at[i]) for i, (a, b) in enumerate(outs)]
    for c in writes:
        c.start()

    def mid_copies(c, slot):
        return (pltpu.make_async_copy(midb.at[slot], mid_o.at[chunk(c)], msem.at[0, slot]),
                pltpu.make_async_copy(hidb.at[slot], hid2_o.at[chunk(c)], msem.at[1, slot]))

    def out_proj(c, _):
        r = chunk(c)
        slot = lax.rem(c, 2)

        @pl.when(c >= 2)
        def _():
            for m in mid_copies(c - 2, slot):
                m.wait()

        acc = x[r].astype(f32)
        for s in range(NZ):
            acc = acc + tn(ho[QR * s:QR * s + QR, r], w[s, QKV:WR])
        midb[slot] = acc
        f = lax.rsqrt(jnp.mean(acc * acc, axis=1, keepdims=True) + eps)
        hidb[slot] = (acc * f * gain2[...].astype(f32)).astype(bf16)
        for m in mid_copies(c, slot):
            m.start()
        return 0

    n = ROW // CH
    lax.fori_loop(0, n, out_proj, 0)
    for c in range(max(n - 2, 0), n):
        for m in mid_copies(c, c % 2):
            m.wait()
    for c in writes:
        c.wait()
    for part in range(2):
        for d in (1, 2, 3):
            zcopy(part, d, z).wait_send()
        for j in (1, 2, 3):
            for kind in (1, 2, 3):
                for c in copies(part, j, kind):
                    c.wait_send()


def forward(x, gain, gain2, cos, sin, qaug, kaug, own):
    heads = NZ * HQ_OWN
    kv = NZ * KV_OWN
    vm = pltpu.VMEM
    return pl.pallas_call(
        forward_kernel,
        out_shape=(sds((ROW, D), f32), sds((ROW, D), bf16), sds((heads * HD, ROW), bf16),
                   sds((heads, 128, ROW), bf16), sds((kv, 128, ROW), bf16), sds((kv, ROW, 128), bf16),
                   sds((kv, ROW, 128), bf16), sds((NZ, WR, D), bf16), sds((ROW, D), bf16)),
        in_specs=[VM] * 7 + [ANY],
        out_specs=(ANY,) * 9,
        scratch_shapes=[
            vm((NZ, WR, D), bf16), vm((ROW, D), bf16), vm((heads * HD, ROW), bf16),
            vm((heads, 128, ROW), bf16), vm((kv, 128, ROW), bf16), vm((kv, ROW, 128), bf16),
            vm((kv, 128, ROW), bf16), vm((kv, ROW, 128), bf16), vm((2, CH, D), f32), vm((2, CH, D), bf16),
            DMA((2, 3)), DMA((2, NZ)), DMA((2, 3, 3)), DMA((2, 3, 3)), DMA((2, 3, 3)), DMA((2, 3, 3)),
            DMA((2, 3, 4)), DMA((2, 3, 4)), DMA((7,)), DMA((1,)), DMA((2, 2))],
        compiler_params=pltpu.CompilerParams(
            collective_id=1, has_side_effects=True, vmem_limit_bytes=60 * 2**20),
        name="attention_forward",
    )(x, gain, gain2, cos, sin, qaug, kaug, own)


def tables(lengths):
    finish = jnp.cumsum(lengths)
    starts = finish - lengths
    place = jnp.arange(ROW, dtype=jnp.int32)
    segment = jnp.sum((place[None, :] >= finish[:, None]).astype(jnp.int32), axis=0)
    chosen = segment[None, :] == jnp.arange(SEGS, dtype=jnp.int32)[:, None]
    offsets = jnp.sum(jnp.where(chosen, starts[:, None], 0), axis=0)
    positions = (place - offsets).astype(f32)
    freqs = rope_base ** (-(jnp.arange(HD // 2, dtype=f32) * 2.0) / HD)
    angles = freqs[:, None] * positions[None, :]
    rest = 128 - HD - SEGS
    qaug = jnp.concatenate([jnp.where(chosen, 0.0, NEG), jnp.zeros((rest, ROW))], axis=0).astype(bf16)
    kaug = jnp.concatenate([chosen.astype(f32), jnp.ones((3, ROW)), jnp.zeros((rest - 3, ROW))], axis=0).astype(bf16)
    return jnp.cos(angles), jnp.sin(angles), qaug, kaug


def unrotate(u, co, si):
    a = u[0:HD // 2]
    b = u[HD // 2:HD]
    return jnp.concatenate([a * co + b * si, b * co - a * si], axis=0).astype(bf16)


def attend_back(qt, kt, kk, vv, dot, ho, dk, dv, gt, cos, sin, g, qb):
    lo = qb * CH
    hi = lo + CH
    q = jnp.concatenate([qt[2 * g, :, lo:hi], qt[2 * g + 1, :, lo:hi]], axis=1)
    heads = []
    for h in range(2):
        at = pl.ds(pl.multiple_of(g * 2 * HD + h * HD, 32), HD)
        do = dot[at, :]
        delta = jnp.sum(do.astype(f32) * ho[at, lo:hi].astype(f32), axis=0, keepdims=True)
        extra = extra_rows(jnp.zeros((128 - HD, CH), f32), -delta, 0)
        heads.append(jnp.concatenate([do, extra], axis=0))
    do = jnp.concatenate(heads, axis=1)
    do_t = do.T
    q_t = q.T
    dq = jnp.zeros((128, 2 * CH), f32)
    for kb in range(qb + 1):
        ks = slice(kb * CH, (kb + 1) * CH)
        p = jnp.exp2(nn(kk[g, ks, :], q) * C2)
        if kb == qb:
            ki = lax.broadcasted_iota(jnp.int32, (CH, CH), 0)
            qi = lax.broadcasted_iota(jnp.int32, (CH, CH), 1)
            keep = jnp.concatenate([ki <= qi, ki <= qi], axis=1)
            p = jnp.where(keep, p, 0.0)
        ds = (p * nn(vv[g, ks, :], do)).astype(bf16)
        dvb = nn(p.astype(bf16), do_t)
        dkb = nn(ds, q_t)
        if kb == qb:
            dv[g, ks, :] = dvb
            dk[g, ks, :] = dkb
        else:
            dv[g, ks, :] += dvb
            dk[g, ks, :] += dkb
        dq = dq + nn(kt[g, :, ks], ds)
    co = cos[:, lo:hi]
    si = sin[:, lo:hi]
    s = g // KV_OWN
    first = s * QKV + lax.rem(g, KV_OWN) * 2 * HD
    for h in range(2):
        at = pl.ds(pl.multiple_of(first + h * HD, 32), HD)
        gt[at, lo:hi] = unrotate(dq[0:HD, h * CH:(h + 1) * CH] * SCALE, co, si)


def backward_kernel(gain, gain2, cos, sin, x, cot, mid, gh2, hid1, ho_i, qt_i, kt_i, kk_i, vv_i, w_i,
                    xg_o, grad_o, gain_o, gain2_o, gm_o,
                    w, ho, qt, kt, kk, vv, dk, dv, gt, gml, dot, h1, xb, cb, mb, gb, gmb, ob,
                    lsem, bsem, wsem, psem):
    z = lax.axis_index("mp")
    loads = [pltpu.make_async_copy(a, b, lsem.at[i]) for i, (a, b) in enumerate(
        ((w_i, w), (ho_i, ho), (qt_i, qt), (kt_i, kt), (kk_i, kk), (vv_i, vv), (hid1, h1)))]
    for c in loads:
        c.start()
    nb = ROW // TB

    def block_loads(b, slot):
        r = chunk(b, TB)
        return [pltpu.make_async_copy(src.at[r], dst.at[slot], bsem.at[i, slot])
                for i, (src, dst) in enumerate(((mid, mb), (cot, cb), (gh2, gb)))]

    def gm_copy(b, slot):
        return pltpu.make_async_copy(gmb.at[slot], gm_o.at[chunk(b, TB)], wsem.at[slot])

    for c in block_loads(0, 0):
        c.start()
    gain2_o[...] = jnp.zeros_like(gain2_o)
    gain_o[...] = jnp.zeros_like(gain_o)

    def grad_mid(b, _):
        slot = lax.rem(b, 2)

        @pl.when(b + 1 < nb)
        def _():
            for c in block_loads(b + 1, 1 - slot):
                c.start()

        for c in block_loads(b, slot):
            c.wait()

        @pl.when(b >= 2)
        def _():
            gm_copy(b - 2, slot).wait()

        m = mb[slot]
        f = lax.rsqrt(jnp.mean(m * m, axis=1, keepdims=True) + eps)
        n = m * f
        g = gb[slot].astype(f32)
        gn = g * n
        gain2_o[...] += jnp.sum(gn, axis=0, keepdims=True)
        ga = gain2[...].astype(f32)
        gm = cb[slot].astype(f32) + f * (g * ga - n * jnp.mean(gn * ga, axis=1, keepdims=True))
        gmb[slot] = gm
        gml[chunk(b, TB)] = gm.astype(bf16)
        gm_copy(b, slot).start()
        return 0

    for qb in range(ROW // CH):
        lax.fori_loop(qb * (CH // TB), (qb + 1) * (CH // TB), grad_mid, 0)
        if qb == 0:
            for c in loads:
                c.wait()

        def heads(s, _, qb=qb):
            t = nt(w[s, QKV:WR], gml[qb * CH:(qb + 1) * CH])
            dot[pl.ds(pl.multiple_of(s * QR, 32), QR), :] = t.astype(bf16)
            return 0

        lax.fori_loop(0, NZ, heads, 0)

        def one(g, _, qb=qb):
            attend_back(qt, kt, kk, vv, dot, ho, dk, dv, gt, cos, sin, g, qb)
            return 0

        lax.fori_loop(0, NZ * KV_OWN, one, 0)
    for b in range(nb - 2, nb):
        gm_copy(b, b % 2).wait()

    def keys(g, _):
        s = g // KV_OWN
        first = s * QKV + QR + lax.rem(g, KV_OWN) * HD
        gt[pl.ds(pl.multiple_of(first, 32), HD), :] = unrotate(dk[g].T[0:HD] * SCALE, cos[...], sin[...])
        gt[pl.ds(pl.multiple_of(first + KR, 32), HD), :] = dv[g].T[0:HD].astype(bf16)
        return 0

    lax.fori_loop(0, NZ * KV_OWN, keys, 0)

    def own_grads(i, _):
        at = pl.ds(pl.multiple_of(z * QKV + i * 192, 32), 192)
        grad_o[pl.ds(pl.multiple_of(i * 192, 32), 192), :] = nn(gt[at, :], h1[...]).astype(bf16)
        return 0

    lax.fori_loop(0, QKV // 192, own_grads, 0)

    def own_o(i, _):
        at = pl.ds(pl.multiple_of(z * QR + i * 192, 32), 192)
        grad_o[pl.ds(pl.multiple_of(QKV + i * 192, 32), 192), :] = nn(ho[at, :], gml[...]).astype(bf16)
        return 0

    lax.fori_loop(0, QR // 192, own_o, 0)

    def tail_loads(b, slot):
        r = chunk(b, TB)
        return [pltpu.make_async_copy(x.at[r], cb.at[slot], bsem.at[0, slot]),
                pltpu.make_async_copy(gm_o.at[r], mb.at[slot], bsem.at[1, slot])]

    def out_copy(b, slot):
        return pltpu.make_async_copy(ob.at[slot], xg_o.at[chunk(b, TB)], psem.at[slot])

    for c in tail_loads(0, 0):
        c.start()

    def tail(b, _):
        slot = lax.rem(b, 2)

        @pl.when(b + 1 < nb)
        def _():
            for c in tail_loads(b + 1, 1 - slot):
                c.start()

        r = chunk(b, TB)
        acc = jnp.zeros((TB, D), f32)
        for s in range(NZ):
            acc = acc + tn(gt[QKV * s:QKV * s + QKV, r], w[s, 0:QKV])
        for c in tail_loads(b, slot):
            c.wait()

        @pl.when(b >= 2)
        def _():
            out_copy(b - 2, slot).wait()

        xx = cb[slot].astype(f32)
        f = lax.rsqrt(jnp.mean(xx * xx, axis=1, keepdims=True) + eps)
        n = xx * f
        gn = acc * n
        gain_o[...] += jnp.sum(gn, axis=0, keepdims=True)
        ga = gain[...].astype(f32)
        out = mb[slot] + f * (acc * ga - n * jnp.mean(gn * ga, axis=1, keepdims=True))
        ob[slot] = out.astype(bf16)
        out_copy(b, slot).start()
        return 0

    lax.fori_loop(0, nb, tail, 0)
    for b in range(nb - 2, nb):
        out_copy(b, b % 2).wait()


def backward(gain, gain2, cos, sin, x, cot, mid, gh2, hid1, ho, qt, kt, kk, vv, w):
    vm = pltpu.VMEM
    heads = NZ * HQ_OWN
    kv = NZ * KV_OWN
    return pl.pallas_call(
        backward_kernel,
        out_shape=(sds((ROW, D), bf16), sds((WR, D), bf16), sds((1, D), f32), sds((1, D), f32), sds((ROW, D), f32)),
        in_specs=[VM] * 4 + [ANY] * 11,
        out_specs=(ANY, VM, VM, VM, ANY),
        scratch_shapes=[
            vm((NZ, WR, D), bf16), vm((heads * HD, ROW), bf16), vm((heads, 128, ROW), bf16),
            vm((kv, 128, ROW), bf16), vm((kv, ROW, 128), bf16), vm((kv, ROW, 128), bf16),
            vm((kv, ROW, 128), f32), vm((kv, ROW, 128), f32), vm((NZ * QKV, ROW), bf16),
            vm((ROW, D), bf16), vm((heads * HD, CH), bf16), vm((ROW, D), bf16),
            vm((2, TB, D), bf16), vm((2, TB, D), bf16), vm((2, TB, D), f32), vm((2, TB, D), bf16),
            vm((2, TB, D), f32), vm((2, TB, D), bf16),
            DMA((7,)), DMA((3, 2)), DMA((2,)), DMA((2,))],
        compiler_params=pltpu.CompilerParams(vmem_limit_bytes=63 * 2**20),
        name="attention_backward",
    )(gain, gain2, cos, sin, x, cot, mid, gh2, hid1, ho, qt, kt, kk, vv, w)


def body(inputs, lengths, q_weight, k_weight, v_weight, o_weight, gate_weight, up_weight, down_weight,
         attn_gain, mlp_gain, cotangent):
    x = inputs.reshape(ROW, D)
    cot = cotangent.reshape(ROW, D)
    gain = attn_gain.reshape(1, D)
    gain2 = mlp_gain.reshape(1, D)
    cos, sin, qaug, kaug = tables(lengths[0])
    own = jnp.concatenate([q_weight.T, k_weight.T, v_weight.T, o_weight], axis=0)
    mid, hidden2, ho, qt, kt, kk, vv, w, hid1 = forward(x, gain, gain2, cos, sin, qaug, kaug, own)
    gate = jnp.dot(hidden2, gate_weight, preferred_element_type=f32)
    upper = jnp.dot(hidden2, up_weight, preferred_element_type=f32)
    sigma = jax.nn.sigmoid(gate)
    act = (gate * sigma * upper).astype(bf16)
    mlp_term = jnp.dot(act, down_weight, preferred_element_type=f32).astype(bf16)
    grad_act = jnp.einsum("td,fd->tf", cot, down_weight, preferred_element_type=f32)
    grad_gate = (grad_act * upper * sigma * (1.0 + gate * (1.0 - sigma))).astype(bf16)
    grad_up = (grad_act * gate * sigma).astype(bf16)
    back_term2 = jnp.einsum("tf,df->td", grad_gate, gate_weight, preferred_element_type=f32)
    back_term2 = back_term2 + jnp.einsum("tf,df->td", grad_up, up_weight, preferred_element_type=f32)
    grad_hidden2 = lax.psum(back_term2.astype(bf16), "mp")
    mlp_out = lax.psum(mlp_term, "mp").astype(f32)
    output = (mid + mlp_out).astype(bf16).reshape(1, ROW, D)
    down_grad = jnp.einsum("td,tf->df", cot, act, preferred_element_type=f32)
    gate_grad = jnp.einsum("td,tf->df", hidden2, grad_gate, preferred_element_type=f32)
    up_grad = jnp.einsum("td,tf->df", hidden2, grad_up, preferred_element_type=f32)
    input_grad, grads, gain_local, gain2_local, _ = backward(
        gain, gain2, cos, sin, x, cot, mid, grad_hidden2, hid1, ho, qt, kt, kk, vv, w)

    def scatter(v, dim=0):
        return lax.psum_scatter(v, "dp", scatter_dimension=dim, tiled=True).astype(f32)

    mlp = scatter(jnp.concatenate([gate_grad, up_grad, down_grad], axis=1).astype(bf16))
    ff = gate_weight.shape[1]
    att = scatter(grads.T)
    return (output, input_grad.reshape(1, ROW, D), att[:, 0:QR], att[:, QR:QR + KR], att[:, QR + KR:QKV],
            att[:, QKV:WR].T, mlp[:, 0:ff], mlp[:, ff:2 * ff], mlp[:, 2 * ff:].T,
            scatter(gain_local[0]), scatter(gain2_local[0]))


def solution(mesh):
    row = P("dp", None, None)
    in_specs = (row, P("dp", None), P(None, "mp"), P(None, "mp"), P(None, "mp"), P("mp", None),
                P(None, "mp"), P(None, "mp"), P("mp", None), P(), P(), row)
    out_specs = (row, row, P("dp", "mp"), P("dp", "mp"), P("dp", "mp"), P("mp", "dp"),
                 P("dp", "mp"), P("dp", "mp"), P("mp", "dp"), P("dp"), P("dp"))
    return jax.shard_map(body, mesh=mesh, in_specs=in_specs, out_specs=out_specs, check_vma=False)
```

```python
import functools

import jax
import jax.numpy as jnp
from jax import lax
from jax.experimental import pallas as pl
from jax.experimental.pallas import tpu as pltpu
from jax.sharding import PartitionSpec as P

D = 1536
HD = 96
ROW = 1024
SEGS = 4
NZ = 4
CH = 256
TB = 128
BL = 64
LAG = 2
RING = 10
HQ_OWN = 4
KV_OWN = 2
QR = HQ_OWN * HD
KR = KV_OWN * HD
QKV = QR + 2 * KR
WR = QKV + QR
SCALE = HD ** -0.5
C2 = SCALE * 1.4426950408889634
NEG = -1e30
eps = 1e-05
rope_base = 100000.0
f32 = jnp.float32
bf16 = jnp.bfloat16
MESH = pl.DeviceIdType.MESH
ANY = pl.BlockSpec(memory_space=pl.ANY)
VM = pl.BlockSpec(memory_space=pltpu.VMEM)
DMA = pltpu.SemaphoreType.DMA
sds = jax.ShapeDtypeStruct


def nt(a, b):
    return lax.dot_general(a, b, (((1,), (1,)), ((), ())), preferred_element_type=f32)


def nn(a, b):
    return lax.dot_general(a, b, (((1,), (0,)), ((), ())), preferred_element_type=f32)


def tn(a, b):
    return lax.dot_general(a, b, (((0,), (0,)), ((), ())), preferred_element_type=f32)


def chunk(c, size=CH):
    return pl.ds(pl.multiple_of(c * size, size), size)


def places():
    dp = lax.axis_index("dp")
    z = lax.axis_index("mp")
    low = lax.rem(dp, 8)
    return dp, z, low


def partner(low, dp, bit):
    on = lax.rem(low // bit, 2)
    return dp + bit - 2 * bit * on


def greet(dp, z, low):
    barrier = pltpu.get_barrier_semaphore()
    for bit in (1, 2, 4):
        pl.semaphore_signal(barrier, inc=1, device_id={"dp": partner(low, dp, bit)}, device_id_type=MESH)
    for other in (1, 2, 3):
        pl.semaphore_signal(barrier, inc=1, device_id={"mp": lax.rem(z + other, NZ)}, device_id_type=MESH)
    pl.semaphore_wait(barrier, 6)


def put(src, dst, ssem, rsem, dev):
    return pltpu.make_async_remote_copy(
        src_ref=src, dst_ref=dst, send_sem=ssem, recv_sem=rsem, device_id=dev, device_id_type=MESH)


def split3(v):
    hi = v.astype(bf16).astype(f32)
    rest = v - hi
    mid = rest.astype(bf16).astype(f32)
    return hi, mid, rest - mid


def extra_rows(base, v, first):
    row = lax.broadcasted_iota(jnp.int32, base.shape, 0)
    out = base
    for i, part in enumerate(split3(v)):
        out = jnp.where(row == first + i, part, out)
    return out.astype(bf16)


def project(w, hid, qt, kt, kk, vt, vv, cos, sin, qaug, kaug, s, c):
    cols = chunk(c)
    t = nt(w[s, 0:QKV], hid[cols])
    co = cos[:, cols]
    si = sin[:, cols]

    def rot(u):
        a = u[0:HD // 2]
        b = u[HD // 2:HD]
        return jnp.concatenate([a * co - b * si, b * co + a * si], axis=0).astype(bf16)

    for h in range(HQ_OWN):
        qt[HQ_OWN * s + h, 0:HD, cols] = rot(t[HD * h:HD * h + HD])
        qt[HQ_OWN * s + h, HD:128, cols] = qaug[:, cols]
    for h in range(KV_OWN):
        g = KV_OWN * s + h
        k = jnp.concatenate([rot(t[QR + HD * h:QR + HD * h + HD]), kaug[:, cols]], axis=0)
        kt[g, :, cols] = k
        kk[g, cols, :] = k.T
        v = t[QR + KR + HD * h:QR + KR + HD * h + HD].astype(bf16)
        v = jnp.concatenate([v, jnp.ones((128 - HD, CH), bf16)], axis=0)
        vt[g, :, cols] = v
        vv[g, cols, :] = v.T


def attend(qt, kk, vt, ho, qaug, g):
    for qb in range(ROW // CH):
        lo = qb * CH
        nk = lo + CH
        q = jnp.concatenate([qt[2 * g, :, lo:nk], qt[2 * g + 1, :, lo:nk]], axis=1)
        st = nn(kk[g, 0:nk, :], q)
        ki = lax.broadcasted_iota(jnp.int32, (CH, CH), 0)
        qi = lax.broadcasted_iota(jnp.int32, (CH, CH), 1)
        keep = jnp.concatenate([ki <= qi, ki <= qi], axis=1)
        dg = jnp.where(keep, st[lo:nk], NEG)
        m = jnp.max(dg, axis=0, keepdims=True)
        if qb:
            m = jnp.maximum(m, jnp.max(st[0:lo], axis=0, keepdims=True))
        mc = m * C2
        o = nn(vt[g, :, lo:nk], jnp.exp2(dg * C2 - mc).astype(bf16))
        if qb:
            o = o + nn(vt[g, :, 0:lo], jnp.exp2(st[0:lo] * C2 - mc).astype(bf16))
        total = o[HD:HD + 1]
        r = (o[0:HD] / total).astype(bf16)
        back = (mc + jnp.log2(total)) * (-1.0 / C2)
        for h in range(2):
            part = slice(h * CH, (h + 1) * CH)
            ho[pl.ds(pl.multiple_of(g * 2 * HD + h * HD, 32), HD), lo:nk] = r[:, part]
            base = qaug[:, lo:nk].astype(f32)
            qt[2 * g + h, HD:128, lo:nk] = extra_rows(base, back[:, part], SEGS)


def order(z, j):
    right = (0, 1, 2, 3), (1, 0, 2, 3), (2, 3, 1, 0), (3, 2, 1, 0)
    s = jnp.int32(0)
    for i in range(NZ):
        s = s + jnp.where(z == i, right[i][j], 0)
    return s


GPARTS = ((0, QKV // 8, 48), (QKV, QR // 8, 32))


def forward_kernel(x, gain, gain2, cos, sin, qaug, kaug, own, cot,
                   mid_o, hid2_o, ho_o, qt_o, kt_o, kk_o, vv_o, w_o, hid1t_o, hid2t_o, cott_o,
                   w, hid, ho, qt, kt, kk, vt, vv, midb, hidb, hidtb, cb, ctb,
                   zsend, zrecv, xsend, xrecv, ysend, yrecv, csend, crecv, osem, wsem, msem, tsem):
    dp, z, low = places()
    pc, px, py = (partner(low, dp, bit) for bit in (1, 2, 4))
    lx = px - dp + low
    ly = py - dp + low
    lxy = ly + lx - low
    load = pltpu.make_async_copy(own, w.at[z], wsem.at[0])
    load.start()
    greet(dp, z, low)
    load.wait()

    def rows(part, where, lo, hi):
        base, size, _ = GPARTS[part]
        return pl.ds(pl.multiple_of(base + where * size + lo, 16), hi - lo)

    def zcopy(part, d, s):
        r = rows(part, low, 0, GPARTS[part][1])
        to = lax.rem(z + d, NZ)
        return put(w.at[s, r], w.at[s, r], zsend.at[part, d - 1], zrecv.at[part, s], {"mp": to})

    for part in range(2):
        for hop in (1, 2, 3):
            for sign in (1, -1):
                to = z + sign * hop

                @pl.when((to >= 0) & (to < NZ))
                def _(part=part, hop=hop, sign=sign):
                    zcopy(part, (sign * hop) % NZ, z).start()

    def copies(part, j, kind):
        s = order(z, j)
        base, size, cut = GPARTS[part]
        a, b, both = (0, cut), (cut, size), (0, size)
        if part == 1:
            a, b = (0, size - 32), (size - 32, size)

        def c(where, half, sems, semr, i, dev):
            r = rows(part, where, *half)
            return put(w.at[s, r], w.at[s, r], sems.at[part, j - 1, i], semr.at[part, j - 1, i], {"dp": dev})

        if kind == 1:
            return [c(low, a, xsend, xrecv, 0, px), c(low, b, ysend, yrecv, 0, py)]
        if kind == 2:
            return [c(low, a, ysend, yrecv, 1, py), c(lx, a, ysend, yrecv, 2, py),
                    c(low, b, xsend, xrecv, 1, px), c(ly, b, xsend, xrecv, 2, px)]
        return [c(at, both, csend, crecv, i, pc) for i, at in enumerate((low, lx, ly, lxy))]

    def stage(part, j, k):
        if k == 1:
            zcopy(part, 1, order(z, j)).wait_recv()
        else:
            for c in copies(part, j, k - 1):
                c.wait_recv()
        if k < 4:
            for c in copies(part, j, k):
                c.start()

    def norm(c, _):
        r = chunk(c)
        xx = x[r].astype(f32)
        f = lax.rsqrt(jnp.mean(xx * xx, axis=1, keepdims=True) + eps)
        h = (xx * f * gain[...].astype(f32)).astype(bf16)
        hid[r] = h
        turned(c, h, hid1t_o)
        return 0

    def turn_copy(c, dst):
        return pltpu.make_async_copy(ctb.at[lax.rem(c, 2)], dst.at[:, chunk(c)], tsem.at[0, lax.rem(c, 2)])

    def turned(c, v, dst):
        pl.when(c >= 2)(lambda: turn_copy(c - 2, dst).wait())
        ctb[lax.rem(c, 2)] = v.T
        turn_copy(c, dst).start()

    def turn_end(dst):
        for c in (ROW // CH - 2, ROW // CH - 1):
            turn_copy(c, dst).wait()

    def cot_load(c):
        return pltpu.make_async_copy(cot.at[chunk(c)], cb.at[lax.rem(c, 2)], tsem.at[1, lax.rem(c, 2)])

    def turn_cot(c, _):
        pl.when(c + 1 < ROW // CH)(lambda: cot_load(c + 1).start())
        cot_load(c).wait()
        turned(c, cb[lax.rem(c, 2)], cott_o)
        return 0

    cot_load(0).start()
    lax.fori_loop(0, ROW // CH, norm, 0)
    turn_end(hid1t_o)

    def projections(s):
        def one(c, _):
            project(w, hid, qt, kt, kk, vt, vv, cos, sin, qaug, kaug, s, c)
            return 0

        lax.fori_loop(0, ROW // CH, one, 0)

    def attends(s):
        def one(g, _):
            attend(qt, kk, vt, ho, qaug, KV_OWN * s + g)
            return 0

        lax.fori_loop(0, KV_OWN, one, 0)

    events = {
        "0a": ((0, 1, 1),),
        "0b": ((0, 1, 2), (0, 2, 1), (0, 1, 3), (0, 2, 2), (0, 3, 1), (0, 1, 4)),
        "1a": ((0, 2, 3), (0, 3, 2), (1, 1, 1)),
        "1b": ((0, 2, 4), (0, 3, 3), (1, 1, 2), (1, 2, 1)),
        "2a": ((0, 3, 4), (1, 1, 3), (1, 2, 2), (1, 3, 1)),
        "2b": ((1, 1, 4), (1, 2, 3), (1, 3, 2)),
        "3a": ((1, 2, 4), (1, 3, 3)),
        "3b": ((1, 3, 4),),
    }
    for j in range(NZ):
        s = order(z, j)
        if j == 1:
            lax.fori_loop(0, ROW // CH, turn_cot, 0)
            turn_end(cott_o)
        projections(s)
        for e in events[f"{j}a"]:
            stage(*e)
        attends(s)
        for e in events[f"{j}b"]:
            stage(*e)
    outs = [(w, w_o), (qt, qt_o), (kt, kt_o), (kk, kk_o), (vv, vv_o), (ho, ho_o)]
    writes = [pltpu.make_async_copy(a, b, osem.at[i]) for i, (a, b) in enumerate(outs)]
    for c in writes:
        c.start()

    def mid_copies(c, slot):
        return (pltpu.make_async_copy(midb.at[slot], mid_o.at[chunk(c)], msem.at[0, slot]),
                pltpu.make_async_copy(hidb.at[slot], hid2_o.at[chunk(c)], msem.at[1, slot]),
                pltpu.make_async_copy(hidtb.at[slot], hid2t_o.at[:, chunk(c)], msem.at[2, slot]))

    def out_proj(c, _):
        r = chunk(c)
        slot = lax.rem(c, 2)

        @pl.when(c >= 2)
        def _():
            for m in mid_copies(c - 2, slot):
                m.wait()

        acc = x[r].astype(f32)
        for s in range(NZ):
            acc = acc + tn(ho[QR * s:QR * s + QR, r], w[s, QKV:WR])
        midb[slot] = acc
        f = lax.rsqrt(jnp.mean(acc * acc, axis=1, keepdims=True) + eps)
        h = (acc * f * gain2[...].astype(f32)).astype(bf16)
        hidb[slot] = h
        hidtb[slot] = h.T
        for m in mid_copies(c, slot):
            m.start()
        return 0

    n = ROW // CH
    lax.fori_loop(0, n, out_proj, 0)
    for c in range(max(n - 2, 0), n):
        for m in mid_copies(c, c % 2):
            m.wait()
    for c in writes:
        c.wait()
    for part in range(2):
        for d in (1, 2, 3):
            zcopy(part, d, z).wait_send()
        for j in (1, 2, 3):
            for kind in (1, 2, 3):
                for c in copies(part, j, kind):
                    c.wait_send()


def forward(x, gain, gain2, cos, sin, qaug, kaug, own, cot):
    heads = NZ * HQ_OWN
    kv = NZ * KV_OWN
    vm = pltpu.VMEM
    return pl.pallas_call(
        forward_kernel,
        out_shape=(sds((ROW, D), f32), sds((ROW, D), bf16), sds((heads * HD, ROW), bf16),
                   sds((heads, 128, ROW), bf16), sds((kv, 128, ROW), bf16), sds((kv, ROW, 128), bf16),
                   sds((kv, ROW, 128), bf16), sds((NZ, WR, D), bf16), sds((D, ROW), bf16), sds((D, ROW), bf16),
                   sds((D, ROW), bf16)),
        in_specs=[VM] * 7 + [ANY] * 2,
        out_specs=(ANY,) * 11,
        scratch_shapes=[
            vm((NZ, WR, D), bf16), vm((ROW, D), bf16), vm((heads * HD, ROW), bf16),
            vm((heads, 128, ROW), bf16), vm((kv, 128, ROW), bf16), vm((kv, ROW, 128), bf16),
            vm((kv, 128, ROW), bf16), vm((kv, ROW, 128), bf16), vm((2, CH, D), f32), vm((2, CH, D), bf16),
            vm((2, D, CH), bf16), vm((2, CH, D), bf16), vm((2, D, CH), bf16),
            DMA((2, 3)), DMA((2, NZ)), DMA((2, 3, 3)), DMA((2, 3, 3)), DMA((2, 3, 3)), DMA((2, 3, 3)),
            DMA((2, 3, 4)), DMA((2, 3, 4)), DMA((6,)), DMA((1,)), DMA((3, 2)), DMA((2, 2))],
        compiler_params=pltpu.CompilerParams(
            collective_id=1, has_side_effects=True, vmem_limit_bytes=60 * 2**20),
        name="attention_forward",
    )(x, gain, gain2, cos, sin, qaug, kaug, own, cot)


def tables(lengths):
    finish = jnp.cumsum(lengths)
    starts = finish - lengths
    place = jnp.arange(ROW, dtype=jnp.int32)
    segment = jnp.sum((place[None, :] >= finish[:, None]).astype(jnp.int32), axis=0)
    chosen = segment[None, :] == jnp.arange(SEGS, dtype=jnp.int32)[:, None]
    offsets = jnp.sum(jnp.where(chosen, starts[:, None], 0), axis=0)
    positions = (place - offsets).astype(f32)
    freqs = rope_base ** (-(jnp.arange(HD // 2, dtype=f32) * 2.0) / HD)
    angles = freqs[:, None] * positions[None, :]
    rest = 128 - HD - SEGS
    qaug = jnp.concatenate([jnp.where(chosen, 0.0, NEG), jnp.zeros((rest, ROW))], axis=0).astype(bf16)
    kaug = jnp.concatenate([chosen.astype(f32), jnp.ones((3, ROW)), jnp.zeros((rest - 3, ROW))], axis=0).astype(bf16)
    return jnp.cos(angles), jnp.sin(angles), qaug, kaug


class RowSum:
    def __init__(self, z, own, rend, rmid, out, ssem, esem, msem, osem, ring, lag):
        self.z, self.own, self.ring, self.lag = z, own, ring, lag
        self.rend, self.rmid, self.out = rend, rmid, out
        self.ssem, self.esem, self.msem, self.osem = ssem, esem, msem, osem

    def who(self, i):
        odd = lax.rem(i, 2)
        return 3 * odd, 1 + odd, 2 - odd, 3 - 3 * odd

    def copy(self, kind, i, to, sem=0):
        s = lax.rem(i, self.ring)
        src, dst, rsem = {
            "end": (self.own(i), self.rend.at[s], self.esem),
            "mid": (self.rmid.at[s], self.rmid.at[s], self.msem),
            "out": (self.out.at[s], self.out.at[s], self.osem)}[kind]
        return put(src, dst, self.ssem.at[sem, s], rsem.at[s], {"mp": to})

    def on(self, place, f):
        pl.when(self.z == place)(f)

    def step1(self, i):
        e, o, m, f = self.who(i)
        self.on(e, lambda: self.copy("end", i, o).start())
        self.on(f, lambda: self.copy("end", i, m).start())

    def step2(self, i):
        e, o, m, f = self.who(i)
        s = lax.rem(i, self.ring)

        def go():
            self.copy("end", i, o).wait_recv()
            self.rmid[s] = (self.own(i)[...].astype(f32) + self.rend[s].astype(f32)).astype(bf16)
            self.copy("mid", i, o).start()

        self.on(m, go)

    def step3(self, i):
        e, o, m, f = self.who(i)
        s = lax.rem(i, self.ring)

        def go():
            self.copy("end", i, e).wait_recv()
            self.copy("mid", i, e).wait_recv()
            self.out[s] = (self.own(i)[...].astype(f32) + self.rend[s].astype(f32)
                           + self.rmid[s].astype(f32)).astype(bf16)
            self.copy("out", i, m, 1).start()
            self.copy("out", i, e).start()

        self.on(o, go)

    def step4(self, i):
        e, o, m, f = self.who(i)

        def go():
            self.copy("out", i, o).wait_recv()
            self.copy("out", i, f, 1).start()

        self.on(m, go)

    def arrive(self, i):
        e, o, m, f = self.who(i)
        self.on(e, lambda: self.copy("out", i, o).wait_recv())
        self.on(f, lambda: self.copy("out", i, m).wait_recv())

    def drain(self, i):
        e, o, m, f = self.who(i)
        self.on(e, lambda: self.copy("end", i, o).wait_send())
        self.on(f, lambda: self.copy("end", i, m).wait_send())

        def middle():
            self.copy("mid", i, o).wait_send()
            self.copy("out", i, f, 1).wait_send()

        def owner():
            self.copy("out", i, m, 1).wait_send()
            self.copy("out", i, e).wait_send()

        self.on(m, middle)
        self.on(o, owner)

    def tick(self, t, count, finish):
        def last(i):
            self.arrive(i)
            finish(i)
            self.drain(i)

        for lag, step in ((4, last), (3, self.step4), (2, self.step3), (1, self.step2), (0, self.step1)):
            i = t - lag * self.lag
            pl.when((i >= 0) & (i < count))(functools.partial(step, i))


class GradSum:
    def __init__(self, dp, low, width, cut, g, c1, x1, y1, x2, y2, ssem, rsem, out, wide=False):
        self.pc, self.px, self.py = (partner(low, dp, bit) for bit in (1, 2, 4))
        self.c, self.x, self.y = lax.rem(low, 2), lax.rem(low // 2, 2), low // 4
        self.g, self.c1, self.x1, self.y1, self.x2, self.y2 = g, c1, x1, y1, x2, y2
        self.ssem, self.rsem, self.out = ssem, rsem, out
        self.width, self.cut, self.wide = width, cut, wide

    def cols(self, u, lo, hi):
        if self.wide:
            return (pl.ds(pl.multiple_of(u * self.width + lo, 128), hi - lo),)
        return (pl.ds(lo, hi - lo),)

    def part(self, u, *at, lo=None, hi=None):
        lo, hi = (0, self.width) if lo is None else (lo, hi)
        return (() if self.wide else (u,)) + at + self.cols(u, lo, hi)

    def put_block(self, u, k, res):
        self.put_part(u, k, 0, self.width, res)

    def put_part(self, u, k, lo, hi, res):
        self.g[self.part(u, k // 4, (k // 2) % 2, k % 2, slice(None), lo=lo, hi=hi)] = res.astype(bf16)

    def copies(self, u, k):
        g, c, x, y = self.g, self.c, self.x, self.y
        every = slice(None)
        a = dict(lo=0, hi=self.cut)
        b = dict(lo=self.cut, hi=self.width)

        def mk(i, src, dst, dev):
            return put(src, dst, self.ssem.at[u, i], self.rsem.at[u, i], {"dp": dev})

        if k == 0:
            return [mk(0, g.at[self.part(u, every, every, 1 - c, every)], self.c1.at[u], self.pc)]
        if k == 1:
            return [mk(1, g.at[self.part(u, every, 1 - x, c, every, **a)], self.x1.at[u], self.px),
                    mk(2, g.at[self.part(u, 1 - y, every, c, every, **b)], self.y1.at[u], self.py)]
        return [mk(3, g.at[self.part(u, 1 - y, x, c, every, **a)], self.y2.at[u], self.py),
                mk(4, g.at[self.part(u, y, 1 - x, c, every, **b)], self.x2.at[u], self.px)]

    def start(self, u):
        for c in self.copies(u, 0):
            c.start()

    def stage(self, k, u):
        width, cut = self.width, self.cut
        g, c, x, y = self.g, self.c, self.x, self.y
        for cp in self.copies(u, k - 1):
            cp.wait_recv()

        def at(i, j, lo, hi):
            return self.part(u, i, j, c, slice(None), lo=lo, hi=hi)

        def add(i, j, lo, hi, other):
            g[at(i, j, lo, hi)] = (g[at(i, j, lo, hi)].astype(f32) + other.astype(f32)).astype(bf16)

        if k == 1:
            for i in range(2):
                for j in range(2):
                    add(i, j, 0, width, self.c1[u, i, j])
        elif k == 2:
            for i in range(2):
                add(i, x, 0, cut, self.x1[u, i])
                add(y, i, cut, width, self.y1[u, i])
        else:
            self.out[:, pl.ds(pl.multiple_of(u * width, 128), cut)] = (
                g[at(y, x, 0, cut)].astype(f32) + self.y2[u].astype(f32))
            self.out[:, pl.ds(pl.multiple_of(u * width + cut, 128), width - cut)] = (
                g[at(y, x, cut, width)].astype(f32) + self.x2[u].astype(f32))
        if k < 3:
            for cp in self.copies(u, k):
                cp.start()

    def drain(self, u):
        for k in range(3):
            for cp in self.copies(u, k):
                cp.wait_send()


def sum_scratch(count, width, cut):
    vm = pltpu.VMEM
    rest = width - cut
    return [vm((count, 2, 2, 2, 192, width), bf16), vm((count, 2, 2, 192, width), bf16),
            vm((count, 2, 192, cut), bf16), vm((count, 2, 192, rest), bf16),
            vm((count, 192, rest), bf16), vm((count, 192, cut), bf16), DMA((count, 5)), DMA((count, 5))]


def ring_scratch(ring, rows):
    vm = pltpu.VMEM
    return [vm((ring, rows, D), bf16), vm((ring, rows, D), bf16), vm((ring, rows, D), bf16),
            DMA((2, ring)), DMA((ring,)), DMA((ring,)), DMA((ring,))]


MLP_UNITS = 6
MLP_WIDTH = 512


def feed_kernel(gain2, hid2, cot, mid, hid2t_i, cott_i, gw_i, uw_i, dw_i,
                mlp_o, gm_o, gml_o, gmlt_o, gain2_o, grad_o,
                gw, uw, dw, a3, side, own, hb, cb, tb, mb, cb2, gmb, gmlb, gmltb,
                rend, rmid, out, zs, ze, zm, zo,
                g, c1, x1, y1, x2, y2, gs, gr,
                lsem, bsem, tsem, msem, wsem):
    dp, z, low = places()
    loads = [pltpu.make_async_copy(a, b, lsem.at[i]) for i, (a, b) in enumerate(
        ((gw_i, gw), (uw_i, uw), (dw_i, dw), (hid2t_i, side), (cott_i, side)))]
    nc = ROW // CH
    nb = ROW // BL
    nj = ROW // 128
    pair = 128 // BL

    def chunk_loads(c):
        return [pltpu.make_async_copy(src.at[chunk(c)], dst.at[lax.rem(c, 2)], bsem.at[i, lax.rem(c, 2)])
                for i, (src, dst) in enumerate(((hid2, hb), (cot, cb)))]

    for c in chunk_loads(0):
        c.start()
    for c in loads[:4]:
        c.start()
    greet(dp, z, low)
    zsum = RowSum(z, lambda i: own.at[chunk(i, BL)], rend, rmid, out, zs, ze, zm, zo, RING, LAG)
    gsum = GradSum(dp, low, MLP_WIDTH, MLP_WIDTH // 2, g, c1, x1, y1, x2, y2, gs, gr, grad_o)
    gain2_o[...] = jnp.zeros_like(gain2_o)

    def gm_loads(j):
        r = chunk(j, 128)
        return [pltpu.make_async_copy(mid.at[r], mb, msem.at[0]),
                pltpu.make_async_copy(cot.at[r], cb2, msem.at[1])]

    def gm_writes(j):
        r = chunk(j, 128)
        s = lax.rem(j, 2)
        return [pltpu.make_async_copy(gmb.at[s], gm_o.at[r], wsem.at[0, s]),
                pltpu.make_async_copy(gmlb.at[s], gml_o.at[r], wsem.at[1, s]),
                pltpu.make_async_copy(gmltb.at[s], gmlt_o.at[:, r], wsem.at[2, s])]

    def finish_pair(j):
        s = lax.rem(j, 2)
        for c in gm_loads(j):
            c.wait()

        @pl.when(j >= 2)
        def _():
            for c in gm_writes(j - 2):
                c.wait()

        gh = jnp.concatenate([out[lax.rem(j * pair + k, RING)] for k in range(pair)], axis=0).astype(f32)
        m = mb[...]
        f = lax.rsqrt(jnp.mean(m * m, axis=1, keepdims=True) + eps)
        n = m * f
        gn = gh * n
        gain2_o[...] += jnp.sum(gn, axis=0, keepdims=True)
        ga = gain2[...].astype(f32)
        gm = cb2[...].astype(f32) + f * (gh * ga - n * jnp.mean(gn * ga, axis=1, keepdims=True))
        gmb[s] = gm
        low_gm = gm.astype(bf16)
        gmlb[s] = low_gm
        gmltb[s] = low_gm.T
        for c in gm_writes(j):
            c.start()

        @pl.when(j + 1 < nj)
        def _():
            for c in gm_loads(j + 1):
                c.start()

    def finish(i):
        pl.when(lax.rem(i, pair) == pair - 1)(lambda: finish_pair(i // pair))

    for c in gm_loads(0):
        c.start()

    def tick(t):
        zsum.tick(t, nb, finish)

    def mlp_write(c):
        return pltpu.make_async_copy(tb.at[lax.rem(c, 2)], mlp_o.at[chunk(c)], tsem.at[lax.rem(c, 2)])

    def mlp_chunk(c, _):
        r = chunk(c)
        s = lax.rem(c, 2)
        for cp in chunk_loads(c):
            cp.wait()

        @pl.when(c + 1 < nc)
        def _():
            for cp in chunk_loads(c + 1):
                cp.start()

        @pl.when(c == 0)
        def _():
            loads[0].wait()
            loads[1].wait()
            loads[2].wait()

        gate = nn(hb[s], gw[...])
        upper = nn(hb[s], uw[...])
        ga = nt(cb[s], dw[...])
        sigma = 1.0 / (1.0 + jnp.exp(-gate))
        silu = gate * sigma
        gg = (ga * upper * sigma * (1.0 + gate * (1.0 - sigma))).astype(bf16)
        gu = (ga * silu).astype(bf16)
        act = (silu * upper).astype(bf16)
        a3[0, r] = gg
        a3[1, r] = gu
        a3[2, r] = act
        own[r] = (nt(gg, gw[...]) + nt(gu, uw[...])).astype(bf16)
        tick(2 * c)

        @pl.when(c >= 2)
        def _():
            mlp_write(c - 2).wait()

        tb[s] = nn(act, dw[...]).astype(bf16)
        mlp_write(c).start()
        tick(2 * c + 1)
        return 0

    def unit(u):
        @pl.when(u == 0)
        def _():
            loads[3].wait()

        @pl.when(u == 4)
        def _():
            loads[4].start()
            loads[4].wait()

        which = u // 2
        cols = chunk(lax.rem(u, 2), MLP_WIDTH)
        rhs = a3[which, :, cols]
        for k in range(8):
            gsum.put_block(u, k, nn(side[k * 192:(k + 1) * 192], rhs))
        gsum.start(u)

    def beat(t, _):
        first = 2 * nc
        u = t - first
        pl.when(u < MLP_UNITS)(lambda: unit(u))
        tick(t)
        for k, lag in ((3, 9), (2, 5), (1, 1)):
            v = u - lag
            pl.when((v >= 0) & (v < MLP_UNITS))(functools.partial(gsum.stage, k, v))
        return 0

    lax.fori_loop(0, nc, mlp_chunk, 0)
    lax.fori_loop(2 * nc, nb + 4 * LAG, beat, 0)

    def drains(u, _):
        gsum.drain(u)
        return 0

    lax.fori_loop(0, MLP_UNITS, drains, 0)
    for c in range(max(nc - 2, 0), nc):
        mlp_write(c).wait()
    for j in range(nj - 2, nj):
        for c in gm_writes(j):
            c.wait()


def feed(gain2, hid2, cot, mid, hid2t, cott, gw, uw, dw):
    vm = pltpu.VMEM
    ff = gw.shape[1]
    return pl.pallas_call(
        feed_kernel,
        out_shape=(sds((ROW, D), bf16), sds((ROW, D), f32), sds((ROW, D), bf16), sds((D, ROW), bf16),
                   sds((1, D), f32), sds((D // 8, 3 * ff), f32)),
        in_specs=[VM] + [ANY] * 8,
        out_specs=(ANY, ANY, ANY, ANY, VM, VM),
        scratch_shapes=[
            vm((D, ff), bf16), vm((D, ff), bf16), vm((ff, D), bf16), vm((3, ROW, ff), bf16),
            vm((D, ROW), bf16), vm((ROW, D), bf16),
            vm((2, CH, D), bf16), vm((2, CH, D), bf16), vm((2, CH, D), bf16),
            vm((128, D), f32), vm((128, D), bf16), vm((2, 128, D), f32), vm((2, 128, D), bf16),
            vm((2, D, 128), bf16)]
        + ring_scratch(RING, BL) + sum_scratch(MLP_UNITS, MLP_WIDTH, MLP_WIDTH // 2)
        + [DMA((5,)), DMA((2, 2)), DMA((2,)), DMA((2,)), DMA((3, 2))],
        compiler_params=pltpu.CompilerParams(
            collective_id=2, has_side_effects=True, vmem_limit_bytes=63 * 2**20),
        name="feed_forward",
    )(gain2, hid2, cot, mid, hid2t, cott, gw, uw, dw)


BL3 = 32
RING3 = 10
LAG3 = 2
ATT_UNITS = 5
ATT_WIDTH = 256


def unrotate(u, co, si):
    a = u[0:HD // 2]
    b = u[HD // 2:HD]
    return jnp.concatenate([a * co + b * si, b * co - a * si], axis=0).astype(bf16)


def attend_back(qk, kk, vv, dot, ho, dk, dv, gt, cos, sin, g, gg, qb):
    lo = qb * CH
    hi = lo + CH
    heads = NZ * HQ_OWN * 128
    q = jnp.concatenate([qk[pl.ds(pl.multiple_of((2 * g + h) * 128, 128), 128), lo:hi] for h in range(2)], axis=1)
    parts = []
    for h in range(2):
        do = dot[pl.ds(pl.multiple_of((2 * gg + h) * HD, 32), HD), lo:hi]
        o = ho[pl.ds(pl.multiple_of((2 * g + h) * HD, 32), HD), lo:hi]
        delta = jnp.sum(do.astype(f32) * o.astype(f32), axis=0, keepdims=True)
        extra = extra_rows(jnp.zeros((128 - HD, CH), f32), -delta, 0)
        parts.append(jnp.concatenate([do, extra], axis=0))
    do = jnp.concatenate(parts, axis=1)
    do_t = do.T
    q_t = q.T
    dq = jnp.zeros((128, 2 * CH), f32)
    for kb in range(qb + 1):
        ks = slice(kb * CH, (kb + 1) * CH)
        p = jnp.exp2(nn(kk[g, ks, :], q) * C2)
        if kb == qb:
            ki = lax.broadcasted_iota(jnp.int32, (CH, CH), 0)
            qi = lax.broadcasted_iota(jnp.int32, (CH, CH), 1)
            keep = jnp.concatenate([ki <= qi, ki <= qi], axis=1)
            p = jnp.where(keep, p, 0.0)
        ds = (p * nn(vv[g, ks, :], do)).astype(bf16)
        dvb = nn(p.astype(bf16), do_t)
        dkb = nn(ds, q_t)
        if kb == qb:
            dv[ks, :] = dvb
            dk[ks, :] = dkb
        else:
            dv[ks, :] += dvb
            dk[ks, :] += dkb
        dq = dq + nn(qk[pl.ds(pl.multiple_of(heads + g * 128, 128), 128), ks], ds)
    first = (g // KV_OWN) * QKV + gg * 2 * HD
    for h in range(2):
        at = pl.ds(pl.multiple_of(first + h * HD, 32), HD)
        gt[at, lo:hi] = unrotate(dq[0:HD, h * CH:(h + 1) * CH] * SCALE, cos[:, lo:hi], sin[:, lo:hi])


def backward_kernel(groups, gain, cos, sin, gain2_i, x, mid, mlp, gm, gml_i, gmlt, hid1t, ho_i, qt_i, kt_i, kk_i, vv_i, w_i,
                    out_o, xg_o, grad_o,
                    w, wo, ho, qk, kk, vv, dk, dv, gt, gml, dot, ga1, own, mb2, ob2, xb, gb, ob,
                    rend, rmid, out, zs, ze, zm, zo,
                    c1, x1, y1, x2, y2, gs, gr,
                    lsem, bsem, wsem, psem, osem, isem):
    dp, z, low = places()
    qrows = NZ * HQ_OWN * 128
    loads = [pltpu.make_async_copy(gml_i, gml, lsem.at[0]),
             pltpu.make_async_copy(ho_i, ho, lsem.at[1]),
             pltpu.make_async_copy(kk_i, kk, lsem.at[2]),
             pltpu.make_async_copy(vv_i, vv, lsem.at[3])]
    loads += [pltpu.make_async_copy(w_i.at[s, pl.ds(QKV + 192 * h, 192)], wo.at[s // 2, s % 2, h], lsem.at[4 + 2 * s + h])
              for s in range(NZ) for h in range(2)]
    loads += [pltpu.make_async_copy(qt_i, qk.at[pl.ds(0, qrows)], lsem.at[12]),
              pltpu.make_async_copy(kt_i, qk.at[pl.ds(qrows, NZ * KV_OWN * 128)], lsem.at[13])]
    wloads = [pltpu.make_async_copy(w_i.at[s, pl.ds(0, QKV)], w.at[s], lsem.at[14 + s]) for s in range(NZ)]
    late = [pltpu.make_async_copy(hid1t, qk.at[pl.ds(0, D)], lsem.at[18]),
            pltpu.make_async_copy(gmlt, qk.at[pl.ds(D, D)], lsem.at[19])]
    nb = ROW // BL3
    nt_blocks = ROW // TB

    def own_load(i):
        s = lax.rem(i, RING3)
        return pltpu.make_async_copy(mlp.at[chunk(i, BL3)], own.at[s], isem.at[s])

    def mid_load(i):
        s = lax.rem(i, 2)
        return pltpu.make_async_copy(mid.at[chunk(i, BL3)], mb2.at[s], osem.at[0, s])

    def out_write(i):
        s = lax.rem(i, 2)
        return pltpu.make_async_copy(ob2.at[s], out_o.at[chunk(i, BL3)], osem.at[1, s])

    own_load(0).start()
    own_load(1).start()
    mid_load(0).start()
    for c in loads:
        c.start()
    greet(dp, z, low)
    zsum = RowSum(z, lambda i: own.at[lax.rem(i, RING3)], rend, rmid, out, zs, ze, zm, zo, RING3, LAG3)
    gsum = GradSum(dp, low, ATT_WIDTH, ATT_WIDTH // 2, wo, c1, x1, y1, x2, y2, gs, gr, grad_o, True)

    def finish(i):
        mid_load(i).wait()
        s = lax.rem(i, 2)

        @pl.when(i >= 2)
        def _():
            out_write(i - 2).wait()

        ob2[s] = (mb2[s] + out[lax.rem(i, RING3)].astype(f32)).astype(bf16)
        out_write(i).start()

        @pl.when(i + 1 < nb)
        def _():
            mid_load(i + 1).start()

    def tick(t):
        pl.when(t < nb)(lambda: own_load(t).wait())
        zsum.tick(t, nb, finish)
        pl.when(t + 2 < nb)(lambda: own_load(t + 2).start())

    def quarter(s, _):
        @pl.when(s == 0)
        def _():
            for c in loads:
                c.wait()
            for c in wloads:
                c.start()

        for h in range(2):
            t = nt(wo[s // 2, lax.rem(s, 2), h], gml[...])
            dot[h * 192:(h + 1) * 192, :] = t.astype(bf16)
        tick(s * (1 + KV_OWN * 4))

        def one(gg, _):
            g = KV_OWN * s + gg
            for qb in range(ROW // CH):
                attend_back(qk, kk, vv, dot, ho, dk, dv, gt, cos, sin, g, gg, qb)
                tick(s * (1 + KV_OWN * 4) + 1 + gg * 4 + qb)
            first = pl.multiple_of(s * QKV + QR + gg * HD, 32)
            gt[pl.ds(first, HD), :] = unrotate(dk[...].T[0:HD] * SCALE, cos[...], sin[...])
            gt[pl.ds(pl.multiple_of(first + KR, 32), HD), :] = dv[...].T[0:HD].astype(bf16)
            return 0

        lax.fori_loop(0, KV_OWN, one, 0)
        return 0

    lax.fori_loop(0, NZ, quarter, 0)
    beats = NZ * (1 + KV_OWN * 4)
    for c in late:
        c.start()
    for c in wloads + late:
        c.wait()

    def qkv_unit(u, _):
        rhs = gt[pl.ds(pl.multiple_of(z * QKV + u * ATT_WIDTH, 128), ATT_WIDTH), :]
        for k in range(8):
            gsum.put_block(u, k, nt(qk[k * 192:(k + 1) * 192, :], rhs))
        gsum.start(u)
        tick(beats + u)

        pl.when(u >= 1)(lambda: gsum.stage(1, u - 1))
        return 0

    lax.fori_loop(0, QKV // ATT_WIDTH, qkv_unit, 0)
    beats += QKV // ATT_WIDTH
    o_at = pl.multiple_of(z * QR, 128)
    for k in range(8):
        gsum.put_block(3, k, nt(qk[D + k * 192:D + (k + 1) * 192, :], ho[pl.ds(o_at, ATT_WIDTH), :]))
    gsum.start(3)
    for k in range(8):
        r = nt(qk[D + k * 192:D + (k + 1) * 192, :], ho[pl.ds(o_at + ATT_WIDTH, QR - ATT_WIDTH), :])
        gsum.put_part(4, k, 0, QR - ATT_WIDTH, r)
    gsum.stage(1, 2)

    def tail_loads(b, slot):
        r = chunk(b, TB)
        return [pltpu.make_async_copy(x.at[r], xb.at[slot], bsem.at[0, slot]),
                pltpu.make_async_copy(gm.at[r], gb.at[slot], bsem.at[1, slot])]

    def out_copy(b, slot):
        return pltpu.make_async_copy(ob.at[slot], xg_o.at[chunk(b, TB)], psem.at[slot])

    for c in tail_loads(0, 0):
        c.start()
    ga1[...] = jnp.zeros_like(ga1)

    def tail(b, _):
        slot = lax.rem(b, 2)

        @pl.when(b + 1 < nt_blocks)
        def _():
            for c in tail_loads(b + 1, 1 - slot):
                c.start()

        r = chunk(b, TB)
        acc = jnp.zeros((TB, D), f32)
        for s in range(NZ):
            acc = acc + tn(gt[QKV * s:QKV * s + QKV, r], w[s])
        for c in tail_loads(b, slot):
            c.wait()

        @pl.when(b >= 2)
        def _():
            out_copy(b - 2, slot).wait()

        xx = xb[slot].astype(f32)
        f = lax.rsqrt(jnp.mean(xx * xx, axis=1, keepdims=True) + eps)
        n = xx * f
        gn = acc * n
        ga1[...] += jnp.sum(gn, axis=0, keepdims=True)
        ga = gain[...].astype(f32)
        res = gb[slot] + f * (acc * ga - n * jnp.mean(gn * ga, axis=1, keepdims=True))
        ob[slot] = res.astype(bf16)
        out_copy(b, slot).start()
        tick(beats + b)
        pl.when(b == 0)(lambda: gsum.stage(1, 3))
        pl.when((b >= 1) & (b < 5))(lambda: gsum.stage(2, b - 1))
        pl.when(b >= 4)(lambda: gsum.stage(3, b - 4))
        return 0

    lax.fori_loop(0, nt_blocks, tail, 0)
    beats += nt_blocks
    row = lax.broadcasted_iota(jnp.int32, (128, D), 0)
    both = by_block(jnp.where(row == 0, ga1[...], jnp.where(row == 1, gain2_i[...], 0.0)).T, groups)
    for k in range(8):
        gsum.put_part(4, k, QR - ATT_WIDTH, ATT_WIDTH, both[k * 192:(k + 1) * 192])
    gsum.start(4)

    def rest(t, _):
        tick(t)
        return 0

    if beats < nb + 4 * LAG3:
        lax.fori_loop(beats, nb + 4 * LAG3, rest, 0)
    for k in (1, 2, 3):
        gsum.stage(k, 4)

    def drains(u, _):
        gsum.drain(u)
        return 0

    lax.fori_loop(0, ATT_UNITS, drains, 0)
    for b in range(nt_blocks - 2, nt_blocks):
        out_copy(b, b % 2).wait()
    for i in (nb - 2, nb - 1):
        out_write(i).wait()


def backward(groups, gain, cos, sin, gain2_sum, x, mid, mlp, gm, gml, gmlt, hid1t, ho, qt, kt, kk, vv, w):
    vm = pltpu.VMEM
    heads = NZ * HQ_OWN
    kv = NZ * KV_OWN
    return pl.pallas_call(
        functools.partial(backward_kernel, groups),
        out_shape=(sds((ROW, D), bf16), sds((ROW, D), bf16), sds((D // 8, ATT_UNITS * ATT_WIDTH), f32)),
        in_specs=[VM] * 4 + [ANY] * 13,
        out_specs=(ANY, ANY, VM),
        scratch_shapes=[
            vm((NZ, QKV, D), bf16), vm((2, 2, 2, 192, D), bf16), vm((heads * HD, ROW), bf16),
            vm(((heads + kv) * 128, ROW), bf16), vm((kv, ROW, 128), bf16), vm((kv, ROW, 128), bf16),
            vm((ROW, 128), f32), vm((ROW, 128), f32), vm((NZ * QKV, ROW), bf16),
            vm((ROW, D), bf16), vm((QR, ROW), bf16), vm((1, D), f32),
            vm((RING3, BL3, D), bf16), vm((2, BL3, D), f32), vm((2, BL3, D), bf16),
            vm((2, TB, D), bf16), vm((2, TB, D), f32), vm((2, TB, D), bf16)]
        + ring_scratch(RING3, BL3) + sum_scratch(ATT_UNITS, ATT_WIDTH, ATT_WIDTH // 2)[1:]
        + [DMA((20,)), DMA((2, 2)), DMA((2,)), DMA((2,)), DMA((2, 2)), DMA((RING3,))],
        compiler_params=pltpu.CompilerParams(
            collective_id=3, has_side_effects=True, vmem_limit_bytes=63 * 2**20),
        name="attention_backward",
    )(gain, cos, sin, gain2_sum, x, mid, mlp, gm, gml, gmlt, hid1t, ho, qt, kt, kk, vv, w)


def by_block(v, groups):
    if groups == 1:
        return v
    rows, cols = v.shape
    return v.reshape(groups, 8, rows // (8 * groups), cols).transpose(1, 0, 2, 3).reshape(rows, cols)


def body(groups, inputs, lengths, q_weight, k_weight, v_weight, o_weight, gate_weight, up_weight, down_weight,
         attn_gain, mlp_gain, cotangent):
    x = inputs.reshape(ROW, D)
    cot = cotangent.reshape(ROW, D)
    gain = attn_gain.reshape(1, D)
    gain2 = mlp_gain.reshape(1, D)
    ff = gate_weight.shape[1]
    cos, sin, qaug, kaug = tables(lengths[0])
    own = jnp.concatenate([q_weight.T, k_weight.T, v_weight.T, o_weight], axis=0)
    mid, hid2, ho, qt, kt, kk, vv, w, hid1t, hid2t, cott = forward(x, gain, gain2, cos, sin, qaug, kaug, own, cot)
    mlp, gm, gml, gmlt, gain2_sum, mlp_grad = feed(
        gain2, hid2, cot, mid, by_block(hid2t, groups), by_block(cott, groups), gate_weight, up_weight, down_weight)
    output, input_grad, att_grad = backward(
        groups, gain, cos, sin, gain2_sum, x, mid, mlp, gm, gml, by_block(gmlt, groups), by_block(hid1t, groups),
        ho, qt.reshape(-1, ROW), kt.reshape(-1, ROW), kk, vv, w)
    if groups > 1:
        n = 8 * groups
        same = [[g * 8 + low for g in range(groups)] for low in range(8)]

        def over(v):
            return lax.psum_scatter(v, "dp", scatter_dimension=0, axis_index_groups=same, tiled=True)

        mlp_grad, att_grad = over(mlp_grad), over(att_grad)
    return (output.reshape(1, ROW, D), input_grad.reshape(1, ROW, D), att_grad[:, 0:QR], att_grad[:, QR:QR + KR],
            att_grad[:, QR + KR:QKV], att_grad[:, QKV:WR].T, mlp_grad[:, 0:ff], mlp_grad[:, ff:2 * ff],
            mlp_grad[:, 2 * ff:].T, att_grad[:, WR], att_grad[:, WR + 1])


def solution(mesh):
    row = P("dp", None, None)
    in_specs = (row, P("dp", None), P(None, "mp"), P(None, "mp"), P(None, "mp"), P("mp", None),
                P(None, "mp"), P(None, "mp"), P("mp", None), P(), P(), row)
    out_specs = (row, row, P("dp", "mp"), P("dp", "mp"), P("dp", "mp"), P("mp", "dp"),
                 P("dp", "mp"), P("dp", "mp"), P("mp", "dp"), P("dp"), P("dp"))
    return jax.shard_map(functools.partial(body, mesh.shape["dp"] // 8), mesh=mesh, in_specs=in_specs,
                         out_specs=out_specs, check_vma=False)
```

```python
import functools

import jax
import jax.numpy as jnp
from jax import lax
from jax.experimental import pallas as pl
from jax.experimental.pallas import tpu as pltpu
from jax.sharding import PartitionSpec as P

D = 1536
HD = 96
ROW = 1024
SEGS = 4
NZ = 4
CH = 256
TB = 128
BL = 64
LAG = 2
RING = 10
HQ_OWN = 4
KV_OWN = 2
QR = HQ_OWN * HD
KR = KV_OWN * HD
QKV = QR + 2 * KR
WR = QKV + QR
SCALE = HD ** -0.5
C2 = SCALE * 1.4426950408889634
NEG = -1e30
eps = 1e-05
rope_base = 100000.0
f32 = jnp.float32
bf16 = jnp.bfloat16
MESH = pl.DeviceIdType.MESH
ANY = pl.BlockSpec(memory_space=pl.ANY)
VM = pl.BlockSpec(memory_space=pltpu.VMEM)
DMA = pltpu.SemaphoreType.DMA
sds = jax.ShapeDtypeStruct


def nt(a, b):
    return lax.dot_general(a, b, (((1,), (1,)), ((), ())), preferred_element_type=f32)


def nn(a, b):
    return lax.dot_general(a, b, (((1,), (0,)), ((), ())), preferred_element_type=f32)


def tn(a, b):
    return lax.dot_general(a, b, (((0,), (0,)), ((), ())), preferred_element_type=f32)


def chunk(c, size=CH):
    return pl.ds(pl.multiple_of(c * size, size), size)


def places():
    dp = lax.axis_index("dp")
    z = lax.axis_index("mp")
    low = lax.rem(dp, 8)
    return dp, z, low


def partner(low, dp, bit):
    on = lax.rem(low // bit, 2)
    return dp + bit - 2 * bit * on


def flip(low, mask):
    for bit in (1, 2, 4):
        if mask & bit:
            low = low + bit - 2 * bit * lax.rem(low // bit, 2)
    return low


def greet(dp, z, low, masks=(1, 2, 4)):
    barrier = pltpu.get_barrier_semaphore()
    for mask in masks:
        pl.semaphore_signal(barrier, inc=1, device_id={"dp": dp - low + flip(low, mask)}, device_id_type=MESH)
    for other in (1, 2, 3):
        pl.semaphore_signal(barrier, inc=1, device_id={"mp": lax.rem(z + other, NZ)}, device_id_type=MESH)
    pl.semaphore_wait(barrier, len(masks) + 3)


def put(src, dst, ssem, rsem, dev):
    return pltpu.make_async_remote_copy(
        src_ref=src, dst_ref=dst, send_sem=ssem, recv_sem=rsem, device_id=dev, device_id_type=MESH)


def split3(v):
    hi = v.astype(bf16).astype(f32)
    rest = v - hi
    mid = rest.astype(bf16).astype(f32)
    return hi, mid, rest - mid


def extra_rows(base, v, first):
    row = lax.broadcasted_iota(jnp.int32, base.shape, 0)
    out = base
    for i, part in enumerate(split3(v)):
        out = jnp.where(row == first + i, part, out)
    return out.astype(bf16)


def project(w, hid, qt, kt, kk, vt, vv, cos, sin, qaug, kaug, s, c):
    cols = chunk(c)
    t = nt(w[s, 0:QKV], hid[cols])
    co = cos[:, cols]
    si = sin[:, cols]

    def rot(u):
        a = u[0:HD // 2]
        b = u[HD // 2:HD]
        return jnp.concatenate([a * co - b * si, b * co + a * si], axis=0).astype(bf16)

    for h in range(HQ_OWN):
        qt[HQ_OWN * s + h, 0:HD, cols] = rot(t[HD * h:HD * h + HD])
        qt[HQ_OWN * s + h, HD:128, cols] = qaug[:, cols]
    for h in range(KV_OWN):
        g = KV_OWN * s + h
        k = jnp.concatenate([rot(t[QR + HD * h:QR + HD * h + HD]), kaug[:, cols]], axis=0)
        kt[g, :, cols] = k
        kk[g, cols, :] = k.T
        v = t[QR + KR + HD * h:QR + KR + HD * h + HD].astype(bf16)
        v = jnp.concatenate([v, jnp.ones((128 - HD, CH), bf16)], axis=0)
        vt[g, :, cols] = v
        vv[g, cols, :] = v.T


def attend(qt, kk, vt, ho, qaug, g, between):
    for qb in range(ROW // CH):
        lo = qb * CH
        nk = lo + CH
        q = jnp.concatenate([qt[2 * g, :, lo:nk], qt[2 * g + 1, :, lo:nk]], axis=1)
        st = nn(kk[g, 0:nk, :], q)
        ki = lax.broadcasted_iota(jnp.int32, (CH, CH), 0)
        qi = lax.broadcasted_iota(jnp.int32, (CH, CH), 1)
        keep = jnp.concatenate([ki <= qi, ki <= qi], axis=1)
        dg = jnp.where(keep, st[lo:nk], NEG)
        m = jnp.max(dg, axis=0, keepdims=True)
        if qb:
            m = jnp.maximum(m, jnp.max(st[0:lo], axis=0, keepdims=True))
        mc = m * C2
        o = nn(vt[g, :, lo:nk], jnp.exp2(dg * C2 - mc).astype(bf16))
        if qb:
            o = o + nn(vt[g, :, 0:lo], jnp.exp2(st[0:lo] * C2 - mc).astype(bf16))
        total = o[HD:HD + 1]
        r = (o[0:HD] / total).astype(bf16)
        back = (mc + jnp.log2(total)) * (-1.0 / C2)
        for h in range(2):
            part = slice(h * CH, (h + 1) * CH)
            ho[pl.ds(pl.multiple_of(g * 2 * HD + h * HD, 32), HD), lo:nk] = r[:, part]
            base = qaug[:, lo:nk].astype(f32)
            qt[2 * g + h, HD:128, lo:nk] = extra_rows(base, back[:, part], SEGS)
        if qb % 2:
            between(qb // 2)


def order(z, j):
    places_of = (0, 1, 2, 3), (1, 0, 2, 3), (2, 3, 1, 0), (3, 2, 1, 0)
    s = jnp.int32(0)
    for i, of in enumerate(places_of):
        for k, quarter in enumerate(of):
            if quarter:
                s = s + jnp.where((z == i) & (j == k), quarter, 0)
    return s


EVENTS = {
    3: (("f", 0, 1), ("f", 0, 2), (1, 0, 1)),
    6: ((2, 0, 1),),
    7: (("f", 0, 3), ("s", 1, 0), (1, 0, 2)),
    ("before", 1): ((3, 0, 1), (1, 0, 3), (4, 0, 1)),
    8: ((2, 0, 2), ("f", 1, 1), ("f", 1, 2)),
    11: ((2, 0, 3),),
    13: ((1, 1, 1),),
    15: (("f", 1, 3),),
    ("before", 2): ((3, 0, 2), (4, 0, 2)),
    16: ((1, 1, 2),),
    20: ((3, 0, 3),),
    22: ((1, 1, 3), (2, 1, 1)),
    ("before", 3): ((4, 0, 3),),
    26: ((2, 1, 2),),
    27: ((3, 1, 1),),
    29: ((2, 1, 3), (3, 1, 2)),
    ("before", 4): ((3, 1, 3),),
}
QSLICE = QKV // 8
OSLICE = QR // 8


def forward_kernel(lengths, gains, cos, sin, x_i, qw_i, kw, vw, ow, cot,
                   mid_o, hid2_o, ho_o, qt_o, kt_o, kk_o, vv_o, w_o, hid1t_o, hid2t_o, cott_o,
                   x, qw, w, hid, ho, qt, kt, kk, vt, vv, qaug, kaug, midb, hidb, hidtb, cb, ctb,
                   zsend, zrecv, xsend, xrecv, ysend, yrecv, csend, crecv, osem, wsem, msem, tsem):
    dp, z, low = places()
    pc, px, py = (partner(low, dp, bit) for bit in (1, 2, 4))
    lx = px - dp + low
    ly = py - dp + low
    lxy = ly + lx - low
    c_at, x_at, y_at = lax.rem(low, 2), lax.rem(low // 2, 2), low // 4
    own = [pltpu.make_async_copy(qw_i, qw, wsem.at[0])]
    own += [pltpu.make_async_copy(src, w.at[z, pl.ds(at, n)], wsem.at[i + 1])
            for i, (src, at, n) in enumerate(((kw, QR, KR), (vw, QR + KR, KR), (ow, QKV, QR)))]
    own += [pltpu.make_async_copy(x_i, x, wsem.at[4])]
    for c in own:
        c.start()
    greet(dp, z, low)
    own[0].wait()
    w[z, 0:QR] = qw[...].T
    own[1].wait()
    own[2].wait()

    def qrows(at, lo=0, hi=QSLICE):
        return pl.ds(pl.multiple_of(at * QSLICE + lo, 16), hi - lo)

    def orows(half, at, core):
        return pl.ds(pl.multiple_of(QKV + half * (QR // 2) + (2 * at + core) * OSLICE, 16), OSLICE)

    def zcopies(part, s, side):
        to = jnp.clip(z + 2 * side - 1, 0, NZ - 1)
        if part == 0:
            slices = ((0, qrows(low)),)
        else:
            slices = ((1, orows(0, y_at, c_at)), (2, orows(1, x_at, c_at)))
        return [put(w.at[s, r], w.at[s, r], zsend.at[i, s, side], zrecv.at[i, s], {"mp": to}) for i, r in slices]

    def send_own(part):
        def go(side):
            for c in zcopies(part, z, side):
                c.start()

        for side in (0, 1):
            pl.when((z < NZ - 1) if side else (z > 0))(functools.partial(go, side))

    send_own(0)
    own[3].wait()
    own[4].wait()

    def copies(part, j, kind):
        s = order(z, j)

        def c(r, sems, semr, i, dev):
            return put(w.at[s, r], w.at[s, r], sems.at[part, j - 1, i], semr.at[part, j - 1, i], {"dp": dev})

        if part == 1:
            if kind == 1:
                return [c(orows(0, y_at, c_at), ysend, yrecv, 0, py), c(orows(1, x_at, c_at), xsend, xrecv, 0, px)]
            return [c(orows(half, at, c_at), csend, crecv, 2 * half + at, pc) for half in (0, 1) for at in (0, 1)]
        cut = QSLICE // 2
        if kind == 1:
            return [c(qrows(low, 0, cut), xsend, xrecv, 0, px), c(qrows(low, cut), ysend, yrecv, 0, py)]
        if kind == 2:
            return [c(qrows(low, 0, cut), ysend, yrecv, 1, py), c(qrows(lx, 0, cut), ysend, yrecv, 2, py),
                    c(qrows(low, cut), xsend, xrecv, 1, px), c(qrows(ly, cut), xsend, xrecv, 2, px)]
        return [c(qrows(at), csend, crecv, i, pc) for i, at in enumerate((low, lx, ly, lxy))]

    def kinds(part):
        return range(1, 3 if part else 4)

    inner = (z > 0) & (z < NZ - 1)

    def pass_on(part, j):
        s = order(z, j)
        return s, jnp.where(s < z, 1, 0)

    def do(kind, part, j):
        if kind == "s":
            send_own(part)
        elif kind == "f":
            @pl.when(inner)
            def _():
                s, side = pass_on(part, j)
                for c in zcopies(part, s, side):
                    c.wait_recv()
                    c.start()
        else:
            if kind == 1:
                @pl.when(jnp.logical_not(inner))
                def _():
                    for c in zcopies(part, order(z, j), 0):
                        c.wait_recv()
            else:
                for c in copies(part, j, kind - 1):
                    c.wait_recv()
            if kind in kinds(part):
                for c in copies(part, j, kind):
                    c.start()

    def beat(step):
        for at, events in EVENTS.items():
            if isinstance(at, int):
                @pl.when(step == at)
                def _(events=events):
                    for e in events:
                        do(*e)

    def before(j):
        for e in EVENTS.get(("before", j), ()):
            do(*e)

    place = lax.broadcasted_iota(jnp.int32, (1, ROW), 1)
    row = lax.broadcasted_iota(jnp.int32, (128 - HD, ROW), 0)
    segment = jnp.zeros((1, ROW), jnp.int32)
    finish = jnp.int32(0)
    for i in range(SEGS):
        finish = finish + lengths[0, i]
        segment = segment + jnp.where(place >= finish, 1, 0)
    same = row == segment
    qaug[...] = jnp.where(same | (row >= SEGS), 0.0, NEG).astype(bf16)
    kaug[...] = jnp.where(same | ((row >= SEGS) & (row < SEGS + 3)), 1.0, 0.0).astype(bf16)

    def norm(c, _):
        r = chunk(c)
        xx = x[r].astype(f32)
        f = lax.rsqrt(jnp.mean(xx * xx, axis=1, keepdims=True) + eps)
        hid[r] = (xx * f * gains[0:1, :].astype(f32)).astype(bf16)
        return 0

    def turn_copy(i):
        s = lax.rem(i, 2)
        n = ROW // CH
        cols = chunk(lax.rem(i, n))
        return (pltpu.make_async_copy(ctb.at[s], hid1t_o.at[:, cols], tsem.at[0, s]),
                pltpu.make_async_copy(ctb.at[s], cott_o.at[:, cols], tsem.at[0, s]))

    def cot_load(c):
        s = lax.rem(c, 2)
        return pltpu.make_async_copy(cot.at[chunk(c)], cb.at[s], tsem.at[1, s])

    def turn_hid(c, _):
        pl.when(c >= 2)(lambda: turn_copy(c - 2)[0].wait())
        ctb[lax.rem(c, 2)] = hid[chunk(c)].T
        turn_copy(c)[0].start()
        return 0

    def turn_cot(c, _):
        cot_load(c).wait()
        turn_copy(c + 2)[0].wait()
        ctb[lax.rem(c, 2)] = cb[lax.rem(c, 2)].T
        turn_copy(c)[1].start()
        pl.when(c + 2 < ROW // CH)(lambda: cot_load(c + 2).start())
        return 0

    cot_load(0).start()
    cot_load(1).start()
    lax.fori_loop(0, ROW // CH, norm, 0)

    def results(j):
        s = order(z, j)
        h = pl.ds(s * HQ_OWN, HQ_OWN)
        g = pl.ds(s * KV_OWN, KV_OWN)
        r = pl.ds(0, QKV)
        pairs = [(w.at[s, r], w_o.at[s, r]), (qt.at[h], qt_o.at[h]), (kt.at[g], kt_o.at[g]),
                 (kk.at[g], kk_o.at[g]), (vv.at[g], vv_o.at[g])]
        return [pltpu.make_async_copy(a, b, osem.at[j, i]) for i, (a, b) in enumerate(pairs)]

    def quarter(j, _):
        s = order(z, j)
        for i in range(1, NZ):
            @pl.when(j == i)
            def _(i=i):
                if i == 1:
                    lax.fori_loop(0, ROW // CH, turn_hid, 0)
                    lax.fori_loop(0, ROW // CH, turn_cot, 0)
                before(i)

        def one(c, _):
            project(w, hid, qt, kt, kk, vt, vv, cos, sin, qaug, kaug, s, c)
            beat(8 * j + c)
            return 0

        lax.fori_loop(0, ROW // CH, one, 0)

        def two(g, _):
            attend(qt, kk, vt, ho, qaug, KV_OWN * s + g, lambda half: beat(8 * j + 4 + 2 * g + half))
            return 0

        lax.fori_loop(0, KV_OWN, two, 0)
        for c in results(j):
            c.start()
        return 0

    lax.fori_loop(0, NZ, quarter, 0)
    before(NZ)
    last = [pltpu.make_async_copy(ho, ho_o, osem.at[NZ, 0])]
    last += [pltpu.make_async_copy(w.at[s, pl.ds(QKV, QR)], w_o.at[s, pl.ds(QKV, QR)], osem.at[NZ, 1 + s])
             for s in range(NZ)]
    for c in last:
        c.start()

    def mid_copies(c, slot):
        return (pltpu.make_async_copy(midb.at[slot], mid_o.at[chunk(c)], msem.at[0, slot]),
                pltpu.make_async_copy(hidb.at[slot], hid2_o.at[chunk(c)], msem.at[1, slot]),
                pltpu.make_async_copy(hidtb.at[slot], hid2t_o.at[:, chunk(c)], msem.at[2, slot]))

    def out_proj(c, _):
        r = chunk(c)
        slot = lax.rem(c, 2)

        @pl.when(c >= 2)
        def _():
            for m in mid_copies(c - 2, slot):
                m.wait()

        acc = x[r].astype(f32)
        for s in range(NZ):
            acc = acc + tn(ho[QR * s:QR * s + QR, r], w[s, QKV:WR])
        midb[slot] = acc
        f = lax.rsqrt(jnp.mean(acc * acc, axis=1, keepdims=True) + eps)
        h = (acc * f * gains[1:2, :].astype(f32)).astype(bf16)
        hidb[slot] = h
        hidtb[slot] = h.T
        for m in mid_copies(c, slot):
            m.start()
        return 0

    n = ROW // CH
    lax.fori_loop(0, n, out_proj, 0)
    for c in range(max(n - 2, 0), n):
        for m in mid_copies(c, c % 2):
            m.wait()
        turn_copy(c)[1].wait()
    for j in range(NZ):
        for c in results(j):
            c.wait()
    for c in last:
        c.wait()
    for part in range(2):
        def sent(s, side, part=part):
            for c in zcopies(part, s, side):
                c.wait_send()

        for side in (0, 1):
            pl.when((z < NZ - 1) if side else (z > 0))(functools.partial(sent, z, side))
        for j in (1, 2, 3):
            pl.when(inner)(functools.partial(lambda j: sent(*pass_on(part, j)), j))
            for kind in kinds(part):
                for c in copies(part, j, kind):
                    c.wait_send()


def forward(lengths, x, gains, cos, sin, qw, kw, vw, ow, cot):
    heads = NZ * HQ_OWN
    kv = NZ * KV_OWN
    vm = pltpu.VMEM
    return pl.pallas_call(
        forward_kernel,
        out_shape=(sds((ROW, D), f32), sds((ROW, D), bf16), sds((heads * HD, ROW), bf16),
                   sds((heads, 128, ROW), bf16), sds((kv, 128, ROW), bf16), sds((kv, ROW, 128), bf16),
                   sds((kv, ROW, 128), bf16), sds((NZ, WR, D), bf16), sds((D, ROW), bf16), sds((D, ROW), bf16),
                   sds((D, ROW), bf16)),
        in_specs=[pl.BlockSpec(memory_space=pltpu.SMEM)] + [VM] * 3 + [ANY] * 6,
        out_specs=(ANY,) * 11,
        scratch_shapes=[
            vm((ROW, D), bf16), vm((D, QR), bf16), vm((NZ, WR, D), bf16), vm((ROW, D), bf16), vm((heads * HD, ROW), bf16),
            vm((heads, 128, ROW), bf16), vm((kv, 128, ROW), bf16), vm((kv, ROW, 128), bf16),
            vm((kv, 128, ROW), bf16), vm((kv, ROW, 128), bf16),
            vm((128 - HD, ROW), bf16), vm((128 - HD, ROW), bf16), vm((2, CH, D), f32), vm((2, CH, D), bf16),
            vm((2, D, CH), bf16), vm((2, CH, D), bf16), vm((2, D, CH), bf16),
            DMA((3, NZ, 2)), DMA((3, NZ)), DMA((2, 3, 3)), DMA((2, 3, 3)), DMA((2, 3, 3)), DMA((2, 3, 3)),
            DMA((2, 3, 4)), DMA((2, 3, 4)), DMA((NZ + 1, 5)), DMA((5,)), DMA((3, 2)), DMA((2, 2))],
        compiler_params=pltpu.CompilerParams(
            collective_id=1, has_side_effects=True, vmem_limit_bytes=60 * 2**20),
        name="attention_forward",
    )(lengths, gains, cos, sin, x, qw, kw, vw, ow, cot)


def angles_of(lengths):
    place = jnp.arange(ROW, dtype=jnp.int32)
    start = jnp.zeros((ROW,), jnp.int32)
    finish = jnp.int32(0)
    for i in range(SEGS - 1):
        finish = finish + lengths[i]
        start = jnp.where(place >= finish, finish, start)
    positions = (place - start).astype(f32)
    freqs = rope_base ** (-(jnp.arange(HD // 2, dtype=f32) * 2.0) / HD)
    angles = freqs[:, None] * positions[None, :]
    return jnp.cos(angles), jnp.sin(angles)


class RowSum:
    def __init__(self, z, own, rend, rmid, out, ssem, esem, msem, osem, ring, lag):
        self.z, self.own, self.ring, self.lag = z, own, ring, lag
        self.rend, self.rmid, self.out = rend, rmid, out
        self.ssem, self.esem, self.msem, self.osem = ssem, esem, msem, osem

    def who(self, i):
        odd = lax.rem(i, 2)
        return 3 * odd, 1 + odd, 2 - odd, 3 - 3 * odd

    def copy(self, kind, i, to, sem=0):
        s = lax.rem(i, self.ring)
        src, dst, rsem = {
            "end": (self.own(i), self.rend.at[s], self.esem),
            "mid": (self.rmid.at[s], self.rmid.at[s], self.msem),
            "out": (self.out.at[s], self.out.at[s], self.osem)}[kind]
        return put(src, dst, self.ssem.at[sem, s], rsem.at[s], {"mp": to})

    def on(self, place, f):
        pl.when(self.z == place)(f)

    def step1(self, i):
        e, o, m, f = self.who(i)
        self.on(e, lambda: self.copy("end", i, o).start())
        self.on(f, lambda: self.copy("end", i, m).start())

    def step2(self, i):
        e, o, m, f = self.who(i)
        s = lax.rem(i, self.ring)

        def go():
            self.copy("end", i, o).wait_recv()
            self.rmid[s] = (self.own(i)[...].astype(f32) + self.rend[s].astype(f32)).astype(bf16)
            self.copy("mid", i, o).start()

        self.on(m, go)

    def step3(self, i):
        e, o, m, f = self.who(i)
        s = lax.rem(i, self.ring)

        def go():
            self.copy("end", i, e).wait_recv()
            self.copy("mid", i, e).wait_recv()
            self.out[s] = (self.own(i)[...].astype(f32) + self.rend[s].astype(f32)
                           + self.rmid[s].astype(f32)).astype(bf16)
            self.copy("out", i, m, 1).start()
            self.copy("out", i, e).start()

        self.on(o, go)

    def step4(self, i):
        e, o, m, f = self.who(i)

        def go():
            self.copy("out", i, o).wait_recv()
            self.copy("out", i, f, 1).start()

        self.on(m, go)

    def arrive(self, i):
        e, o, m, f = self.who(i)
        self.on(e, lambda: self.copy("out", i, o).wait_recv())
        self.on(f, lambda: self.copy("out", i, m).wait_recv())

    def drain(self, i):
        e, o, m, f = self.who(i)
        self.on(e, lambda: self.copy("end", i, o).wait_send())
        self.on(f, lambda: self.copy("end", i, m).wait_send())

        def middle():
            self.copy("mid", i, o).wait_send()
            self.copy("out", i, f, 1).wait_send()

        def owner():
            self.copy("out", i, m, 1).wait_send()
            self.copy("out", i, e).wait_send()

        self.on(m, middle)
        self.on(o, owner)

    def tick(self, t, count, finish):
        def last(i):
            self.arrive(i)
            finish(i)
            self.drain(i)

        for lag, step in ((4, last), (3, self.step4), (2, self.step3), (1, self.step2), (0, self.step1)):
            i = t - lag * self.lag
            pl.when((i >= 0) & (i < count))(functools.partial(step, i))


class GradSum:
    def __init__(self, dp, low, width, cut, g, c1, x1, y1, x2, y2, ssem, rsem, emit, wide=False):
        self.pc, self.px, self.py = (partner(low, dp, bit) for bit in (1, 2, 4))
        self.c, self.x, self.y = lax.rem(low, 2), lax.rem(low // 2, 2), low // 4
        self.g, self.c1, self.x1, self.y1, self.x2, self.y2 = g, c1, x1, y1, x2, y2
        self.ssem, self.rsem, self.emit = ssem, rsem, emit
        self.width, self.cut, self.wide = width, cut, wide

    def cols(self, u, lo, hi):
        if self.wide:
            return (pl.ds(pl.multiple_of(u * self.width + lo, 128), hi - lo),)
        return (pl.ds(lo, hi - lo),)

    def part(self, u, *at, lo=None, hi=None):
        lo, hi = (0, self.width) if lo is None else (lo, hi)
        return (() if self.wide else (u,)) + at + self.cols(u, lo, hi)

    def put_block(self, u, k, res):
        self.put_part(u, k, 0, self.width, res)

    def put_part(self, u, k, lo, hi, res):
        self.g[self.part(u, k // 4, (k // 2) % 2, k % 2, slice(None), lo=lo, hi=hi)] = res.astype(bf16)

    def copies(self, u, k):
        g, c, x, y = self.g, self.c, self.x, self.y
        every = slice(None)
        a = dict(lo=0, hi=self.cut)
        b = dict(lo=self.cut, hi=self.width)

        def mk(i, src, dst, dev):
            return put(src, dst, self.ssem.at[u, i], self.rsem.at[u, i], {"dp": dev})

        if k == 0:
            return [mk(0, g.at[self.part(u, every, every, 1 - c, every)], self.c1.at[u], self.pc)]
        if k == 1:
            return [mk(1, g.at[self.part(u, every, 1 - x, c, every, **a)], self.x1.at[u], self.px),
                    mk(2, g.at[self.part(u, 1 - y, every, c, every, **b)], self.y1.at[u], self.py)]
        return [mk(3, g.at[self.part(u, 1 - y, x, c, every, **a)], self.y2.at[u], self.py),
                mk(4, g.at[self.part(u, y, 1 - x, c, every, **b)], self.x2.at[u], self.px)]

    def start(self, u):
        for c in self.copies(u, 0):
            c.start()

    def stage(self, k, u):
        width, cut = self.width, self.cut
        g, c, x, y = self.g, self.c, self.x, self.y
        for cp in self.copies(u, k - 1):
            cp.wait_recv()

        def at(i, j, lo, hi):
            return self.part(u, i, j, c, slice(None), lo=lo, hi=hi)

        def add(i, j, lo, hi, other):
            g[at(i, j, lo, hi)] = (g[at(i, j, lo, hi)].astype(f32) + other.astype(f32)).astype(bf16)

        if k == 1:
            for i in range(2):
                for j in range(2):
                    add(i, j, 0, width, self.c1[u, i, j])
        elif k == 2:
            for i in range(2):
                add(i, x, 0, cut, self.x1[u, i])
                add(y, i, cut, width, self.y1[u, i])
        else:
            self.emit(u, 0, cut, g[at(y, x, 0, cut)].astype(f32) + self.y2[u].astype(f32))
            self.emit(u, cut, width, g[at(y, x, cut, width)].astype(f32) + self.x2[u].astype(f32))
        if k < 3:
            for cp in self.copies(u, k):
                cp.start()

    def drain(self, u):
        for k in range(3):
            for cp in self.copies(u, k):
                cp.wait_send()


def sum_scratch(count, width, cut):
    vm = pltpu.VMEM
    rest = width - cut
    return [vm((count, 2, 2, 2, 192, width), bf16), vm((count, 2, 2, 192, width), bf16),
            vm((count, 2, 192, cut), bf16), vm((count, 2, 192, rest), bf16),
            vm((count, 192, rest), bf16), vm((count, 192, cut), bf16), DMA((count, 5)), DMA((count, 5))]


def ring_scratch(ring, rows):
    vm = pltpu.VMEM
    return [vm((ring, rows, D), bf16), vm((ring, rows, D), bf16), vm((ring, rows, D), bf16),
            DMA((2, ring)), DMA((ring,)), DMA((ring,)), DMA((ring,))]


MLP_UNITS = 6
MLP_WIDTH = 512


def feed_kernel(gains, hid2, cot, mid, hid2t_i, cott_i, gw_i, uw_i, dw_i,
                mlp_o, gm_o, gml_o, gmlt_o, gain2_o, gate_o, up_o, down_o,
                gw, uw, dw, a3, side, own, hb, cb, tb, mb, cb2, gmb, gmlb, gmltb,
                rend, rmid, out, zs, ze, zm, zo,
                g, c1, x1, y1, x2, y2, gs, gr,
                lsem, bsem, tsem, msem, wsem):
    dp, z, low = places()
    loads = [pltpu.make_async_copy(a, b, lsem.at[i]) for i, (a, b) in enumerate(
        ((gw_i, gw), (uw_i, uw), (dw_i, dw), (hid2t_i, side), (cott_i, side)))]
    nc = ROW // CH
    nb = ROW // BL
    nj = ROW // 128
    pair = 128 // BL

    def chunk_loads(c):
        return [pltpu.make_async_copy(src.at[chunk(c)], dst.at[lax.rem(c, 2)], bsem.at[i, lax.rem(c, 2)])
                for i, (src, dst) in enumerate(((hid2, hb), (cot, cb)))]

    for c in chunk_loads(0):
        c.start()
    for c in loads[:4]:
        c.start()
    greet(dp, z, low)
    def emit(u, lo, hi, v):
        half = lax.rem(u, 2) * MLP_WIDTH
        at = pl.ds(pl.multiple_of(half + lo, 128), hi - lo)
        for i, ref in enumerate((gate_o, up_o, down_o)):
            @pl.when(u // 2 == i)
            def _(ref=ref):
                ref[:, at] = v

    zsum = RowSum(z, lambda i: own.at[chunk(i, BL)], rend, rmid, out, zs, ze, zm, zo, RING, LAG)
    gsum = GradSum(dp, low, MLP_WIDTH, MLP_WIDTH // 2, g, c1, x1, y1, x2, y2, gs, gr, emit)
    gain2_o[...] = jnp.zeros_like(gain2_o)

    def gm_loads(j):
        r = chunk(j, 128)
        return [pltpu.make_async_copy(mid.at[r], mb, msem.at[0]),
                pltpu.make_async_copy(cot.at[r], cb2, msem.at[1])]

    def gm_writes(j):
        r = chunk(j, 128)
        s = lax.rem(j, 2)
        return [pltpu.make_async_copy(gmb.at[s], gm_o.at[r], wsem.at[0, s]),
                pltpu.make_async_copy(gmlb.at[s], gml_o.at[r], wsem.at[1, s]),
                pltpu.make_async_copy(gmltb.at[s], gmlt_o.at[:, r], wsem.at[2, s])]

    def finish_pair(j):
        s = lax.rem(j, 2)
        for c in gm_loads(j):
            c.wait()

        @pl.when(j >= 2)
        def _():
            for c in gm_writes(j - 2):
                c.wait()

        gh = jnp.concatenate([out[lax.rem(j * pair + k, RING)] for k in range(pair)], axis=0).astype(f32)
        m = mb[...]
        f = lax.rsqrt(jnp.mean(m * m, axis=1, keepdims=True) + eps)
        n = m * f
        gn = gh * n
        gain2_o[...] += jnp.sum(gn, axis=0, keepdims=True)
        ga = gains[1:2, :].astype(f32)
        gm = cb2[...].astype(f32) + f * (gh * ga - n * jnp.mean(gn * ga, axis=1, keepdims=True))
        gmb[s] = gm
        low_gm = gm.astype(bf16)
        gmlb[s] = low_gm
        gmltb[s] = low_gm.T
        for c in gm_writes(j):
            c.start()

        @pl.when(j + 1 < nj)
        def _():
            for c in gm_loads(j + 1):
                c.start()

    def finish(i):
        pl.when(lax.rem(i, pair) == pair - 1)(lambda: finish_pair(i // pair))

    for c in gm_loads(0):
        c.start()

    def tick(t):
        zsum.tick(t, nb, finish)

    def mlp_write(c):
        return pltpu.make_async_copy(tb.at[lax.rem(c, 2)], mlp_o.at[chunk(c)], tsem.at[lax.rem(c, 2)])

    def mlp_chunk(c, _):
        r = chunk(c)
        s = lax.rem(c, 2)
        for cp in chunk_loads(c):
            cp.wait()

        @pl.when(c + 1 < nc)
        def _():
            for cp in chunk_loads(c + 1):
                cp.start()

        @pl.when(c == 0)
        def _():
            loads[0].wait()
            loads[1].wait()
            loads[2].wait()

        gate = nn(hb[s], gw[...])
        upper = nn(hb[s], uw[...])
        ga = nt(cb[s], dw[...])
        sigma = 1.0 / (1.0 + jnp.exp(-gate))
        silu = gate * sigma
        gg = (ga * upper * sigma * (1.0 + gate * (1.0 - sigma))).astype(bf16)
        gu = (ga * silu).astype(bf16)
        act = (silu * upper).astype(bf16)
        a3[0, r] = gg
        a3[1, r] = gu
        a3[2, r] = act
        own[r] = (nt(gg, gw[...]) + nt(gu, uw[...])).astype(bf16)
        tick(2 * c)

        @pl.when(c >= 2)
        def _():
            mlp_write(c - 2).wait()

        tb[s] = nn(act, dw[...]).astype(bf16)
        mlp_write(c).start()
        tick(2 * c + 1)
        return 0

    def unit(u):
        @pl.when(u == 0)
        def _():
            loads[3].wait()

        @pl.when(u == 4)
        def _():
            loads[4].start()
            loads[4].wait()

        which = u // 2
        cols = chunk(lax.rem(u, 2), MLP_WIDTH)
        rhs = a3[which, :, cols]
        for k in range(8):
            gsum.put_block(u, k, nn(side[k * 192:(k + 1) * 192], rhs))
        gsum.start(u)

    def beat(t, _):
        first = 2 * nc
        u = t - first
        pl.when(u < MLP_UNITS)(lambda: unit(u))
        tick(t)
        for k, lag in ((3, 9), (2, 5), (1, 1)):
            v = u - lag
            pl.when((v >= 0) & (v < MLP_UNITS))(functools.partial(gsum.stage, k, v))
        return 0

    lax.fori_loop(0, nc, mlp_chunk, 0)
    lax.fori_loop(2 * nc, nb + 4 * LAG, beat, 0)

    def drains(u, _):
        gsum.drain(u)
        return 0

    lax.fori_loop(0, MLP_UNITS, drains, 0)
    for c in range(max(nc - 2, 0), nc):
        mlp_write(c).wait()
    for j in range(nj - 2, nj):
        for c in gm_writes(j):
            c.wait()


def feed(gains, hid2, cot, mid, hid2t, cott, gw, uw, dw):
    vm = pltpu.VMEM
    ff = gw.shape[1]
    return pl.pallas_call(
        feed_kernel,
        out_shape=(sds((ROW, D), bf16), sds((ROW, D), f32), sds((ROW, D), bf16), sds((D, ROW), bf16),
                   sds((1, D), f32), sds((D // 8, ff), f32), sds((D // 8, ff), f32), sds((D // 8, ff), f32)),
        in_specs=[VM] + [ANY] * 8,
        out_specs=(ANY, ANY, ANY, ANY, VM, VM, VM, VM),
        scratch_shapes=[
            vm((D, ff), bf16), vm((D, ff), bf16), vm((ff, D), bf16), vm((3, ROW, ff), bf16),
            vm((D, ROW), bf16), vm((ROW, D), bf16),
            vm((2, CH, D), bf16), vm((2, CH, D), bf16), vm((2, CH, D), bf16),
            vm((128, D), f32), vm((128, D), bf16), vm((2, 128, D), f32), vm((2, 128, D), bf16),
            vm((2, D, 128), bf16)]
        + ring_scratch(RING, BL) + sum_scratch(MLP_UNITS, MLP_WIDTH, MLP_WIDTH // 2)
        + [DMA((5,)), DMA((2, 2)), DMA((2,)), DMA((2,)), DMA((3, 2))],
        compiler_params=pltpu.CompilerParams(
            collective_id=2, has_side_effects=True, vmem_limit_bytes=63 * 2**20),
        name="feed_forward",
    )(gains, hid2, cot, mid, hid2t, cott, gw, uw, dw)


BL3 = 64
RING3 = 10
LAG3 = 2
WIDTH = QR
CUT = 128


def unrotate(u, co, si):
    a = u[0:HD // 2]
    b = u[HD // 2:HD]
    return jnp.concatenate([a * co + b * si, b * co - a * si], axis=0).astype(bf16)


def attend_back(qk, kk, vv, dot, ho, dk, dv, gt, cos, sin, g, gg, qb):
    lo = qb * CH
    hi = lo + CH
    heads = NZ * HQ_OWN * 128
    q = jnp.concatenate([qk[pl.ds(pl.multiple_of((2 * g + h) * 128, 128), 128), lo:hi] for h in range(2)], axis=1)
    parts = []
    for h in range(2):
        do = dot[pl.ds(pl.multiple_of((2 * gg + h) * HD, 32), HD), lo:hi]
        o = ho[pl.ds(pl.multiple_of((2 * g + h) * HD, 32), HD), lo:hi]
        delta = jnp.sum(do.astype(f32) * o.astype(f32), axis=0, keepdims=True)
        extra = extra_rows(jnp.zeros((128 - HD, CH), f32), -delta, 0)
        parts.append(jnp.concatenate([do, extra], axis=0))
    do = jnp.concatenate(parts, axis=1)
    do_t = do.T
    q_t = q.T
    dq = jnp.zeros((128, 2 * CH), f32)
    for kb in range(qb + 1):
        ks = slice(kb * CH, (kb + 1) * CH)
        p = jnp.exp2(nn(kk[g, ks, :], q) * C2)
        if kb == qb:
            ki = lax.broadcasted_iota(jnp.int32, (CH, CH), 0)
            qi = lax.broadcasted_iota(jnp.int32, (CH, CH), 1)
            keep = jnp.concatenate([ki <= qi, ki <= qi], axis=1)
            p = jnp.where(keep, p, 0.0)
        ds = (p * nn(vv[g, ks, :], do)).astype(bf16)
        dvb = nn(p.astype(bf16), do_t)
        dkb = nn(ds, q_t)
        if kb == qb:
            dv[ks, :] = dvb
            dk[ks, :] = dkb
        else:
            dv[ks, :] += dvb
            dk[ks, :] += dkb
        dq = dq + nn(qk[pl.ds(pl.multiple_of(heads + g * 128, 128), 128), ks], ds)
    first = (g // KV_OWN) * QKV + gg * 2 * HD
    for h in range(2):
        at = pl.ds(pl.multiple_of(first + h * HD, 32), HD)
        gt[at, lo:hi] = unrotate(dq[0:HD, h * CH:(h + 1) * CH] * SCALE, cos[:, lo:hi], sin[:, lo:hi])


def backward_kernel(groups, gains, cos, sin, gain2_i, x, mid, mlp, gm, gml_i, gmlt, hid1t, ho_i, qt_i, kt_i, kk_i, vv_i, w_i,
                    out_o, xg_o, qg_o, kg_o, vg_o, og_o, gains_o,
                    w, wo, ho, qk, kk, vv, dk, dv, gt, gml, dot, ga1, own, mb2, ob2, xb, gb, ob,
                    rend, rmid, out, zs, ze, zm, zo,
                    c1, x1, y1, x2, y2, gs, gr, og, oc1, ox1, oy1, ox2, oy2, ogs, ogr, tb, gsend, grecv,
                    lsem, bsem, wsem, psem, osem, isem, tsem, ssem, rsem):
    dp, z, low = places()
    qrows = NZ * HQ_OWN * 128
    loads = [pltpu.make_async_copy(ho_i, ho, lsem.at[1]),
             pltpu.make_async_copy(gml_i, gml, lsem.at[0]),
             pltpu.make_async_copy(kk_i, kk, lsem.at[2]),
             pltpu.make_async_copy(vv_i, vv, lsem.at[3])]
    loads += [pltpu.make_async_copy(w_i.at[s, pl.ds(QKV + 192 * h, 192)], wo.at[s // 2, s % 2, h], lsem.at[4 + 2 * s + h])
              for s in range(NZ) for h in range(2)]
    loads += [pltpu.make_async_copy(qt_i, qk.at[pl.ds(0, qrows)], lsem.at[12]),
              pltpu.make_async_copy(kt_i, qk.at[pl.ds(qrows, NZ * KV_OWN * 128)], lsem.at[13])]
    wloads = [pltpu.make_async_copy(w_i.at[s, pl.ds(0, QKV)], w.at[s], lsem.at[14 + s]) for s in range(NZ)]
    late = [pltpu.make_async_copy(hid1t, qk.at[pl.ds(0, D)], lsem.at[18])]
    nb = ROW // BL3
    nt_blocks = ROW // TB

    def own_load(i):
        s = lax.rem(i, RING3)
        return pltpu.make_async_copy(mlp.at[chunk(i, BL3)], own.at[s], isem.at[s])

    def mid_load(i):
        s = lax.rem(i, 2)
        return pltpu.make_async_copy(mid.at[chunk(i, BL3)], mb2.at[s], osem.at[0, s])

    def out_write(i):
        s = lax.rem(i, 2)
        return pltpu.make_async_copy(ob2.at[s], out_o.at[chunk(i, BL3)], osem.at[1, s])

    def turned_load(k):
        return pltpu.make_async_copy(gmlt.at[pl.ds(k * 192, 192)], tb.at[k % 2], tsem.at[k % 2])

    own_load(0).start()
    own_load(1).start()
    mid_load(0).start()
    turned_load(0).start()
    turned_load(1).start()
    for c in loads:
        c.start()
    greet(dp, z, low, range(1, 8))
    zsum = RowSum(z, lambda i: own.at[lax.rem(i, RING3)], rend, rmid, out, zs, ze, zm, zo, RING3, LAG3)

    def emit(u, lo, hi, v):
        if u == 0:
            qg_o[:, lo:hi] = v
            return
        for ref, first in ((kg_o, 0), (vg_o, KR)):
            a, b = max(lo, first), min(hi, first + KR)
            if a < b:
                ref[:, a - first:b - first] = v[:, a - lo:b - lo]

    def emit_o(u, lo, hi, v):
        og_o[:, lo:hi] = v

    gsum = GradSum(dp, low, WIDTH, CUT, wo, c1, x1, y1, x2, y2, gs, gr, emit, True)
    osum = GradSum(dp, low, WIDTH, CUT, og, oc1, ox1, oy1, ox2, oy2, ogs, ogr, emit_o)

    def finish(i):
        mid_load(i).wait()
        s = lax.rem(i, 2)

        @pl.when(i >= 2)
        def _():
            out_write(i - 2).wait()

        ob2[s] = (mb2[s] + out[lax.rem(i, RING3)].astype(f32)).astype(bf16)
        out_write(i).start()

        @pl.when(i + 1 < nb)
        def _():
            mid_load(i + 1).start()

    per = 64 // BL3

    def tick(beat):
        for k in range(per):
            t = beat * per + k
            pl.when(t < nb)(functools.partial(lambda t: own_load(t).wait(), t))
            zsum.tick(t, nb, finish)
            pl.when(t + 2 < nb)(functools.partial(lambda t: own_load(t + 2).start(), t))

    tick(0)
    loads[0].wait()
    o_rows = ho[pl.ds(pl.multiple_of(z * QR, 128), QR), :]
    for k in range(8):
        turned_load(k).wait()
        osum.put_block(0, k, nt(tb[k % 2], o_rows))
        if k + 2 < 8:
            turned_load(k + 2).start()
    osum.start(0)
    tick(1)
    for c in loads[1:]:
        c.wait()
    for c in wloads:
        c.start()

    def extra(g):
        return (5 * g + 4) // 8

    def quarter(s, _):
        for h in range(2):
            t = nt(wo[s // 2, lax.rem(s, 2), h], gml[...])
            dot[h * 192:(h + 1) * 192, :] = t.astype(bf16)

        def one(gg, _):
            g = KV_OWN * s + gg
            for qb in range(ROW // CH):
                attend_back(qk, kk, vv, dot, ho, dk, dv, gt, cos, sin, g, gg, qb)
                if qb == 2:
                    pl.when(extra(g + 1) > extra(g))(lambda: tick(2 + g + extra(g)))
                if qb == 3:
                    tick(2 + g + extra(g + 1))
            first = pl.multiple_of(s * QKV + QR + gg * HD, 32)
            gt[pl.ds(first, HD), :] = unrotate(dk[...].T[0:HD] * SCALE, cos[...], sin[...])
            gt[pl.ds(pl.multiple_of(first + KR, 32), HD), :] = dv[...].T[0:HD].astype(bf16)
            return 0

        lax.fori_loop(0, KV_OWN, one, 0)
        for k in (1, 2, 3):
            pl.when(s == k - 1)(functools.partial(osum.stage, k, 0))
        return 0

    lax.fori_loop(0, NZ, quarter, 0)
    beats = 2 + 13
    for c in late:
        c.start()
    for c in wloads + late:
        c.wait()

    for u in range(2):
        rhs = gt[pl.ds(pl.multiple_of(z * QKV + u * WIDTH, 128), WIDTH), :]
        for k in range(8):
            gsum.put_block(u, k, nt(qk[k * 192:(k + 1) * 192, :], rhs))
        gsum.start(u)
        tick(beats + u)
    beats += 2

    def tail_loads(b, slot):
        r = chunk(b, TB)
        return [pltpu.make_async_copy(x.at[r], xb.at[slot], bsem.at[0, slot]),
                pltpu.make_async_copy(gm.at[r], gb.at[slot], bsem.at[1, slot])]

    def out_copy(b, slot):
        return pltpu.make_async_copy(ob.at[slot], xg_o.at[chunk(b, TB)], psem.at[slot])

    for c in tail_loads(0, 0):
        c.start()
    ga1[...] = jnp.zeros_like(ga1)

    def tail(b, _):
        slot = lax.rem(b, 2)

        @pl.when(b + 1 < nt_blocks)
        def _():
            for c in tail_loads(b + 1, 1 - slot):
                c.start()

        r = chunk(b, TB)
        acc = jnp.zeros((TB, D), f32)
        for s in range(NZ):
            acc = acc + tn(gt[QKV * s:QKV * s + QKV, r], w[s])
        for c in tail_loads(b, slot):
            c.wait()

        @pl.when(b >= 2)
        def _():
            out_copy(b - 2, slot).wait()

        xx = xb[slot].astype(f32)
        f = lax.rsqrt(jnp.mean(xx * xx, axis=1, keepdims=True) + eps)
        n = xx * f
        gn = acc * n
        ga1[...] += jnp.sum(gn, axis=0, keepdims=True)
        ga = gains[0:1, :].astype(f32)
        res = gb[slot] + f * (acc * ga - n * jnp.mean(gn * ga, axis=1, keepdims=True))
        ob[slot] = res.astype(bf16)
        out_copy(b, slot).start()
        pl.when(lax.rem(b, 2) == 1)(lambda: tick(beats + b // 2))
        pl.when(b == 0)(lambda: (gsum.stage(1, 0), gsum.stage(1, 1)) and None)
        pl.when(b == 2)(lambda: gsum.stage(2, 0))
        pl.when(b == 4)(lambda: gsum.stage(2, 1))
        pl.when(b == 6)(lambda: gsum.stage(3, 0))
        return 0

    lax.fori_loop(0, nt_blocks, tail, 0)
    beats += nt_blocks // 2

    def gains_copy(mask):
        to = flip(low, mask)
        return put(gsend.at[to], grecv.at[low], ssem.at[mask], rsem.at[mask], {"dp": dp - low + to})

    share = D // 8 // groups
    for k in range(8):
        for i, v in enumerate((ga1, gain2_i)):
            gsend[k, i:i + 1, 0:D // 8] = jnp.concatenate(
                [v[:, (g * 8 + k) * share:(g * 8 + k + 1) * share] for g in range(groups)], axis=1)
    for mask in range(1, 8):
        gains_copy(mask).start()

    def rest(t, _):
        tick(t)
        return 0

    ends = (nb + 4 * LAG3 + per - 1) // per
    if beats < ends:
        lax.fori_loop(beats, ends, rest, 0)
    gsum.stage(3, 1)
    total = gsend[low]
    for mask in range(1, 8):
        gains_copy(mask).wait_recv()
        total = total + grecv[flip(low, mask)]
    gains_o[...] = total
    for mask in range(1, 8):
        gains_copy(mask).wait_send()
    for u in range(2):
        gsum.drain(u)
    osum.drain(0)
    for b in range(nt_blocks - 2, nt_blocks):
        out_copy(b, b % 2).wait()
    for i in (nb - 2, nb - 1):
        out_write(i).wait()


def backward(groups, gains, cos, sin, gain2_sum, x, mid, mlp, gm, gml, gmlt, hid1t, ho, qt, kt, kk, vv, w):
    vm = pltpu.VMEM
    heads = NZ * HQ_OWN
    kv = NZ * KV_OWN
    return pl.pallas_call(
        functools.partial(backward_kernel, groups),
        out_shape=(sds((ROW, D), bf16), sds((ROW, D), bf16), sds((D // 8, QR), f32), sds((D // 8, KR), f32),
                   sds((D // 8, KR), f32), sds((D // 8, QR), f32), sds((8, 256), f32)),
        in_specs=[VM] * 4 + [ANY] * 13,
        out_specs=(ANY, ANY) + (VM,) * 5,
        scratch_shapes=[
            vm((NZ, QKV, D), bf16), vm((2, 2, 2, 192, D), bf16), vm((heads * HD, ROW), bf16),
            vm(((heads + kv) * 128, ROW), bf16), vm((kv, ROW, 128), bf16), vm((kv, ROW, 128), bf16),
            vm((ROW, 128), f32), vm((ROW, 128), f32), vm((NZ * QKV, ROW), bf16),
            vm((ROW, D), bf16), vm((QR, ROW), bf16), vm((1, D), f32),
            vm((RING3, BL3, D), bf16), vm((2, BL3, D), f32), vm((2, BL3, D), bf16),
            vm((2, TB, D), bf16), vm((2, TB, D), f32), vm((2, TB, D), bf16)]
        + ring_scratch(RING3, BL3) + sum_scratch(2, WIDTH, CUT)[1:] + sum_scratch(1, WIDTH, CUT)
        + [vm((2, 192, ROW), bf16), vm((8, 8, 256), f32), vm((8, 8, 256), f32),
           DMA((19,)), DMA((2, 2)), DMA((2,)), DMA((2,)), DMA((2, 2)), DMA((RING3,)), DMA((2,)), DMA((8,)), DMA((8,))],
        compiler_params=pltpu.CompilerParams(
            collective_id=3, has_side_effects=True, vmem_limit_bytes=63 * 2**20),
        name="attention_backward",
    )(gains, cos, sin, gain2_sum, x, mid, mlp, gm, gml, gmlt, hid1t, ho, qt, kt, kk, vv, w)


def by_block(v, groups):
    if groups == 1:
        return v
    rows, cols = v.shape
    return v.reshape(groups, 8, rows // (8 * groups), cols).transpose(1, 0, 2, 3).reshape(rows, cols)


def body(groups, inputs, lengths, q_weight, k_weight, v_weight, o_weight, gate_weight, up_weight, down_weight,
         attn_gain, mlp_gain, cotangent):
    x = inputs.reshape(ROW, D)
    cot = cotangent.reshape(ROW, D)
    first = lax.broadcasted_iota(jnp.int32, (2, D), 0) == 0
    gains = jnp.where(first, attn_gain[None, :], mlp_gain[None, :])
    cos, sin = angles_of(lengths[0])
    mid, hid2, ho, qt, kt, kk, vv, w, hid1t, hid2t, cott = forward(
        lengths, x, gains, cos, sin, q_weight, k_weight.T, v_weight.T, o_weight, cot)
    mlp, gm, gml, gmlt, gain2_sum, gate_g, up_g, down_g = feed(
        gains, hid2, cot, mid, by_block(hid2t, groups), by_block(cott, groups), gate_weight, up_weight, down_weight)
    output, input_grad, q_g, k_g, v_g, o_g, gain_sums = backward(
        groups, gains, cos, sin, gain2_sum, x, mid, mlp, gm, gml, by_block(gmlt, groups), by_block(hid1t, groups),
        ho, qt.reshape(-1, ROW), kt.reshape(-1, ROW), kk, vv, w)
    grads = [q_g, k_g, v_g, o_g, gate_g, up_g, down_g, gain_sums]
    if groups > 1:
        same = [[g * 8 + low for g in range(groups)] for low in range(8)]
        grads = [lax.psum_scatter(v, "dp", scatter_dimension=int(i == 7), axis_index_groups=same, tiled=True)
                 for i, v in enumerate(grads[:7] + [gain_sums[:, 0:D // 8]])]
    output, input_grad, *grads = hand_over(output, input_grad, *grads)
    grads[3], grads[6] = grads[3].T, grads[6].T
    grads[7:] = grads[7][0, 0:D // 8 // groups], grads[7][1, 0:D // 8 // groups]
    return (output.reshape(1, ROW, D), input_grad.reshape(1, ROW, D), *grads)


def hand_over_kernel(n, *refs):
    held, load, store = refs[2 * n:3 * n], refs[3 * n], refs[3 * n + 1]
    pieces = []
    for i in range(n):
        rows = held[i].shape[0]
        parts = 4 if rows % 64 == 0 and rows > 512 else 1
        pieces += [(i, pl.ds(p * (rows // parts), rows // parts)) for p in range(parts)]
    first = [pltpu.make_async_copy(refs[i].at[r], held[i].at[r], load.at[k]) for k, (i, r) in enumerate(pieces)]
    then = [pltpu.make_async_copy(held[i].at[r], refs[n + i].at[r], store.at[k]) for k, (i, r) in enumerate(pieces)]
    for c in first:
        c.start()
    for a, b in zip(first, then):
        a.wait()
        b.start()
    for c in then:
        c.wait()


def hand_over(*arrays):
    n = len(arrays)
    return pl.pallas_call(
        functools.partial(hand_over_kernel, n),
        out_shape=tuple(sds(v.shape, v.dtype) for v in arrays),
        in_specs=[ANY] * n,
        out_specs=(ANY,) * n,
        scratch_shapes=[pltpu.VMEM(v.shape, v.dtype) for v in arrays] + [DMA((4 * n,)), DMA((4 * n,))],
        compiler_params=pltpu.CompilerParams(vmem_limit_bytes=63 * 2**20),
        name="hand_over",
    )(*arrays)


def solution(mesh):
    row = P("dp", None, None)
    in_specs = (row, P("dp", None), P(None, "mp"), P(None, "mp"), P(None, "mp"), P("mp", None),
                P(None, "mp"), P(None, "mp"), P("mp", None), P(), P(), row)
    out_specs = (row, row, P("dp", "mp"), P("dp", "mp"), P("dp", "mp"), P("mp", "dp"),
                 P("dp", "mp"), P("dp", "mp"), P("mp", "dp"), P("dp"), P("dp"))
    return jax.shard_map(functools.partial(body, mesh.shape["dp"] // 8), mesh=mesh, in_specs=in_specs,
                         out_specs=out_specs, check_vma=False)
```

```python
import functools

import jax
import jax.numpy as jnp
import numpy as np
from jax import lax
from jax.experimental import pallas as pl
from jax.experimental.pallas import tpu as pltpu
from jax.sharding import PartitionSpec as P

D = 1536
HD = 96
ROW = 1024
SEGS = 4
NZ = 4
CH = 256
TB = 128
BL = 32
LAG = 4
RING = 18
BL3 = 64
AHEAD = 4
HQ_OWN = 4
KV_OWN = 2
QR = HQ_OWN * HD
KR = KV_OWN * HD
QKV = QR + 2 * KR
WR = QKV + QR
SCALE = HD ** -0.5
C2 = SCALE * 1.4426950408889634
NEG = -1e30
eps = 1e-05
rope_base = 100000.0
f32 = jnp.float32
bf16 = jnp.bfloat16
MESH = pl.DeviceIdType.MESH
ANY = pl.BlockSpec(memory_space=pl.ANY)
VM = pl.BlockSpec(memory_space=pltpu.VMEM)
DMA = pltpu.SemaphoreType.DMA
sds = jax.ShapeDtypeStruct


def nt(a, b):
    return lax.dot_general(a, b, (((1,), (1,)), ((), ())), preferred_element_type=f32)


def nn(a, b):
    return lax.dot_general(a, b, (((1,), (0,)), ((), ())), preferred_element_type=f32)


def tn(a, b):
    return lax.dot_general(a, b, (((0,), (0,)), ((), ())), preferred_element_type=f32)


def chunk(c, size=CH):
    return pl.ds(pl.multiple_of(c * size, size), size)


def places():
    dp = lax.axis_index("dp")
    z = lax.axis_index("mp")
    low = lax.rem(dp, 8)
    return dp, z, low


def partner(low, dp, bit):
    on = lax.rem(low // bit, 2)
    return dp + bit - 2 * bit * on


def flip(low, mask):
    for bit in (1, 2, 4):
        if mask & bit:
            low = low + bit - 2 * bit * lax.rem(low // bit, 2)
    return low


def greet(dp, z, low, masks=(1, 2, 4)):
    barrier = pltpu.get_barrier_semaphore()
    for mask in masks:
        pl.semaphore_signal(barrier, inc=1, device_id={"dp": dp - low + flip(low, mask)}, device_id_type=MESH)
    for other in (1, 2, 3):
        pl.semaphore_signal(barrier, inc=1, device_id={"mp": lax.rem(z + other, NZ)}, device_id_type=MESH)
    pl.semaphore_wait(barrier, len(masks) + 3)


def put(src, dst, ssem, rsem, dev):
    return pltpu.make_async_remote_copy(
        src_ref=src, dst_ref=dst, send_sem=ssem, recv_sem=rsem, device_id=dev, device_id_type=MESH)


def split3(v):
    hi = v.astype(bf16).astype(f32)
    rest = v - hi
    mid = rest.astype(bf16).astype(f32)
    return hi, mid, rest - mid


def extra_rows(base, v, first):
    row = lax.broadcasted_iota(jnp.int32, base.shape, 0)
    out = base
    for i, part in enumerate(split3(v)):
        out = jnp.where(row == first + i, part, out)
    return out.astype(bf16)


def project(w, hid, qt, kt, kk, vt, vv, cos, sin, qaug, kaug, s, c):
    cols = chunk(c)
    t = nt(w[s, 0:QKV], hid[cols])
    co = cos[:, cols]
    si = sin[:, cols]

    def rot(u):
        a = u[0:HD // 2]
        b = u[HD // 2:HD]
        return jnp.concatenate([a * co - b * si, b * co + a * si], axis=0).astype(bf16)

    for h in range(HQ_OWN):
        qt[HQ_OWN * s + h, 0:HD, cols] = rot(t[HD * h:HD * h + HD])
        qt[HQ_OWN * s + h, HD:128, cols] = qaug[:, cols]
    for h in range(KV_OWN):
        g = KV_OWN * s + h
        k = jnp.concatenate([rot(t[QR + HD * h:QR + HD * h + HD]), kaug[:, cols]], axis=0)
        kt[g, :, cols] = k
        kk[g, cols, :] = k.T
        v = t[QR + KR + HD * h:QR + KR + HD * h + HD].astype(bf16)
        v = jnp.concatenate([v, jnp.ones((128 - HD, CH), bf16)], axis=0)
        vt[g, :, cols] = v
        vv[g, cols, :] = v.T


def attend(qt, kk, vt, ho, qaug, g, between):
    for qb in range(ROW // CH):
        lo = qb * CH
        nk = lo + CH
        q = jnp.concatenate([qt[2 * g, :, lo:nk], qt[2 * g + 1, :, lo:nk]], axis=1)
        st = nn(kk[g, 0:nk, :], q)
        ki = lax.broadcasted_iota(jnp.int32, (CH, CH), 0)
        qi = lax.broadcasted_iota(jnp.int32, (CH, CH), 1)
        keep = jnp.concatenate([ki <= qi, ki <= qi], axis=1)
        dg = jnp.where(keep, st[lo:nk], NEG)
        m = jnp.max(dg, axis=0, keepdims=True)
        if qb:
            m = jnp.maximum(m, jnp.max(st[0:lo], axis=0, keepdims=True))
        mc = m * C2
        o = nn(vt[g, :, lo:nk], jnp.exp2(dg * C2 - mc).astype(bf16))
        if qb:
            o = o + nn(vt[g, :, 0:lo], jnp.exp2(st[0:lo] * C2 - mc).astype(bf16))
        total = o[HD:HD + 1]
        r = (o[0:HD] / total).astype(bf16)
        back = (mc + jnp.log2(total)) * (-1.0 / C2)
        for h in range(2):
            part = slice(h * CH, (h + 1) * CH)
            ho[pl.ds(pl.multiple_of(g * 2 * HD + h * HD, 32), HD), lo:nk] = r[:, part]
            base = qaug[:, lo:nk].astype(f32)
            qt[2 * g + h, HD:128, lo:nk] = extra_rows(base, back[:, part], SEGS)
        if qb % 2:
            between(qb // 2)


def angle_tables(lengths, freqs, cos, sin):
    place = lax.broadcasted_iota(jnp.int32, (1, ROW), 1)
    start = jnp.zeros((1, ROW), jnp.int32)
    finish = jnp.int32(0)
    for i in range(SEGS - 1):
        finish = finish + lengths[0, i]
        start = jnp.where(place >= finish, finish, start)
    angles = freqs[...] * (place - start).astype(f32)
    cos[...] = jnp.cos(angles)
    sin[...] = jnp.sin(angles)


def order(z, j):
    places_of = (0, 1, 2, 3), (1, 0, 2, 3), (2, 3, 1, 0), (3, 2, 1, 0)
    s = jnp.int32(0)
    for i, of in enumerate(places_of):
        for k, quarter in enumerate(of):
            if quarter:
                s = s + jnp.where((z == i) & (j == k), quarter, 0)
    return s


EVENTS = {
    3: (("f", 0, 1), ("f", 0, 2), (1, 0, 1)),
    6: ((2, 0, 1),),
    7: (("f", 0, 3), ("s", 1, 0), (1, 0, 2)),
    ("before", 1): ((3, 0, 1), (1, 0, 3), (4, 0, 1)),
    8: ((2, 0, 2), ("f", 1, 1), ("f", 1, 2)),
    11: ((2, 0, 3),),
    13: ((1, 1, 1),),
    15: (("f", 1, 3),),
    ("before", 2): ((3, 0, 2), (4, 0, 2)),
    16: ((1, 1, 2),),
    20: ((3, 0, 3),),
    22: ((1, 1, 3), (2, 1, 1)),
    ("before", 3): ((4, 0, 3),),
    26: ((2, 1, 2),),
    27: ((3, 1, 1),),
    29: ((2, 1, 3), (3, 1, 2)),
    ("before", 4): ((3, 1, 3),),
}
QSLICE = QKV // 8
OSLICE = QR // 8


def forward_kernel(lengths, gains, freqs, x_i, qw_i, kw, vw, ow, cot,
                   mid_o, hid2_o, ho_o, qt_o, kt_o, kk_o, vv_o, w_o, hid1t_o, hid2t_o, cott_o,
                   cos, sin, x, qw, w, hid, ho, qt, kt, kk, vt, vv, qaug, kaug, midb, hidb, hidtb, cb, ctb,
                   zsend, zrecv, xsend, xrecv, ysend, yrecv, csend, crecv, osem, wsem, msem, tsem):
    dp, z, low = places()
    pc, px, py = (partner(low, dp, bit) for bit in (1, 2, 4))
    lx = px - dp + low
    ly = py - dp + low
    lxy = ly + lx - low
    c_at, x_at, y_at = lax.rem(low, 2), lax.rem(low // 2, 2), low // 4
    own = [pltpu.make_async_copy(qw_i, qw, wsem.at[0])]
    own += [pltpu.make_async_copy(src, w.at[z, pl.ds(at, n)], wsem.at[i + 1])
            for i, (src, at, n) in enumerate(((kw, QR, KR), (vw, QR + KR, KR), (ow, QKV, QR)))]
    own += [pltpu.make_async_copy(x_i, x, wsem.at[4])]
    for c in own:
        c.start()
    greet(dp, z, low)
    own[0].wait()
    w[z, 0:QR] = qw[...].T
    own[1].wait()
    own[2].wait()

    def qrows(at, lo=0, hi=QSLICE):
        return pl.ds(pl.multiple_of(at * QSLICE + lo, 16), hi - lo)

    def orows(half, at, core):
        return pl.ds(pl.multiple_of(QKV + half * (QR // 2) + (2 * at + core) * OSLICE, 16), OSLICE)

    def zcopies(part, s, side):
        to = jnp.clip(z + 2 * side - 1, 0, NZ - 1)
        if part == 0:
            slices = ((0, qrows(low)),)
        else:
            slices = ((1, orows(0, y_at, c_at)), (2, orows(1, x_at, c_at)))
        return [put(w.at[s, r], w.at[s, r], zsend.at[i, s, side], zrecv.at[i, s], {"mp": to}) for i, r in slices]

    def send_own(part):
        def go(side):
            for c in zcopies(part, z, side):
                c.start()

        for side in (0, 1):
            pl.when((z < NZ - 1) if side else (z > 0))(functools.partial(go, side))

    send_own(0)
    own[3].wait()
    own[4].wait()

    def copies(part, j, kind):
        s = order(z, j)

        def c(r, sems, semr, i, dev):
            return put(w.at[s, r], w.at[s, r], sems.at[part, j - 1, i], semr.at[part, j - 1, i], {"dp": dev})

        if part == 1:
            if kind == 1:
                return [c(orows(0, y_at, c_at), ysend, yrecv, 0, py), c(orows(1, x_at, c_at), xsend, xrecv, 0, px)]
            return [c(orows(half, at, c_at), csend, crecv, 2 * half + at, pc) for half in (0, 1) for at in (0, 1)]
        cut = QSLICE // 2
        if kind == 1:
            return [c(qrows(low, 0, cut), xsend, xrecv, 0, px), c(qrows(low, cut), ysend, yrecv, 0, py)]
        if kind == 2:
            return [c(qrows(low, 0, cut), ysend, yrecv, 1, py), c(qrows(lx, 0, cut), ysend, yrecv, 2, py),
                    c(qrows(low, cut), xsend, xrecv, 1, px), c(qrows(ly, cut), xsend, xrecv, 2, px)]
        return [c(qrows(at), csend, crecv, i, pc) for i, at in enumerate((low, lx, ly, lxy))]

    def kinds(part):
        return range(1, 3 if part else 4)

    inner = (z > 0) & (z < NZ - 1)

    def pass_on(part, j):
        s = order(z, j)
        return s, jnp.where(s < z, 1, 0)

    def do(kind, part, j):
        if kind == "s":
            send_own(part)
        elif kind == "f":
            @pl.when(inner)
            def _():
                s, side = pass_on(part, j)
                for c in zcopies(part, s, side):
                    c.wait_recv()
                    c.start()
        else:
            if kind == 1:
                @pl.when(jnp.logical_not(inner))
                def _():
                    for c in zcopies(part, order(z, j), 0):
                        c.wait_recv()
            else:
                for c in copies(part, j, kind - 1):
                    c.wait_recv()
            if kind in kinds(part):
                for c in copies(part, j, kind):
                    c.start()

    def beat(step):
        for at, events in EVENTS.items():
            if isinstance(at, int):
                @pl.when(step == at)
                def _(events=events):
                    for e in events:
                        do(*e)

    def before(j):
        for e in EVENTS.get(("before", j), ()):
            do(*e)

    angle_tables(lengths, freqs, cos, sin)
    place = lax.broadcasted_iota(jnp.int32, (1, ROW), 1)
    row = lax.broadcasted_iota(jnp.int32, (128 - HD, ROW), 0)
    segment = jnp.zeros((1, ROW), jnp.int32)
    finish = jnp.int32(0)
    for i in range(SEGS):
        finish = finish + lengths[0, i]
        segment = segment + jnp.where(place >= finish, 1, 0)
    same = row == segment
    qaug[...] = jnp.where(same | (row >= SEGS), 0.0, NEG).astype(bf16)
    kaug[...] = jnp.where(same | ((row >= SEGS) & (row < SEGS + 3)), 1.0, 0.0).astype(bf16)

    def norm(c, _):
        r = chunk(c)
        xx = x[r].astype(f32)
        f = lax.rsqrt(jnp.mean(xx * xx, axis=1, keepdims=True) + eps)
        hid[r] = (xx * f * gains[0:1, :].astype(f32)).astype(bf16)
        return 0

    def turn_copy(i):
        s = lax.rem(i, 2)
        n = ROW // CH
        cols = chunk(lax.rem(i, n))
        return (pltpu.make_async_copy(ctb.at[s], hid1t_o.at[:, cols], tsem.at[0, s]),
                pltpu.make_async_copy(ctb.at[s], cott_o.at[:, cols], tsem.at[0, s]))

    def cot_load(c):
        s = lax.rem(c, 2)
        return pltpu.make_async_copy(cot.at[chunk(c)], cb.at[s], tsem.at[1, s])

    def turn_hid(c, _):
        pl.when(c >= 2)(lambda: turn_copy(c - 2)[0].wait())
        ctb[lax.rem(c, 2)] = hid[chunk(c)].T
        turn_copy(c)[0].start()
        return 0

    def turn_cot(c, _):
        cot_load(c).wait()
        turn_copy(c + 2)[0].wait()
        ctb[lax.rem(c, 2)] = cb[lax.rem(c, 2)].T
        turn_copy(c)[1].start()
        pl.when(c + 2 < ROW // CH)(lambda: cot_load(c + 2).start())
        return 0

    cot_load(0).start()
    cot_load(1).start()
    lax.fori_loop(0, ROW // CH, norm, 0)

    def results(j):
        s = order(z, j)
        h = pl.ds(s * HQ_OWN, HQ_OWN)
        g = pl.ds(s * KV_OWN, KV_OWN)
        r = pl.ds(0, QKV)
        pairs = [(w.at[s, r], w_o.at[s, r]), (qt.at[h], qt_o.at[h]), (kt.at[g], kt_o.at[g]),
                 (kk.at[g], kk_o.at[g]), (vv.at[g], vv_o.at[g])]
        return [pltpu.make_async_copy(a, b, osem.at[j, i]) for i, (a, b) in enumerate(pairs)]

    def quarter(j, _):
        s = order(z, j)
        for i in range(1, NZ):
            @pl.when(j == i)
            def _(i=i):
                if i == 1:
                    lax.fori_loop(0, ROW // CH, turn_hid, 0)
                    lax.fori_loop(0, ROW // CH, turn_cot, 0)
                before(i)

        def one(c, _):
            project(w, hid, qt, kt, kk, vt, vv, cos, sin, qaug, kaug, s, c)
            beat(8 * j + c)
            return 0

        lax.fori_loop(0, ROW // CH, one, 0)

        def two(g, _):
            attend(qt, kk, vt, ho, qaug, KV_OWN * s + g, lambda half: beat(8 * j + 4 + 2 * g + half))
            return 0

        lax.fori_loop(0, KV_OWN, two, 0)
        for c in results(j):
            c.start()
        return 0

    lax.fori_loop(0, NZ, quarter, 0)
    before(NZ)
    last = [pltpu.make_async_copy(ho, ho_o, osem.at[NZ, 0])]
    last += [pltpu.make_async_copy(w.at[s, pl.ds(QKV, QR)], w_o.at[s, pl.ds(QKV, QR)], osem.at[NZ, 1 + s])
             for s in range(NZ)]
    for c in last:
        c.start()

    def mid_copies(c, slot):
        return (pltpu.make_async_copy(midb.at[slot], mid_o.at[chunk(c)], msem.at[0, slot]),
                pltpu.make_async_copy(hidb.at[slot], hid2_o.at[chunk(c)], msem.at[1, slot]),
                pltpu.make_async_copy(hidtb.at[slot], hid2t_o.at[:, chunk(c)], msem.at[2, slot]))

    def out_proj(c, _):
        r = chunk(c)
        slot = lax.rem(c, 2)

        @pl.when(c >= 2)
        def _():
            for m in mid_copies(c - 2, slot):
                m.wait()

        acc = x[r].astype(f32)
        for s in range(NZ):
            acc = acc + tn(ho[QR * s:QR * s + QR, r], w[s, QKV:WR])
        midb[slot] = acc
        f = lax.rsqrt(jnp.mean(acc * acc, axis=1, keepdims=True) + eps)
        h = (acc * f * gains[1:2, :].astype(f32)).astype(bf16)
        hidb[slot] = h
        hidtb[slot] = h.T
        for m in mid_copies(c, slot):
            m.start()
        return 0

    n = ROW // CH
    lax.fori_loop(0, n, out_proj, 0)
    for c in range(max(n - 2, 0), n):
        for m in mid_copies(c, c % 2):
            m.wait()
        turn_copy(c)[1].wait()
    for j in range(NZ):
        for c in results(j):
            c.wait()
    for c in last:
        c.wait()
    for part in range(2):
        def sent(s, side, part=part):
            for c in zcopies(part, s, side):
                c.wait_send()

        for side in (0, 1):
            pl.when((z < NZ - 1) if side else (z > 0))(functools.partial(sent, z, side))
        for j in (1, 2, 3):
            pl.when(inner)(functools.partial(lambda j: sent(*pass_on(part, j)), j))
            for kind in kinds(part):
                for c in copies(part, j, kind):
                    c.wait_send()


def forward(lengths, x, gains, freqs, qw, kw, vw, ow, cot):
    heads = NZ * HQ_OWN
    kv = NZ * KV_OWN
    vm = pltpu.VMEM
    return pl.pallas_call(
        forward_kernel,
        out_shape=(sds((ROW, D), f32), sds((ROW, D), bf16), sds((heads * HD, ROW), bf16),
                   sds((heads, 128, ROW), bf16), sds((kv, 128, ROW), bf16), sds((kv, ROW, 128), bf16),
                   sds((kv, ROW, 128), bf16), sds((NZ, WR, D), bf16), sds((D, ROW), bf16), sds((D, ROW), bf16),
                   sds((D, ROW), bf16)),
        in_specs=[pl.BlockSpec(memory_space=pltpu.SMEM)] + [VM] * 2 + [ANY] * 6,
        out_specs=(ANY,) * 11,
        scratch_shapes=[
            vm((HD // 2, ROW), f32), vm((HD // 2, ROW), f32),
            vm((ROW, D), bf16), vm((D, QR), bf16), vm((NZ, WR, D), bf16), vm((ROW, D), bf16), vm((heads * HD, ROW), bf16),
            vm((heads, 128, ROW), bf16), vm((kv, 128, ROW), bf16), vm((kv, ROW, 128), bf16),
            vm((kv, 128, ROW), bf16), vm((kv, ROW, 128), bf16),
            vm((128 - HD, ROW), bf16), vm((128 - HD, ROW), bf16), vm((2, CH, D), f32), vm((2, CH, D), bf16),
            vm((2, D, CH), bf16), vm((2, CH, D), bf16), vm((2, D, CH), bf16),
            DMA((3, NZ, 2)), DMA((3, NZ)), DMA((2, 3, 3)), DMA((2, 3, 3)), DMA((2, 3, 3)), DMA((2, 3, 3)),
            DMA((2, 3, 4)), DMA((2, 3, 4)), DMA((NZ + 1, 5)), DMA((5,)), DMA((3, 2)), DMA((2, 2))],
        compiler_params=pltpu.CompilerParams(
            collective_id=1, has_side_effects=True, vmem_limit_bytes=60 * 2**20),
        name="attention_forward",
    )(lengths, gains, freqs, x, qw, kw, vw, ow, cot)


def frequencies():
    return jnp.asarray(np.power(np.float32(rope_base), -(np.arange(HD // 2, dtype=np.float32) * 2) / np.float32(HD))[:, None])


class RowSum:
    def __init__(self, z, own, rend, rmid, out, ssem, esem, msem, osem, ring, lag, begun=0, turn=1):
        self.z, self.own, self.ring, self.lag, self.begun, self.turn = z, own, ring, lag, begun, turn
        self.rend, self.rmid, self.out = rend, rmid, out
        self.ssem, self.esem, self.msem, self.osem = ssem, esem, msem, osem

    def who(self, i):
        odd = lax.rem(i // self.turn, 2)
        return 3 * odd, 1 + odd, 2 - odd, 3 - 3 * odd

    def copy(self, kind, i, to, sem=0):
        s = lax.rem(i, self.ring)
        src, dst, rsem = {
            "end": (self.own(i), self.rend.at[s], self.esem),
            "mid": (self.rmid.at[s], self.rmid.at[s], self.msem),
            "out": (self.out.at[s], self.out.at[s], self.osem)}[kind]
        return put(src, dst, self.ssem.at[sem, s], rsem.at[s], {"mp": to})

    def on(self, place, f):
        pl.when(self.z == place)(f)

    def step1(self, i):
        e, o, m, f = self.who(i)
        self.on(e, lambda: self.copy("end", i, o).start())
        self.on(f, lambda: self.copy("end", i, m).start())

    def step2(self, i):
        e, o, m, f = self.who(i)
        s = lax.rem(i, self.ring)

        def go():
            self.copy("end", i, o).wait_recv()
            self.rmid[s] = (self.own(i)[...].astype(f32) + self.rend[s].astype(f32)).astype(bf16)
            self.copy("mid", i, o).start()

        self.on(m, go)

    def step3(self, i):
        e, o, m, f = self.who(i)
        s = lax.rem(i, self.ring)

        def go():
            @pl.when(i >= self.begun)
            def _():
                self.copy("end", i, e).wait_recv()
                self.copy("mid", i, e).wait_recv()

            self.out[s] = (self.own(i)[...].astype(f32) + self.rend[s].astype(f32)
                           + self.rmid[s].astype(f32)).astype(bf16)
            self.copy("out", i, m, 1).start()
            self.copy("out", i, e).start()

        self.on(o, go)

    def step4(self, i):
        e, o, m, f = self.who(i)

        def go():
            self.copy("out", i, o).wait_recv()
            self.copy("out", i, f, 1).start()

        self.on(m, go)

    def arrive(self, i):
        e, o, m, f = self.who(i)
        self.on(e, lambda: self.copy("out", i, o).wait_recv())
        self.on(f, lambda: self.copy("out", i, m).wait_recv())

    def drain(self, i):
        e, o, m, f = self.who(i)

        @pl.when(i >= self.begun)
        def _():
            self.on(e, lambda: self.copy("end", i, o).wait_send())
            self.on(f, lambda: self.copy("end", i, m).wait_send())
            self.on(m, lambda: self.copy("mid", i, o).wait_send())

        def middle():
            self.copy("out", i, f, 1).wait_send()

        def owner():
            self.copy("out", i, m, 1).wait_send()
            self.copy("out", i, e).wait_send()

        self.on(m, middle)
        self.on(o, owner)

    def half_done(self, i):
        e, o, m, f = self.who(i)
        self.on(e, lambda: self.copy("end", i, o).wait_send())
        self.on(f, lambda: self.copy("end", i, m).wait_send())
        self.on(m, lambda: self.copy("mid", i, o).wait_send())

        def owner():
            self.copy("end", i, e).wait_recv()
            self.copy("mid", i, e).wait_recv()

        self.on(o, owner)

    def tick(self, t, count, finish, begun=0, ahead=0):
        def last(i):
            self.arrive(i)
            finish(i)
            self.drain(i)

        for lag, step in ((4, last), (3, self.step4), (2, self.step3), (1, self.step2), (0, self.step1)):
            i = t - lag * self.lag
            lo, hi = (begun, count + ahead) if lag < 2 else (0, count)
            pl.when((i >= lo) & (i < hi))(functools.partial(step, i))


class GradSum:
    def __init__(self, dp, low, width, cut, g, c1, x1, y1, x2, y2, ssem, rsem, emit, wide=False):
        self.pc, self.px, self.py = (partner(low, dp, bit) for bit in (1, 2, 4))
        self.c, self.x, self.y = lax.rem(low, 2), lax.rem(low // 2, 2), low // 4
        self.g, self.c1, self.x1, self.y1, self.x2, self.y2 = g, c1, x1, y1, x2, y2
        self.ssem, self.rsem, self.emit = ssem, rsem, emit
        self.width, self.cut, self.wide = width, cut, wide

    def cols(self, u, lo, hi):
        if self.wide:
            return (pl.ds(pl.multiple_of(u * self.width + lo, 128), hi - lo),)
        return (pl.ds(lo, hi - lo),)

    def part(self, u, *at, lo=None, hi=None):
        lo, hi = (0, self.width) if lo is None else (lo, hi)
        return (() if self.wide else (u,)) + at + self.cols(u, lo, hi)

    def put_block(self, u, k, res):
        self.put_part(u, k, 0, self.width, res)

    def put_part(self, u, k, lo, hi, res):
        self.g[self.part(u, k // 4, (k // 2) % 2, k % 2, slice(None), lo=lo, hi=hi)] = res.astype(bf16)

    def copies(self, u, k):
        g, c, x, y = self.g, self.c, self.x, self.y
        every = slice(None)
        a = dict(lo=0, hi=self.cut)
        b = dict(lo=self.cut, hi=self.width)

        def mk(i, src, dst, dev):
            return put(src, dst, self.ssem.at[u, i], self.rsem.at[u, i], {"dp": dev})

        if k == 0:
            return [mk(0, g.at[self.part(u, every, every, 1 - c, every)], self.c1.at[u], self.pc)]
        if k == 1:
            return [mk(1, g.at[self.part(u, every, 1 - x, c, every, **a)], self.x1.at[u], self.px),
                    mk(2, g.at[self.part(u, 1 - y, every, c, every, **b)], self.y1.at[u], self.py)]
        return [mk(3, g.at[self.part(u, 1 - y, x, c, every, **a)], self.y2.at[u], self.py),
                mk(4, g.at[self.part(u, y, 1 - x, c, every, **b)], self.x2.at[u], self.px)]

    def start(self, u):
        for c in self.copies(u, 0):
            c.start()

    def stage(self, k, u):
        width, cut = self.width, self.cut
        g, c, x, y = self.g, self.c, self.x, self.y
        for cp in self.copies(u, k - 1):
            cp.wait_recv()

        def at(i, j, lo, hi):
            return self.part(u, i, j, c, slice(None), lo=lo, hi=hi)

        def add(i, j, lo, hi, other):
            g[at(i, j, lo, hi)] = (g[at(i, j, lo, hi)].astype(f32) + other.astype(f32)).astype(bf16)

        if k == 1:
            for i in range(2):
                for j in range(2):
                    add(i, j, 0, width, self.c1[u, i, j])
        elif k == 2:
            for i in range(2):
                add(i, x, 0, cut, self.x1[u, i])
                add(y, i, cut, width, self.y1[u, i])
        else:
            self.emit(u, 0, cut, g[at(y, x, 0, cut)].astype(f32) + self.y2[u].astype(f32))
            self.emit(u, cut, width, g[at(y, x, cut, width)].astype(f32) + self.x2[u].astype(f32))
        if k < 3:
            for cp in self.copies(u, k):
                cp.start()

    def drain(self, u):
        for k in range(3):
            for cp in self.copies(u, k):
                cp.wait_send()


def sum_scratch(count, width, cut):
    vm = pltpu.VMEM
    rest = width - cut
    return [vm((count, 2, 2, 2, 192, width), bf16), vm((count, 2, 2, 192, width), bf16),
            vm((count, 2, 192, cut), bf16), vm((count, 2, 192, rest), bf16),
            vm((count, 192, rest), bf16), vm((count, 192, cut), bf16), DMA((count, 5)), DMA((count, 5))]


def ring_scratch(ring, rows):
    vm = pltpu.VMEM
    return [vm((ring, rows, D), bf16), vm((ring, rows, D), bf16), vm((ring, rows, D), bf16),
            DMA((2, ring)), DMA((ring,)), DMA((ring,)), DMA((ring,))]


MLP_UNITS = 6
MLP_WIDTH = 512


def feed_kernel(gains, hid2, cot, mid, hid2t_i, cott_i, gw_i, uw_i, dw_i,
                mlp_o, gm_o, gml_o, gmlt_o, gain2_o, gate_o, up_o, down_o, end_o, mid_o,
                gw, uw, dw, a3, side, own, hb, cb, tb, mb, cb2, gmb, gmlb, gmltb,
                rend, rmid, out, zs, ze, zm, zo,
                g, c1, x1, y1, x2, y2, gs, gr,
                lsem, bsem, tsem, msem, wsem, asem):
    dp, z, low = places()
    loads = [pltpu.make_async_copy(a, b, lsem.at[i]) for i, (a, b) in enumerate(
        ((gw_i, gw), (uw_i, uw), (dw_i, dw), (hid2t_i, side), (cott_i, side)))]
    nc = ROW // CH
    nb = ROW // BL
    nj = ROW // 128
    pair = 128 // BL
    per = BL3 // BL

    def chunk_loads(c):
        return [pltpu.make_async_copy(src.at[chunk(c)], dst.at[lax.rem(c, 2)], bsem.at[i, lax.rem(c, 2)])
                for i, (src, dst) in enumerate(((hid2, hb), (cot, cb)))]

    for c in chunk_loads(0):
        c.start()
    for c in loads[:4]:
        c.start()
    greet(dp, z, low)
    def emit(u, lo, hi, v):
        half = lax.rem(u, 2) * MLP_WIDTH
        at = pl.ds(pl.multiple_of(half + lo, 128), hi - lo)
        for i, ref in enumerate((gate_o, up_o, down_o)):
            @pl.when(u // 2 == i)
            def _(ref=ref):
                ref[:, at] = v

    zsum = RowSum(z, lambda i: own.at[chunk(lax.rem(i, nb), BL)], rend, rmid, out, zs, ze, zm, zo, RING, LAG, turn=BL3 // BL)
    gsum = GradSum(dp, low, MLP_WIDTH, MLP_WIDTH // 2, g, c1, x1, y1, x2, y2, gs, gr, emit)
    gain2_o[...] = jnp.zeros_like(gain2_o)

    def gm_loads(j):
        r = chunk(j, 128)
        return [pltpu.make_async_copy(mid.at[r], mb, msem.at[0]),
                pltpu.make_async_copy(cot.at[r], cb2, msem.at[1])]

    def gm_writes(j):
        r = chunk(j, 128)
        s = lax.rem(j, 2)
        return [pltpu.make_async_copy(gmb.at[s], gm_o.at[r], wsem.at[0, s]),
                pltpu.make_async_copy(gmlb.at[s], gml_o.at[r], wsem.at[1, s]),
                pltpu.make_async_copy(gmltb.at[s], gmlt_o.at[:, r], wsem.at[2, s])]

    def finish_pair(j):
        s = lax.rem(j, 2)
        for c in gm_loads(j):
            c.wait()

        @pl.when(j >= 2)
        def _():
            for c in gm_writes(j - 2):
                c.wait()

        gh = jnp.concatenate([out[lax.rem(j * pair + k, RING)] for k in range(pair)], axis=0).astype(f32)
        m = mb[...]
        f = lax.rsqrt(jnp.mean(m * m, axis=1, keepdims=True) + eps)
        n = m * f
        gn = gh * n
        gain2_o[...] += jnp.sum(gn, axis=0, keepdims=True)
        ga = gains[1:2, :].astype(f32)
        gm = cb2[...].astype(f32) + f * (gh * ga - n * jnp.mean(gn * ga, axis=1, keepdims=True))
        gmb[s] = gm
        low_gm = gm.astype(bf16)
        gmlb[s] = low_gm
        gmltb[s] = low_gm.T
        for c in gm_writes(j):
            c.start()

        @pl.when(j + 1 < nj)
        def _():
            for c in gm_loads(j + 1):
                c.start()

    def finish(i):
        pl.when(lax.rem(i, pair) == pair - 1)(lambda: finish_pair(i // pair))

    for c in gm_loads(0):
        c.start()

    def tick(t):
        for k in range(per):
            zsum.tick(per * t + k, nb, finish, ahead=AHEAD * per)

    again = pltpu.make_async_copy(mlp_o.at[pl.ds(0, AHEAD * BL3)], own.at[pl.ds(0, AHEAD * BL3)], asem)

    def mlp_write(c):
        return pltpu.make_async_copy(tb.at[lax.rem(c, 2)], mlp_o.at[chunk(c)], tsem.at[lax.rem(c, 2)])

    def mlp_chunk(c, _):
        r = chunk(c)
        s = lax.rem(c, 2)
        for cp in chunk_loads(c):
            cp.wait()

        @pl.when(c + 1 < nc)
        def _():
            for cp in chunk_loads(c + 1):
                cp.start()

        @pl.when(c == 0)
        def _():
            loads[0].wait()
            loads[1].wait()
            loads[2].wait()

        gate = nn(hb[s], gw[...])
        upper = nn(hb[s], uw[...])
        ga = nt(cb[s], dw[...])
        sigma = 1.0 / (1.0 + jnp.exp(-gate))
        silu = gate * sigma
        gg = (ga * upper * sigma * (1.0 + gate * (1.0 - sigma))).astype(bf16)
        gu = (ga * silu).astype(bf16)
        act = (silu * upper).astype(bf16)
        a3[0, r] = gg
        a3[1, r] = gu
        a3[2, r] = act
        own[r] = (nt(gg, gw[...]) + nt(gu, uw[...])).astype(bf16)
        tick(2 * c)

        @pl.when(c >= 2)
        def _():
            mlp_write(c - 2).wait()

        tb[s] = nn(act, dw[...]).astype(bf16)
        mlp_write(c).start()
        tick(2 * c + 1)
        return 0

    def unit(u):
        @pl.when(u == 0)
        def _():
            loads[3].wait()

        @pl.when(u == 4)
        def _():
            loads[4].start()
            loads[4].wait()

        which = u // 2
        cols = chunk(lax.rem(u, 2), MLP_WIDTH)
        rhs = a3[which, :, cols]
        for k in range(8):
            gsum.put_block(u, k, nn(side[k * 192:(k + 1) * 192], rhs))
        gsum.start(u)

    def beat(t, _):
        first = 2 * nc
        u = t - first

        @pl.when(t == first)
        def _():
            for c in range(max(nc - 2, 0), nc):
                mlp_write(c).wait()

        @pl.when(t == nb // per)
        def _():
            again.start()
            again.wait()

        pl.when(u < MLP_UNITS)(lambda: unit(u))
        tick(t)
        for k, lag in ((3, 8), (2, 4), (1, 1)):
            v = u - lag
            pl.when((v >= 0) & (v < MLP_UNITS))(functools.partial(gsum.stage, k, v))
        return 0

    lax.fori_loop(0, nc, mlp_chunk, 0)
    lax.fori_loop(2 * nc, (nb + 4 * LAG + per - 1) // per, beat, 0)

    def drains(u, _):
        gsum.drain(u)
        return 0

    lax.fori_loop(0, MLP_UNITS, drains, 0)
    for j in range(nj - 2, nj):
        for c in gm_writes(j):
            c.wait()
    keep = []
    for i in range(AHEAD * per):
        zsum.half_done(nb + i)
        s = (nb + i) % RING
        keep += [pltpu.make_async_copy(rend.at[s], end_o.at[i], zs.at[0, s]),
                 pltpu.make_async_copy(rmid.at[s], mid_o.at[i], zs.at[1, s])]
    for c in keep:
        c.start()
    for c in keep:
        c.wait()


def feed(gains, hid2, cot, mid, hid2t, cott, gw, uw, dw):
    vm = pltpu.VMEM
    ff = gw.shape[1]
    return pl.pallas_call(
        feed_kernel,
        out_shape=(sds((ROW, D), bf16), sds((ROW, D), f32), sds((ROW, D), bf16), sds((D, ROW), bf16),
                   sds((1, D), f32), sds((D // 8, ff), f32), sds((D // 8, ff), f32), sds((D // 8, ff), f32),
                   sds((AHEAD * BL3 // BL, BL, D), bf16), sds((AHEAD * BL3 // BL, BL, D), bf16)),
        in_specs=[VM] + [ANY] * 8,
        out_specs=(ANY, ANY, ANY, ANY, VM, VM, VM, VM, ANY, ANY),
        scratch_shapes=[
            vm((D, ff), bf16), vm((D, ff), bf16), vm((ff, D), bf16), vm((3, ROW, ff), bf16),
            vm((D, ROW), bf16), vm((ROW, D), bf16),
            vm((2, CH, D), bf16), vm((2, CH, D), bf16), vm((2, CH, D), bf16),
            vm((128, D), f32), vm((128, D), bf16), vm((2, 128, D), f32), vm((2, 128, D), bf16),
            vm((2, D, 128), bf16)]
        + ring_scratch(RING, BL) + sum_scratch(MLP_UNITS, MLP_WIDTH, MLP_WIDTH // 2)
        + [DMA((5,)), DMA((2, 2)), DMA((2,)), DMA((2,)), DMA((3, 2)), DMA],
        compiler_params=pltpu.CompilerParams(
            collective_id=2, has_side_effects=True, vmem_limit_bytes=63 * 2**20),
        name="feed_forward",
    )(gains, hid2, cot, mid, hid2t, cott, gw, uw, dw)


RING3 = 10
LAG3 = 2
WIDTH = QR
BEATS = 10
CUT = 128


def unrotate(u, co, si):
    a = u[0:HD // 2]
    b = u[HD // 2:HD]
    return jnp.concatenate([a * co + b * si, b * co - a * si], axis=0).astype(bf16)


def attend_back(qk, kk, vv, dot, ho, dk, dv, gt, cos, sin, g, gg, qb):
    lo = qb * CH
    hi = lo + CH
    heads = NZ * HQ_OWN * 128
    q = jnp.concatenate([qk[pl.ds(pl.multiple_of((2 * g + h) * 128, 128), 128), lo:hi] for h in range(2)], axis=1)
    parts = []
    for h in range(2):
        do = dot[pl.ds(pl.multiple_of((2 * gg + h) * HD, 32), HD), lo:hi]
        o = ho[pl.ds(pl.multiple_of((2 * g + h) * HD, 32), HD), lo:hi]
        delta = jnp.sum(do.astype(f32) * o.astype(f32), axis=0, keepdims=True)
        extra = extra_rows(jnp.zeros((128 - HD, CH), f32), -delta, 0)
        parts.append(jnp.concatenate([do, extra], axis=0))
    do = jnp.concatenate(parts, axis=1)
    do_t = do.T
    q_t = q.T
    dq = jnp.zeros((128, 2 * CH), f32)
    for kb in range(qb + 1):
        ks = slice(kb * CH, (kb + 1) * CH)
        p = jnp.exp2(nn(kk[g, ks, :], q) * C2)
        if kb == qb:
            ki = lax.broadcasted_iota(jnp.int32, (CH, CH), 0)
            qi = lax.broadcasted_iota(jnp.int32, (CH, CH), 1)
            keep = jnp.concatenate([ki <= qi, ki <= qi], axis=1)
            p = jnp.where(keep, p, 0.0)
        ds = (p * nn(vv[g, ks, :], do)).astype(bf16)
        dvb = nn(p.astype(bf16), do_t)
        dkb = nn(ds, q_t)
        if kb == qb:
            dv[ks, :] = dvb
            dk[ks, :] = dkb
        else:
            dv[ks, :] += dvb
            dk[ks, :] += dkb
        dq = dq + nn(qk[pl.ds(pl.multiple_of(heads + g * 128, 128), 128), ks], ds)
    first = (g // KV_OWN) * QKV + gg * 2 * HD
    for h in range(2):
        at = pl.ds(pl.multiple_of(first + h * HD, 32), HD)
        gt[at, lo:hi] = unrotate(dq[0:HD, h * CH:(h + 1) * CH] * SCALE, cos[:, lo:hi], sin[:, lo:hi])


def backward_kernel(groups, lengths, gains, freqs, gain2_i, x, mid, mlp, gm, gml_i, gmlt, hid1t, ho_i, qt_i, kt_i, kk_i, vv_i, w_i, end_i, mid_i,
                    out_o, xg_o, qg_o, kg_o, vg_o, og_o, gains_o,
                    cos, sin, w, wo, ho, qk, kk, vv, dk, dv, gt, gml, dot, ga1, own, mb2, ob2, xb, gb, ob,
                    rend, rmid, out, zs, ze, zm, zo,
                    c1, x1, y1, x2, y2, gs, gr, og, oc1, ox1, oy1, ox2, oy2, ogs, ogr, tb, gsend, grecv,
                    lsem, bsem, wsem, psem, osem, isem, tsem, ssem, rsem, asem):
    dp, z, low = places()
    qrows = NZ * HQ_OWN * 128
    loads = [pltpu.make_async_copy(ho_i, ho, lsem.at[1]),
             pltpu.make_async_copy(gml_i, gml, lsem.at[0]),
             pltpu.make_async_copy(kk_i, kk, lsem.at[2]),
             pltpu.make_async_copy(vv_i, vv, lsem.at[3])]
    loads += [pltpu.make_async_copy(w_i.at[s, pl.ds(QKV + 192 * h, 192)], wo.at[s // 2, s % 2, h], lsem.at[4 + 2 * s + h])
              for s in range(NZ) for h in range(2)]
    loads += [pltpu.make_async_copy(qt_i, qk.at[pl.ds(0, qrows)], lsem.at[12]),
              pltpu.make_async_copy(kt_i, qk.at[pl.ds(qrows, NZ * KV_OWN * 128)], lsem.at[13])]
    wloads = [pltpu.make_async_copy(w_i.at[s, pl.ds(0, QKV)], w.at[s], lsem.at[14 + s]) for s in range(NZ)]
    late = [pltpu.make_async_copy(hid1t, qk.at[pl.ds(0, D)], lsem.at[18])]
    nb = ROW // BL3
    nt_blocks = ROW // TB

    def own_load(i):
        s = lax.rem(i, RING3)
        return pltpu.make_async_copy(mlp.at[chunk(i, BL3)], own.at[s], isem.at[s])

    def mid_load(i):
        s = lax.rem(i, 2)
        return pltpu.make_async_copy(mid.at[chunk(i, BL3)], mb2.at[s], osem.at[0, s])

    def out_write(i):
        s = lax.rem(i, 2)
        return pltpu.make_async_copy(ob2.at[s], out_o.at[chunk(i, BL3)], osem.at[1, s])

    def turned_load(k):
        return pltpu.make_async_copy(gmlt.at[pl.ds(k * 192, 192)], tb.at[k % 2], tsem.at[k % 2])

    begun = [pltpu.make_async_copy(src, dst.at[pl.ds(0, AHEAD)], asem.at[i])
             for i, (src, dst) in enumerate(((end_i, rend), (mid_i, rmid)))]
    for c in begun:
        c.start()
    for i in range(2 * LAG3 + 2):
        own_load(i).start()
    mid_load(0).start()
    turned_load(0).start()
    turned_load(1).start()
    for c in loads:
        c.start()
    greet(dp, z, low, range(1, 8))
    angle_tables(lengths, freqs, cos, sin)
    zsum = RowSum(z, lambda i: own.at[lax.rem(i, RING3)], rend, rmid, out, zs, ze, zm, zo, RING3, LAG3, AHEAD)

    def emit(u, lo, hi, v):
        if u == 0:
            qg_o[:, lo:hi] = v
            return
        for ref, first in ((kg_o, 0), (vg_o, KR)):
            a, b = max(lo, first), min(hi, first + KR)
            if a < b:
                ref[:, a - first:b - first] = v[:, a - lo:b - lo]

    def emit_o(u, lo, hi, v):
        og_o[:, lo:hi] = v

    gsum = GradSum(dp, low, WIDTH, CUT, wo, c1, x1, y1, x2, y2, gs, gr, emit, True)
    osum = GradSum(dp, low, WIDTH, CUT, og, oc1, ox1, oy1, ox2, oy2, ogs, ogr, emit_o)

    def finish(i):
        mid_load(i).wait()
        s = lax.rem(i, 2)

        @pl.when(i >= 2)
        def _():
            out_write(i - 2).wait()

        ob2[s] = (mb2[s] + out[lax.rem(i, RING3)].astype(f32)).astype(bf16)
        out_write(i).start()

        @pl.when(i + 1 < nb)
        def _():
            mid_load(i + 1).start()

    def tick(beat):
        t = beat + 2 * LAG3
        pl.when((t >= AHEAD) & (t < nb))(lambda: own_load(t).wait())
        zsum.tick(t, nb, finish, begun=AHEAD)
        pl.when(t + 2 < nb)(lambda: own_load(t + 2).start())

    for i in range(AHEAD):
        own_load(i).wait()
    for c in begun:
        c.wait()
    tick(0)
    tick(1)
    loads[0].wait()
    o_rows = ho[pl.ds(pl.multiple_of(z * QR, 128), QR), :]
    for k in range(8):
        turned_load(k).wait()
        osum.put_block(0, k, nt(tb[k % 2], o_rows))
        if k + 2 < 8:
            turned_load(k + 2).start()
    osum.start(0)
    tick(2)
    for c in loads[1:]:
        c.wait()
    for c in wloads:
        c.start()

    def quarter(s, _):
        for h in range(2):
            t = nt(wo[s // 2, lax.rem(s, 2), h], gml[...])
            dot[h * 192:(h + 1) * 192, :] = t.astype(bf16)

        def one(gg, _):
            g = KV_OWN * s + gg
            for qb in range(ROW // CH):
                attend_back(qk, kk, vv, dot, ho, dk, dv, gt, cos, sin, g, gg, qb)
                done = 10 * g + qb * (qb + 1) // 2
                was, now = (done * BEATS) // 80, ((done + qb + 1) * BEATS) // 80
                pl.when(now > was)(functools.partial(tick, 3 + was))
            first = pl.multiple_of(s * QKV + QR + gg * HD, 32)
            gt[pl.ds(first, HD), :] = unrotate(dk[...].T[0:HD] * SCALE, cos[...], sin[...])
            gt[pl.ds(pl.multiple_of(first + KR, 32), HD), :] = dv[...].T[0:HD].astype(bf16)
            return 0

        lax.fori_loop(0, KV_OWN, one, 0)
        for k in (1, 2, 3):
            pl.when(s == k - 1)(functools.partial(osum.stage, k, 0))
        return 0

    lax.fori_loop(0, NZ, quarter, 0)
    beats = 3 + BEATS
    for c in late:
        c.start()
    for c in wloads + late:
        c.wait()

    for u in range(2):
        rhs = gt[pl.ds(pl.multiple_of(z * QKV + u * WIDTH, 128), WIDTH), :]
        for k in range(8):
            gsum.put_block(u, k, nt(qk[k * 192:(k + 1) * 192, :], rhs))
        gsum.start(u)
        tick(beats + u)
    beats += 2

    def tail_loads(b, slot):
        r = chunk(b, TB)
        return [pltpu.make_async_copy(x.at[r], xb.at[slot], bsem.at[0, slot]),
                pltpu.make_async_copy(gm.at[r], gb.at[slot], bsem.at[1, slot])]

    def out_copy(b, slot):
        return pltpu.make_async_copy(ob.at[slot], xg_o.at[chunk(b, TB)], psem.at[slot])

    for c in tail_loads(0, 0):
        c.start()
    ga1[...] = jnp.zeros_like(ga1)

    def tail(b, _):
        slot = lax.rem(b, 2)

        @pl.when(b + 1 < nt_blocks)
        def _():
            for c in tail_loads(b + 1, 1 - slot):
                c.start()

        r = chunk(b, TB)
        acc = jnp.zeros((TB, D), f32)
        for s in range(NZ):
            acc = acc + tn(gt[QKV * s:QKV * s + QKV, r], w[s])
        for c in tail_loads(b, slot):
            c.wait()

        @pl.when(b >= 2)
        def _():
            out_copy(b - 2, slot).wait()

        xx = xb[slot].astype(f32)
        f = lax.rsqrt(jnp.mean(xx * xx, axis=1, keepdims=True) + eps)
        n = xx * f
        gn = acc * n
        ga1[...] += jnp.sum(gn, axis=0, keepdims=True)
        ga = gains[0:1, :].astype(f32)
        res = gb[slot] + f * (acc * ga - n * jnp.mean(gn * ga, axis=1, keepdims=True))
        ob[slot] = res.astype(bf16)
        out_copy(b, slot).start()
        pl.when(lax.rem(b, 2) == 1)(lambda: tick(beats + b // 2))
        pl.when(b == 0)(lambda: (gsum.stage(1, 0), gsum.stage(1, 1)) and None)
        pl.when(b == 2)(lambda: gsum.stage(2, 0))
        pl.when(b == 4)(lambda: gsum.stage(2, 1))
        pl.when(b == 6)(lambda: gsum.stage(3, 0))
        return 0

    lax.fori_loop(0, nt_blocks, tail, 0)
    beats += nt_blocks // 2

    def gains_copy(mask):
        to = flip(low, mask)
        return put(gsend.at[to], grecv.at[low], ssem.at[mask], rsem.at[mask], {"dp": dp - low + to})

    share = D // 8 // groups
    for k in range(8):
        for i, v in enumerate((ga1, gain2_i)):
            gsend[k, i:i + 1, 0:D // 8] = jnp.concatenate(
                [v[:, (g * 8 + k) * share:(g * 8 + k + 1) * share] for g in range(groups)], axis=1)
    for mask in range(1, 8):
        gains_copy(mask).start()

    def rest(t, _):
        tick(t)
        return 0

    ends = nb + 2 * LAG3
    if beats < ends:
        lax.fori_loop(beats, ends, rest, 0)
    gsum.stage(3, 1)
    total = gsend[low]
    for mask in range(1, 8):
        gains_copy(mask).wait_recv()
        total = total + grecv[flip(low, mask)]
    gains_o[...] = total
    for mask in range(1, 8):
        gains_copy(mask).wait_send()
    for u in range(2):
        gsum.drain(u)
    osum.drain(0)
    for b in range(nt_blocks - 2, nt_blocks):
        out_copy(b, b % 2).wait()
    for i in (nb - 2, nb - 1):
        out_write(i).wait()


def backward(groups, lengths, gains, freqs, gain2_sum, x, mid, mlp, gm, gml, gmlt, hid1t, ho, qt, kt, kk, vv, w, ends, mids):
    vm = pltpu.VMEM
    heads = NZ * HQ_OWN
    kv = NZ * KV_OWN
    return pl.pallas_call(
        functools.partial(backward_kernel, groups),
        out_shape=(sds((ROW, D), bf16), sds((ROW, D), bf16), sds((D // 8, QR), f32), sds((D // 8, KR), f32),
                   sds((D // 8, KR), f32), sds((D // 8, QR), f32), sds((8, 256), f32)),
        in_specs=[pl.BlockSpec(memory_space=pltpu.SMEM)] + [VM] * 3 + [ANY] * 15,
        out_specs=(ANY, ANY) + (VM,) * 5,
        scratch_shapes=[
            vm((HD // 2, ROW), f32), vm((HD // 2, ROW), f32), vm((NZ, QKV, D), bf16), vm((2, 2, 2, 192, D), bf16), vm((heads * HD, ROW), bf16),
            vm(((heads + kv) * 128, ROW), bf16), vm((kv, ROW, 128), bf16), vm((kv, ROW, 128), bf16),
            vm((ROW, 128), f32), vm((ROW, 128), f32), vm((NZ * QKV, ROW), bf16),
            vm((ROW, D), bf16), vm((QR, ROW), bf16), vm((1, D), f32),
            vm((RING3, BL3, D), bf16), vm((2, BL3, D), f32), vm((2, BL3, D), bf16),
            vm((2, TB, D), bf16), vm((2, TB, D), f32), vm((2, TB, D), bf16)]
        + ring_scratch(RING3, BL3) + sum_scratch(2, WIDTH, CUT)[1:] + sum_scratch(1, WIDTH, CUT)
        + [vm((2, 192, ROW), bf16), vm((8, 8, 256), f32), vm((8, 8, 256), f32),
           DMA((19,)), DMA((2, 2)), DMA((2,)), DMA((2,)), DMA((2, 2)), DMA((RING3,)), DMA((2,)), DMA((8,)), DMA((8,)), DMA((2,))],
        compiler_params=pltpu.CompilerParams(
            collective_id=3, has_side_effects=True, vmem_limit_bytes=63 * 2**20),
        name="attention_backward",
    )(lengths, gains, freqs, gain2_sum, x, mid, mlp, gm, gml, gmlt, hid1t, ho, qt, kt, kk, vv, w,
      ends, mids)


def by_block(v, groups):
    if groups == 1:
        return v
    rows, cols = v.shape
    return v.reshape(groups, 8, rows // (8 * groups), cols).transpose(1, 0, 2, 3).reshape(rows, cols)


def body(groups, inputs, lengths, q_weight, k_weight, v_weight, o_weight, gate_weight, up_weight, down_weight,
         attn_gain, mlp_gain, cotangent):
    x = inputs.reshape(ROW, D)
    cot = cotangent.reshape(ROW, D)
    first = lax.broadcasted_iota(jnp.int32, (2, D), 0) == 0
    gains = jnp.where(first, attn_gain[None, :], mlp_gain[None, :])
    freqs = frequencies()
    mid, hid2, ho, qt, kt, kk, vv, w, hid1t, hid2t, cott = forward(
        lengths, x, gains, freqs, q_weight, k_weight.T, v_weight.T, o_weight, cot)
    mlp, gm, gml, gmlt, gain2_sum, gate_g, up_g, down_g, ends, mids = feed(
        gains, hid2, cot, mid, by_block(hid2t, groups), by_block(cott, groups), gate_weight, up_weight, down_weight)
    output, input_grad, q_g, k_g, v_g, o_g, gain_sums = backward(
        groups, lengths, gains, freqs, gain2_sum, x, mid, mlp, gm, gml, by_block(gmlt, groups), by_block(hid1t, groups),
        ho, qt.reshape(-1, ROW), kt.reshape(-1, ROW), kk, vv, w, ends.reshape(-1, BL3, D), mids.reshape(-1, BL3, D))
    grads = [q_g, k_g, v_g, o_g, gate_g, up_g, down_g, gain_sums]
    if groups > 1:
        same = [[g * 8 + low for g in range(groups)] for low in range(8)]
        grads = [lax.psum_scatter(v, "dp", scatter_dimension=int(i == 7), axis_index_groups=same, tiled=True)
                 for i, v in enumerate(grads[:7] + [gain_sums[:, 0:D // 8]])]
    output, input_grad, *grads = hand_over(output, input_grad, *grads)
    grads[3], grads[6] = grads[3].T, grads[6].T
    grads[7:] = grads[7][0, 0:D // 8 // groups], grads[7][1, 0:D // 8 // groups]
    return (output.reshape(1, ROW, D), input_grad.reshape(1, ROW, D), *grads)


def hand_over_kernel(n, *refs):
    held, load, store = refs[2 * n:3 * n], refs[3 * n], refs[3 * n + 1]
    pieces = []
    for i in range(n):
        rows = held[i].shape[0]
        parts = 4 if rows % 64 == 0 and rows > 512 else 1
        pieces += [(i, pl.ds(p * (rows // parts), rows // parts)) for p in range(parts)]
    first = [pltpu.make_async_copy(refs[i].at[r], held[i].at[r], load.at[k]) for k, (i, r) in enumerate(pieces)]
    then = [pltpu.make_async_copy(held[i].at[r], refs[n + i].at[r], store.at[k]) for k, (i, r) in enumerate(pieces)]
    for c in first:
        c.start()
    for a, b in zip(first, then):
        a.wait()
        b.start()
    for c in then:
        c.wait()


def hand_over(*arrays):
    n = len(arrays)
    return pl.pallas_call(
        functools.partial(hand_over_kernel, n),
        out_shape=tuple(sds(v.shape, v.dtype) for v in arrays),
        in_specs=[ANY] * n,
        out_specs=(ANY,) * n,
        scratch_shapes=[pltpu.VMEM(v.shape, v.dtype) for v in arrays] + [DMA((4 * n,)), DMA((4 * n,))],
        compiler_params=pltpu.CompilerParams(vmem_limit_bytes=63 * 2**20),
        name="hand_over",
    )(*arrays)


def solution(mesh):
    row = P("dp", None, None)
    in_specs = (row, P("dp", None), P(None, "mp"), P(None, "mp"), P(None, "mp"), P("mp", None),
                P(None, "mp"), P(None, "mp"), P("mp", None), P(), P(), row)
    out_specs = (row, row, P("dp", "mp"), P("dp", "mp"), P("dp", "mp"), P("mp", "dp"),
                 P("dp", "mp"), P("dp", "mp"), P("mp", "dp"), P("dp"), P("dp"))
    return jax.shard_map(functools.partial(body, mesh.shape["dp"] // 8), mesh=mesh, in_specs=in_specs,
                         out_specs=out_specs, check_vma=False)
```

```python
import functools

import jax
import jax.numpy as jnp
import numpy as np
from jax import lax
from jax.experimental import pallas as pl
from jax.experimental.pallas import tpu as pltpu
from jax.sharding import PartitionSpec as P

D = 1536
HD = 96
ROW = 1024
SEGS = 4
NZ = 4
CH = 256
TB = 256
BL = 64
LAG = 2
RING = 10
BL3 = 64
AHEAD = 4
HQ_OWN = 4
KV_OWN = 2
QR = HQ_OWN * HD
KR = KV_OWN * HD
QKV = QR + 2 * KR
WR = QKV + QR
SCALE = HD ** -0.5
C2 = SCALE * 1.4426950408889634
NEG = -1e30
eps = 1e-05
rope_base = 100000.0
f32 = jnp.float32
bf16 = jnp.bfloat16
MESH = pl.DeviceIdType.MESH
ANY = pl.BlockSpec(memory_space=pl.ANY)
VM = pl.BlockSpec(memory_space=pltpu.VMEM)
DMA = pltpu.SemaphoreType.DMA
sds = jax.ShapeDtypeStruct


def nt(a, b):
    return lax.dot_general(a, b, (((1,), (1,)), ((), ())), preferred_element_type=f32)


def nn(a, b):
    return lax.dot_general(a, b, (((1,), (0,)), ((), ())), preferred_element_type=f32)


def tn(a, b):
    return lax.dot_general(a, b, (((0,), (0,)), ((), ())), preferred_element_type=f32)


def chunk(c, size=CH):
    return pl.ds(pl.multiple_of(c * size, size), size)


def places():
    dp = lax.axis_index("dp")
    z = lax.axis_index("mp")
    low = lax.rem(dp, 8)
    return dp, z, low


def partner(low, dp, bit):
    on = lax.rem(low // bit, 2)
    return dp + bit - 2 * bit * on


def flip(low, mask):
    for bit in (1, 2, 4):
        if mask & bit:
            low = low + bit - 2 * bit * lax.rem(low // bit, 2)
    return low


def greet(dp, z, low, masks=(1, 2, 4)):
    barrier = pltpu.get_barrier_semaphore()
    for mask in masks:
        pl.semaphore_signal(barrier, inc=1, device_id={"dp": dp - low + flip(low, mask)}, device_id_type=MESH)
    for other in (1, 2, 3):
        pl.semaphore_signal(barrier, inc=1, device_id={"mp": lax.rem(z + other, NZ)}, device_id_type=MESH)
    pl.semaphore_wait(barrier, len(masks) + 3)


def put(src, dst, ssem, rsem, dev):
    return pltpu.make_async_remote_copy(
        src_ref=src, dst_ref=dst, send_sem=ssem, recv_sem=rsem, device_id=dev, device_id_type=MESH)


def split3(v):
    hi = v.astype(bf16).astype(f32)
    rest = v - hi
    mid = rest.astype(bf16).astype(f32)
    return hi, mid, rest - mid


def extra_rows(base, v, first):
    row = lax.broadcasted_iota(jnp.int32, base.shape, 0)
    out = base
    for i, part in enumerate(split3(v)):
        out = jnp.where(row == first + i, part, out)
    return out.astype(bf16)


def project(w, hid, qt, kt, kk, vt, vv, cos, sin, qaug, kaug, s, c):
    cols = chunk(c)
    t = nt(w[s, 0:QKV], hid[cols])
    co = cos[:, cols]
    si = sin[:, cols]

    def rot(u):
        a = u[0:HD // 2]
        b = u[HD // 2:HD]
        return jnp.concatenate([a * co - b * si, b * co + a * si], axis=0).astype(bf16)

    for h in range(HQ_OWN):
        qt[HQ_OWN * s + h, 0:HD, cols] = rot(t[HD * h:HD * h + HD])
        qt[HQ_OWN * s + h, HD:128, cols] = qaug[:, cols]
    for h in range(KV_OWN):
        g = KV_OWN * s + h
        k = jnp.concatenate([rot(t[QR + HD * h:QR + HD * h + HD]), kaug[:, cols]], axis=0)
        kt[g, :, cols] = k
        kk[g, cols, :] = k.T
        v = t[QR + KR + HD * h:QR + KR + HD * h + HD].astype(bf16)
        v = jnp.concatenate([v, jnp.ones((128 - HD, CH), bf16)], axis=0)
        vt[g, :, cols] = v
        vv[g, cols, :] = v.T


def attend(qt, kk, vt, ho, qaug, g, between):
    ki = lax.broadcasted_iota(jnp.int32, (CH, CH), 0)
    qi = lax.broadcasted_iota(jnp.int32, (CH, CH), 1)
    keep = jnp.concatenate([ki <= qi, ki <= qi], axis=1)

    def scores(qb):
        lo = qb * CH
        nk = lo + CH
        q = jnp.concatenate([qt[2 * g, :, lo:nk], qt[2 * g + 1, :, lo:nk]], axis=1)
        return [nn(kk[g, kb * CH:(kb + 1) * CH, :], q) for kb in range(qb + 1)]

    def rest(qb, st):
        lo = qb * CH
        nk = lo + CH
        st[qb] = jnp.where(keep, st[qb], NEG)
        m = jnp.max(st[qb], axis=0, keepdims=True)
        for kb in range(qb):
            m = jnp.maximum(m, jnp.max(st[kb], axis=0, keepdims=True))
        mc = m * C2
        o = jnp.zeros((128, 2 * CH), f32)
        for kb in range(qb + 1):
            o = o + nn(vt[g, :, kb * CH:(kb + 1) * CH], jnp.exp2(st[kb] * C2 - mc).astype(bf16))
        total = o[HD:HD + 1]
        r = (o[0:HD] / total).astype(bf16)
        back = (mc + jnp.log2(total)) * (-1.0 / C2)
        for h in range(2):
            part = slice(h * CH, (h + 1) * CH)
            ho[pl.ds(pl.multiple_of(g * 2 * HD + h * HD, 32), HD), lo:nk] = r[:, part]
            base = qaug[:, lo:nk].astype(f32)
            qt[2 * g + h, HD:128, lo:nk] = extra_rows(base, back[:, part], SEGS)

    st = scores(0)
    for qb in range(ROW // CH):
        following = scores(qb + 1) if qb + 1 < ROW // CH else None
        rest(qb, st)
        st = following
    between(0)
    between(1)


def angle_tables(lengths, freqs, cos, sin):
    place = lax.broadcasted_iota(jnp.int32, (1, ROW), 1)
    start = jnp.zeros((1, ROW), jnp.int32)
    finish = jnp.int32(0)
    for i in range(SEGS - 1):
        finish = finish + lengths[0, i]
        start = jnp.where(place >= finish, finish, start)
    angles = freqs[...] * (place - start).astype(f32)
    cos[...] = jnp.cos(angles)
    sin[...] = jnp.sin(angles)


def order(z, j):
    places_of = (0, 1, 2, 3), (1, 0, 2, 3), (2, 3, 1, 0), (3, 2, 1, 0)
    s = jnp.int32(0)
    for i, of in enumerate(places_of):
        for k, quarter in enumerate(of):
            if quarter:
                s = s + jnp.where((z == i) & (j == k), quarter, 0)
    return s


EVENTS = {
    3: (("f", 0, 1), ("f", 0, 2), (1, 0, 1)),
    6: ((2, 0, 1),),
    7: (("f", 0, 3), ("s", 1, 0), (1, 0, 2)),
    ("before", 1): ((3, 0, 1), (1, 0, 3), (4, 0, 1)),
    8: ((2, 0, 2), ("f", 1, 1), ("f", 1, 2)),
    11: ((2, 0, 3),),
    13: ((1, 1, 1),),
    15: (("f", 1, 3),),
    ("before", 2): ((3, 0, 2), (4, 0, 2)),
    16: ((1, 1, 2),),
    20: ((3, 0, 3),),
    22: ((1, 1, 3), (2, 1, 1)),
    ("before", 3): ((4, 0, 3),),
    26: ((2, 1, 2),),
    27: ((3, 1, 1),),
    29: ((2, 1, 3), (3, 1, 2)),
    ("before", 4): ((3, 1, 3),),
}
QSLICE = QKV // 8
OSLICE = QR // 8


def forward_kernel(lengths, gains, freqs, x_i, qw_i, kw, vw, ow, cot,
                   mid_o, hid2_o, ho_o, qt_o, kt_o, kk_o, vv_o, w_o, hid1t_o, hid2t_o, cott_o,
                   cos, sin, x, qw, w, hid, ho, qt, kt, kk, vt, vv, qaug, kaug, midb, hidb, hidtb, cb, ctb,
                   zsend, zrecv, xsend, xrecv, ysend, yrecv, csend, crecv, osem, wsem, msem, tsem):
    dp, z, low = places()
    pc, px, py = (partner(low, dp, bit) for bit in (1, 2, 4))
    lx = px - dp + low
    ly = py - dp + low
    lxy = ly + lx - low
    c_at, x_at, y_at = lax.rem(low, 2), lax.rem(low // 2, 2), low // 4
    own = [pltpu.make_async_copy(qw_i, qw, wsem.at[0])]
    own += [pltpu.make_async_copy(src, w.at[z, pl.ds(at, n)], wsem.at[i + 1])
            for i, (src, at, n) in enumerate(((kw, QR, KR), (vw, QR + KR, KR), (ow, QKV, QR)))]
    own += [pltpu.make_async_copy(x_i, x, wsem.at[4])]
    for c in own:
        c.start()
    greet(dp, z, low)
    own[0].wait()
    w[z, 0:QR] = qw[...].T
    own[1].wait()
    own[2].wait()

    def qrows(at, lo=0, hi=QSLICE):
        return pl.ds(pl.multiple_of(at * QSLICE + lo, 16), hi - lo)

    def orows(half, at, core):
        return pl.ds(pl.multiple_of(QKV + half * (QR // 2) + (2 * at + core) * OSLICE, 16), OSLICE)

    def zcopies(part, s, side):
        to = jnp.clip(z + 2 * side - 1, 0, NZ - 1)
        if part == 0:
            slices = ((0, qrows(low)),)
        else:
            slices = ((1, orows(0, y_at, c_at)), (2, orows(1, x_at, c_at)))
        return [put(w.at[s, r], w.at[s, r], zsend.at[i, s, side], zrecv.at[i, s], {"mp": to}) for i, r in slices]

    def send_own(part):
        def go(side):
            for c in zcopies(part, z, side):
                c.start()

        for side in (0, 1):
            pl.when((z < NZ - 1) if side else (z > 0))(functools.partial(go, side))

    send_own(0)
    own[3].wait()
    own[4].wait()

    def copies(part, j, kind):
        s = order(z, j)

        def c(r, sems, semr, i, dev):
            return put(w.at[s, r], w.at[s, r], sems.at[part, j - 1, i], semr.at[part, j - 1, i], {"dp": dev})

        if part == 1:
            if kind == 1:
                return [c(orows(0, y_at, c_at), ysend, yrecv, 0, py), c(orows(1, x_at, c_at), xsend, xrecv, 0, px)]
            return [c(orows(half, at, c_at), csend, crecv, 2 * half + at, pc) for half in (0, 1) for at in (0, 1)]
        cut = QSLICE // 2
        if kind == 1:
            return [c(qrows(low, 0, cut), xsend, xrecv, 0, px), c(qrows(low, cut), ysend, yrecv, 0, py)]
        if kind == 2:
            return [c(qrows(low, 0, cut), ysend, yrecv, 1, py), c(qrows(lx, 0, cut), ysend, yrecv, 2, py),
                    c(qrows(low, cut), xsend, xrecv, 1, px), c(qrows(ly, cut), xsend, xrecv, 2, px)]
        return [c(qrows(at), csend, crecv, i, pc) for i, at in enumerate((low, lx, ly, lxy))]

    def kinds(part):
        return range(1, 3 if part else 4)

    inner = (z > 0) & (z < NZ - 1)

    def pass_on(part, j):
        s = order(z, j)
        return s, jnp.where(s < z, 1, 0)

    def do(kind, part, j):
        if kind == "s":
            send_own(part)
        elif kind == "f":
            @pl.when(inner)
            def _():
                s, side = pass_on(part, j)
                for c in zcopies(part, s, side):
                    c.wait_recv()
                    c.start()
        else:
            if kind == 1:
                @pl.when(jnp.logical_not(inner))
                def _():
                    for c in zcopies(part, order(z, j), 0):
                        c.wait_recv()
            else:
                for c in copies(part, j, kind - 1):
                    c.wait_recv()
            if kind in kinds(part):
                for c in copies(part, j, kind):
                    c.start()

    def beat(step):
        for at, events in EVENTS.items():
            if isinstance(at, int):
                @pl.when(step == at)
                def _(events=events):
                    for e in events:
                        do(*e)

    def before(j):
        for e in EVENTS.get(("before", j), ()):
            do(*e)

    angle_tables(lengths, freqs, cos, sin)
    place = lax.broadcasted_iota(jnp.int32, (1, ROW), 1)
    row = lax.broadcasted_iota(jnp.int32, (128 - HD, ROW), 0)
    segment = jnp.zeros((1, ROW), jnp.int32)
    finish = jnp.int32(0)
    for i in range(SEGS):
        finish = finish + lengths[0, i]
        segment = segment + jnp.where(place >= finish, 1, 0)
    same = row == segment
    qaug[...] = jnp.where(same | (row >= SEGS), 0.0, NEG).astype(bf16)
    kaug[...] = jnp.where(same | ((row >= SEGS) & (row < SEGS + 3)), 1.0, 0.0).astype(bf16)

    def norm(c, _):
        r = chunk(c)
        xx = x[r].astype(f32)
        f = lax.rsqrt(jnp.mean(xx * xx, axis=1, keepdims=True) + eps)
        hid[r] = (xx * f * gains[0:1, :].astype(f32)).astype(bf16)
        return 0

    def turn_copy(i):
        s = lax.rem(i, 2)
        n = ROW // CH
        cols = chunk(lax.rem(i, n))
        return (pltpu.make_async_copy(ctb.at[s], hid1t_o.at[:, cols], tsem.at[0, s]),
                pltpu.make_async_copy(ctb.at[s], cott_o.at[:, cols], tsem.at[0, s]))

    def cot_load(c):
        s = lax.rem(c, 2)
        return pltpu.make_async_copy(cot.at[chunk(c)], cb.at[s], tsem.at[1, s])

    def turn_hid(c, _):
        pl.when(c >= 2)(lambda: turn_copy(c - 2)[0].wait())
        ctb[lax.rem(c, 2)] = hid[chunk(c)].T
        turn_copy(c)[0].start()
        return 0

    def turn_cot(c, _):
        cot_load(c).wait()
        turn_copy(c + 2)[0].wait()
        ctb[lax.rem(c, 2)] = cb[lax.rem(c, 2)].T
        turn_copy(c)[1].start()
        pl.when(c + 2 < ROW // CH)(lambda: cot_load(c + 2).start())
        return 0

    cot_load(0).start()
    cot_load(1).start()
    lax.fori_loop(0, ROW // CH, norm, 0)

    def results(j):
        s = order(z, j)
        h = pl.ds(s * HQ_OWN, HQ_OWN)
        g = pl.ds(s * KV_OWN, KV_OWN)
        r = pl.ds(0, QKV)
        pairs = [(w.at[s, r], w_o.at[s, r]), (qt.at[h], qt_o.at[h]), (kt.at[g], kt_o.at[g]),
                 (kk.at[g], kk_o.at[g]), (vv.at[g], vv_o.at[g])]
        return [pltpu.make_async_copy(a, b, osem.at[j, i]) for i, (a, b) in enumerate(pairs)]

    def quarter(j, _):
        s = order(z, j)
        for i in range(1, NZ):
            @pl.when(j == i)
            def _(i=i):
                if i == 1:
                    lax.fori_loop(0, ROW // CH, turn_hid, 0)
                    lax.fori_loop(0, ROW // CH, turn_cot, 0)
                before(i)

        def one(c, _):
            project(w, hid, qt, kt, kk, vt, vv, cos, sin, qaug, kaug, s, c)
            beat(8 * j + c)
            return 0

        lax.fori_loop(0, ROW // CH, one, 0)

        def two(g, _):
            attend(qt, kk, vt, ho, qaug, KV_OWN * s + g, lambda half: beat(8 * j + 4 + 2 * g + half))
            return 0

        lax.fori_loop(0, KV_OWN, two, 0)
        for c in results(j):
            c.start()
        return 0

    lax.fori_loop(0, NZ, quarter, 0)
    before(NZ)
    last = [pltpu.make_async_copy(ho, ho_o, osem.at[NZ, 0])]
    last += [pltpu.make_async_copy(w.at[s, pl.ds(QKV, QR)], w_o.at[s, pl.ds(QKV, QR)], osem.at[NZ, 1 + s])
             for s in range(NZ)]
    for c in last:
        c.start()

    def mid_copies(c, slot):
        return (pltpu.make_async_copy(midb.at[slot], mid_o.at[chunk(c)], msem.at[0, slot]),
                pltpu.make_async_copy(hidb.at[slot], hid2_o.at[chunk(c)], msem.at[1, slot]),
                pltpu.make_async_copy(hidtb.at[slot], hid2t_o.at[:, chunk(c)], msem.at[2, slot]))

    def out_proj(c, _):
        r = chunk(c)
        slot = lax.rem(c, 2)

        @pl.when(c >= 2)
        def _():
            for m in mid_copies(c - 2, slot):
                m.wait()

        acc = x[r].astype(f32)
        for s in range(NZ):
            acc = acc + tn(ho[QR * s:QR * s + QR, r], w[s, QKV:WR])
        midb[slot] = acc
        f = lax.rsqrt(jnp.mean(acc * acc, axis=1, keepdims=True) + eps)
        h = (acc * f * gains[1:2, :].astype(f32)).astype(bf16)
        hidb[slot] = h
        hidtb[slot] = h.T
        for m in mid_copies(c, slot):
            m.start()
        return 0

    n = ROW // CH
    lax.fori_loop(0, n, out_proj, 0)
    for c in range(max(n - 2, 0), n):
        for m in mid_copies(c, c % 2):
            m.wait()
        turn_copy(c)[1].wait()
    for j in range(NZ):
        for c in results(j):
            c.wait()
    for c in last:
        c.wait()
    for part in range(2):
        def sent(s, side, part=part):
            for c in zcopies(part, s, side):
                c.wait_send()

        for side in (0, 1):
            pl.when((z < NZ - 1) if side else (z > 0))(functools.partial(sent, z, side))
        for j in (1, 2, 3):
            pl.when(inner)(functools.partial(lambda j: sent(*pass_on(part, j)), j))
            for kind in kinds(part):
                for c in copies(part, j, kind):
                    c.wait_send()


def forward(lengths, x, gains, freqs, qw, kw, vw, ow, cot):
    heads = NZ * HQ_OWN
    kv = NZ * KV_OWN
    vm = pltpu.VMEM
    return pl.pallas_call(
        forward_kernel,
        out_shape=(sds((ROW, D), f32), sds((ROW, D), bf16), sds((heads * HD, ROW), bf16),
                   sds((heads, 128, ROW), bf16), sds((kv, 128, ROW), bf16), sds((kv, ROW, 128), bf16),
                   sds((kv, ROW, 128), bf16), sds((NZ, WR, D), bf16), sds((D, ROW), bf16), sds((D, ROW), bf16),
                   sds((D, ROW), bf16)),
        in_specs=[pl.BlockSpec(memory_space=pltpu.SMEM)] + [VM] * 2 + [ANY] * 6,
        out_specs=(ANY,) * 11,
        scratch_shapes=[
            vm((HD // 2, ROW), f32), vm((HD // 2, ROW), f32),
            vm((ROW, D), bf16), vm((D, QR), bf16), vm((NZ, WR, D), bf16), vm((ROW, D), bf16), vm((heads * HD, ROW), bf16),
            vm((heads, 128, ROW), bf16), vm((kv, 128, ROW), bf16), vm((kv, ROW, 128), bf16),
            vm((kv, 128, ROW), bf16), vm((kv, ROW, 128), bf16),
            vm((128 - HD, ROW), bf16), vm((128 - HD, ROW), bf16), vm((2, CH, D), f32), vm((2, CH, D), bf16),
            vm((2, D, CH), bf16), vm((2, CH, D), bf16), vm((2, D, CH), bf16),
            DMA((3, NZ, 2)), DMA((3, NZ)), DMA((2, 3, 3)), DMA((2, 3, 3)), DMA((2, 3, 3)), DMA((2, 3, 3)),
            DMA((2, 3, 4)), DMA((2, 3, 4)), DMA((NZ + 1, 5)), DMA((5,)), DMA((3, 2)), DMA((2, 2))],
        compiler_params=pltpu.CompilerParams(
            collective_id=1, has_side_effects=True, vmem_limit_bytes=60 * 2**20),
        name="attention_forward",
    )(lengths, gains, freqs, x, qw, kw, vw, ow, cot)


def frequencies():
    return jnp.asarray(np.power(np.float32(rope_base), -(np.arange(HD // 2, dtype=np.float32) * 2) / np.float32(HD))[:, None])


class RowSum:
    def __init__(self, z, own, rend, rmid, out, ssem, esem, msem, osem, ring, lag, begun=0, turn=1):
        self.z, self.own, self.ring, self.lag, self.begun, self.turn = z, own, ring, lag, begun, turn
        self.rend, self.rmid, self.out = rend, rmid, out
        self.ssem, self.esem, self.msem, self.osem = ssem, esem, msem, osem

    def who(self, i):
        odd = lax.rem(i // self.turn, 2)
        return 3 * odd, 1 + odd, 2 - odd, 3 - 3 * odd

    def copy(self, kind, i, to, sem=0):
        s = lax.rem(i, self.ring)
        src, dst, rsem = {
            "end": (self.own(i), self.rend.at[s], self.esem),
            "mid": (self.rmid.at[s], self.rmid.at[s], self.msem),
            "out": (self.out.at[s], self.out.at[s], self.osem)}[kind]
        return put(src, dst, self.ssem.at[sem, s], rsem.at[s], {"mp": to})

    def on(self, place, f):
        pl.when(self.z == place)(f)

    def step1(self, i):
        e, o, m, f = self.who(i)
        self.on(e, lambda: self.copy("end", i, o).start())
        self.on(f, lambda: self.copy("end", i, m).start())

    def step2(self, i):
        e, o, m, f = self.who(i)
        s = lax.rem(i, self.ring)

        def go():
            self.copy("end", i, o).wait_recv()
            self.rmid[s] = (self.own(i)[...].astype(f32) + self.rend[s].astype(f32)).astype(bf16)
            self.copy("mid", i, o).start()

        self.on(m, go)

    def step3(self, i):
        e, o, m, f = self.who(i)
        s = lax.rem(i, self.ring)

        def go():
            @pl.when(i >= self.begun)
            def _():
                self.copy("end", i, e).wait_recv()
                self.copy("mid", i, e).wait_recv()

            self.out[s] = (self.own(i)[...].astype(f32) + self.rend[s].astype(f32)
                           + self.rmid[s].astype(f32)).astype(bf16)
            self.copy("out", i, m, 1).start()
            self.copy("out", i, e).start()

        self.on(o, go)

    def step4(self, i):
        e, o, m, f = self.who(i)

        def go():
            self.copy("out", i, o).wait_recv()
            self.copy("out", i, f, 1).start()

        self.on(m, go)

    def arrive(self, i):
        e, o, m, f = self.who(i)
        self.on(e, lambda: self.copy("out", i, o).wait_recv())
        self.on(f, lambda: self.copy("out", i, m).wait_recv())

    def drain(self, i):
        e, o, m, f = self.who(i)

        @pl.when(i >= self.begun)
        def _():
            self.on(e, lambda: self.copy("end", i, o).wait_send())
            self.on(f, lambda: self.copy("end", i, m).wait_send())
            self.on(m, lambda: self.copy("mid", i, o).wait_send())

        def middle():
            self.copy("out", i, f, 1).wait_send()

        def owner():
            self.copy("out", i, m, 1).wait_send()
            self.copy("out", i, e).wait_send()

        self.on(m, middle)
        self.on(o, owner)

    def half_done(self, i):
        e, o, m, f = self.who(i)
        self.on(e, lambda: self.copy("end", i, o).wait_send())
        self.on(f, lambda: self.copy("end", i, m).wait_send())
        self.on(m, lambda: self.copy("mid", i, o).wait_send())

        def owner():
            self.copy("end", i, e).wait_recv()
            self.copy("mid", i, e).wait_recv()

        self.on(o, owner)

    def tick(self, t, count, finish, begun=0, ahead=0):
        def last(i):
            self.arrive(i)
            finish(i)
            self.drain(i)

        for lag, step in ((4, last), (3, self.step4), (2, self.step3), (1, self.step2), (0, self.step1)):
            i = t - lag * self.lag
            lo, hi = (begun, count + ahead) if lag < 2 else (0, count)
            pl.when((i >= lo) & (i < hi))(functools.partial(step, i))


class GradSum:
    def __init__(self, dp, low, width, cut, g, c1, x1, y1, x2, y2, ssem, rsem, emit, wide=False):
        self.pc, self.px, self.py = (partner(low, dp, bit) for bit in (1, 2, 4))
        self.c, self.x, self.y = lax.rem(low, 2), lax.rem(low // 2, 2), low // 4
        self.g, self.c1, self.x1, self.y1, self.x2, self.y2 = g, c1, x1, y1, x2, y2
        self.ssem, self.rsem, self.emit = ssem, rsem, emit
        self.width, self.cut, self.wide = width, cut, wide

    def cols(self, u, lo, hi):
        if self.wide:
            return (pl.ds(pl.multiple_of(u * self.width + lo, 128), hi - lo),)
        return (pl.ds(lo, hi - lo),)

    def part(self, u, *at, lo=None, hi=None):
        lo, hi = (0, self.width) if lo is None else (lo, hi)
        return (() if self.wide else (u,)) + at + self.cols(u, lo, hi)

    def put_block(self, u, k, res):
        self.put_part(u, k, 0, self.width, res)

    def put_part(self, u, k, lo, hi, res):
        self.g[self.part(u, k // 4, (k // 2) % 2, k % 2, slice(None), lo=lo, hi=hi)] = res.astype(bf16)

    def copies(self, u, k):
        g, c, x, y = self.g, self.c, self.x, self.y
        every = slice(None)
        a = dict(lo=0, hi=self.cut)
        b = dict(lo=self.cut, hi=self.width)

        def mk(i, src, dst, dev):
            return put(src, dst, self.ssem.at[u, i], self.rsem.at[u, i], {"dp": dev})

        if k == 0:
            return [mk(0, g.at[self.part(u, every, every, 1 - c, every)], self.c1.at[u], self.pc)]
        if k == 1:
            return [mk(1, g.at[self.part(u, every, 1 - x, c, every, **a)], self.x1.at[u], self.px),
                    mk(2, g.at[self.part(u, 1 - y, every, c, every, **b)], self.y1.at[u], self.py)]
        return [mk(3, g.at[self.part(u, 1 - y, x, c, every, **a)], self.y2.at[u], self.py),
                mk(4, g.at[self.part(u, y, 1 - x, c, every, **b)], self.x2.at[u], self.px)]

    def start(self, u):
        for c in self.copies(u, 0):
            c.start()

    def stage(self, k, u):
        width, cut = self.width, self.cut
        g, c, x, y = self.g, self.c, self.x, self.y
        for cp in self.copies(u, k - 1):
            cp.wait_recv()

        def at(i, j, lo, hi):
            return self.part(u, i, j, c, slice(None), lo=lo, hi=hi)

        def add(i, j, lo, hi, other):
            g[at(i, j, lo, hi)] = (g[at(i, j, lo, hi)].astype(f32) + other.astype(f32)).astype(bf16)

        if k == 1:
            for i in range(2):
                for j in range(2):
                    add(i, j, 0, width, self.c1[u, i, j])
        elif k == 2:
            for i in range(2):
                add(i, x, 0, cut, self.x1[u, i])
                add(y, i, cut, width, self.y1[u, i])
        else:
            self.emit(u, 0, cut, g[at(y, x, 0, cut)].astype(f32) + self.y2[u].astype(f32))
            self.emit(u, cut, width, g[at(y, x, cut, width)].astype(f32) + self.x2[u].astype(f32))
        if k < 3:
            for cp in self.copies(u, k):
                cp.start()

    def drain(self, u):
        for k in range(3):
            for cp in self.copies(u, k):
                cp.wait_send()


def sum_scratch(count, width, cut):
    vm = pltpu.VMEM
    rest = width - cut
    return [vm((count, 2, 2, 2, 192, width), bf16), vm((count, 2, 2, 192, width), bf16),
            vm((count, 2, 192, cut), bf16), vm((count, 2, 192, rest), bf16),
            vm((count, 192, rest), bf16), vm((count, 192, cut), bf16), DMA((count, 5)), DMA((count, 5))]


def ring_scratch(ring, rows):
    vm = pltpu.VMEM
    return [vm((ring, rows, D), bf16), vm((ring, rows, D), bf16), vm((ring, rows, D), bf16),
            DMA((2, ring)), DMA((ring,)), DMA((ring,)), DMA((ring,))]


MLP_UNITS = 6
MLP_WIDTH = 512


def feed_kernel(gains, hid2, cot, mid, hid2t_i, cott_i, gw_i, uw_i, dw_i, w_i,
                mlp_o, gm_o, dot_o, gmlt_o, gain2_o, gate_o, up_o, down_o, end_o, mid_o,
                gw, uw, dw, a3, side, own, hb, cb, tb, mb, cb2, gmb, dotb, gmltb,
                rend, rmid, out, zs, ze, zm, zo,
                g, c1, x1, y1, x2, y2, gs, gr,
                lsem, bsem, tsem, msem, wsem, asem, vsem):
    dp, z, low = places()
    loads = [pltpu.make_async_copy(a, b, lsem.at[i]) for i, (a, b) in enumerate(
        ((gw_i, gw), (uw_i, uw), (dw_i, dw), (hid2t_i, side), (cott_i, side)))]
    oloads = []
    for s in range(NZ):
        for ref, lo, hi in ((dw, 0, D - 2 * CH), (hb.at[0], D - 2 * CH, D - CH), (hb.at[1], D - CH, D)):
            a, b = max(lo, s * QR), min(hi, (s + 1) * QR)
            if a < b:
                oloads.append(pltpu.make_async_copy(
                    w_i.at[s, pl.ds(QKV + a - s * QR, b - a)], ref.at[pl.ds(a - lo, b - a)], vsem.at[len(oloads)]))
    nc = ROW // CH
    nb = ROW // BL
    nj = ROW // 128
    pair = 128 // BL
    per = BL3 // BL

    def chunk_loads(c):
        return [pltpu.make_async_copy(src.at[chunk(c)], dst.at[lax.rem(c, 2)], bsem.at[i, lax.rem(c, 2)])
                for i, (src, dst) in enumerate(((hid2, hb), (cot, cb)))]

    for c in chunk_loads(0):
        c.start()
    for c in loads[:4]:
        c.start()
    greet(dp, z, low)
    def emit(u, lo, hi, v):
        half = lax.rem(u, 2) * MLP_WIDTH
        at = pl.ds(pl.multiple_of(half + lo, 128), hi - lo)
        for i, ref in enumerate((gate_o, up_o, down_o)):
            @pl.when(u // 2 == i)
            def _(ref=ref):
                ref[:, at] = v

    zsum = RowSum(z, lambda i: own.at[chunk(lax.rem(i, nb), BL)], rend, rmid, out, zs, ze, zm, zo, RING, LAG, turn=BL3 // BL)
    gsum = GradSum(dp, low, MLP_WIDTH, MLP_WIDTH // 2, g, c1, x1, y1, x2, y2, gs, gr, emit)
    gain2_o[...] = jnp.zeros_like(gain2_o)

    def gm_loads(j):
        r = chunk(j, 128)
        return [pltpu.make_async_copy(mid.at[r], mb, msem.at[0]),
                pltpu.make_async_copy(cot.at[r], cb2, msem.at[1])]

    def gm_writes(j):
        r = chunk(j, 128)
        s = lax.rem(j, 2)
        return [pltpu.make_async_copy(gmb.at[s], gm_o.at[r], wsem.at[0, s]),
                pltpu.make_async_copy(dotb.at[s], dot_o.at[:, r], wsem.at[1, s]),
                pltpu.make_async_copy(gmltb.at[s], gmlt_o.at[:, r], wsem.at[2, s])]

    def finish_pair(j):
        s = lax.rem(j, 2)
        for c in gm_loads(j):
            c.wait()

        @pl.when(j >= 2)
        def _():
            for c in gm_writes(j - 2):
                c.wait()

        gh = jnp.concatenate([out[lax.rem(j * pair + k, RING)] for k in range(pair)], axis=0).astype(f32)
        m = mb[...]
        f = lax.rsqrt(jnp.mean(m * m, axis=1, keepdims=True) + eps)
        n = m * f
        gn = gh * n
        gain2_o[...] += jnp.sum(gn, axis=0, keepdims=True)
        ga = gains[1:2, :].astype(f32)
        gm = cb2[...].astype(f32) + f * (gh * ga - n * jnp.mean(gn * ga, axis=1, keepdims=True))
        gmb[s] = gm
        low_gm = gm.astype(bf16)
        gmltb[s] = low_gm.T

        @pl.when(j == 0)
        def _():
            for c in oloads:
                c.wait()

        dotb[s, 0:D - 2 * CH] = nt(dw[...], low_gm).astype(bf16)
        for k in range(2):
            first = D - (2 - k) * CH
            dotb[s, first:first + CH] = nt(hb[k], low_gm).astype(bf16)
        for c in gm_writes(j):
            c.start()

        @pl.when(j + 1 < nj)
        def _():
            for c in gm_loads(j + 1):
                c.start()

    def finish(i):
        pl.when(lax.rem(i, pair) == pair - 1)(lambda: finish_pair(i // pair))

    for c in gm_loads(0):
        c.start()

    def tick(t):
        for k in range(per):
            zsum.tick(per * t + k, nb, finish, ahead=AHEAD * per)

    again = pltpu.make_async_copy(mlp_o.at[pl.ds(0, AHEAD * BL3)], own.at[pl.ds(0, AHEAD * BL3)], asem)

    def mlp_write(c):
        return pltpu.make_async_copy(tb.at[lax.rem(c, 2)], mlp_o.at[chunk(c)], tsem.at[lax.rem(c, 2)])

    def mlp_chunk(c, _):
        r = chunk(c)
        s = lax.rem(c, 2)
        for cp in chunk_loads(c):
            cp.wait()

        @pl.when(c + 1 < nc)
        def _():
            for cp in chunk_loads(c + 1):
                cp.start()

        @pl.when(c == 0)
        def _():
            loads[0].wait()
            loads[1].wait()
            loads[2].wait()

        gate = nn(hb[s], gw[...])
        upper = nn(hb[s], uw[...])
        ga = nt(cb[s], dw[...])
        sigma = 1.0 / (1.0 + jnp.exp(-gate))
        silu = gate * sigma
        gg = (ga * upper * sigma * (1.0 + gate * (1.0 - sigma))).astype(bf16)
        gu = (ga * silu).astype(bf16)
        act = (silu * upper).astype(bf16)
        a3[0, r] = gg
        a3[1, r] = gu
        a3[2, r] = act
        own[r] = (nt(gg, gw[...]) + nt(gu, uw[...])).astype(bf16)
        tick(2 * c)

        @pl.when(c >= 2)
        def _():
            mlp_write(c - 2).wait()

        tb[s] = nn(act, dw[...]).astype(bf16)
        mlp_write(c).start()
        tick(2 * c + 1)
        return 0

    def unit(u):
        @pl.when(u == 0)
        def _():
            loads[3].wait()

        @pl.when(u == 4)
        def _():
            loads[4].start()
            loads[4].wait()

        which = u // 2
        cols = chunk(lax.rem(u, 2), MLP_WIDTH)
        rhs = a3[which, :, cols]
        for k in range(8):
            gsum.put_block(u, k, nn(side[k * 192:(k + 1) * 192], rhs))
        gsum.start(u)

    def beat(t, _):
        first = 2 * nc
        u = t - first

        @pl.when(t == first)
        def _():
            for c in range(max(nc - 2, 0), nc):
                mlp_write(c).wait()

        @pl.when(t == nb // per)
        def _():
            again.start()
            again.wait()

        pl.when(u < MLP_UNITS)(lambda: unit(u))
        tick(t)
        for k, lag in ((3, 10), (2, 6), (1, 2)):
            v = u - lag
            pl.when((v >= 0) & (v < MLP_UNITS))(functools.partial(gsum.stage, k, v))
        return 0

    lax.fori_loop(0, nc, mlp_chunk, 0)
    for c in oloads:
        c.start()
    lax.fori_loop(2 * nc, (nb + 4 * LAG + per - 1) // per, beat, 0)

    def drains(u, _):
        gsum.drain(u)
        return 0

    lax.fori_loop(0, MLP_UNITS, drains, 0)
    for j in range(nj - 2, nj):
        for c in gm_writes(j):
            c.wait()
    keep = []
    for i in range(AHEAD * per):
        zsum.half_done(nb + i)
        s = (nb + i) % RING
        keep += [pltpu.make_async_copy(rend.at[s], end_o.at[i], zs.at[0, s]),
                 pltpu.make_async_copy(rmid.at[s], mid_o.at[i], zs.at[1, s])]
    for c in keep:
        c.start()
    for c in keep:
        c.wait()


def feed(gains, hid2, cot, mid, hid2t, cott, gw, uw, dw, w):
    vm = pltpu.VMEM
    ff = gw.shape[1]
    return pl.pallas_call(
        feed_kernel,
        out_shape=(sds((ROW, D), bf16), sds((ROW, D), f32), sds((D, ROW), bf16), sds((D, ROW), bf16),
                   sds((1, D), f32), sds((D // 8, ff), f32), sds((D // 8, ff), f32), sds((D // 8, ff), f32),
                   sds((AHEAD * BL3 // BL, BL, D), bf16), sds((AHEAD * BL3 // BL, BL, D), bf16)),
        in_specs=[VM] + [ANY] * 9,
        out_specs=(ANY, ANY, ANY, ANY, VM, VM, VM, VM, ANY, ANY),
        scratch_shapes=[
            vm((D, ff), bf16), vm((D, ff), bf16), vm((ff, D), bf16), vm((3, ROW, ff), bf16),
            vm((D, ROW), bf16), vm((ROW, D), bf16),
            vm((2, CH, D), bf16), vm((2, CH, D), bf16), vm((2, CH, D), bf16),
            vm((128, D), f32), vm((128, D), bf16), vm((2, 128, D), f32), vm((2, D, 128), bf16),
            vm((2, D, 128), bf16)]
        + ring_scratch(RING, BL) + sum_scratch(MLP_UNITS, MLP_WIDTH, MLP_WIDTH // 2)
        + [DMA((5,)), DMA((2, 2)), DMA((2,)), DMA((2,)), DMA((3, 2)), DMA, DMA((6,))],
        compiler_params=pltpu.CompilerParams(
            collective_id=2, has_side_effects=True, vmem_limit_bytes=63 * 2**20),
        name="feed_forward",
    )(gains, hid2, cot, mid, hid2t, cott, gw, uw, dw, w)


RING3 = 10
LAG3 = 2
WIDTH = QR
BEATS = 9
CUT = 128


def unrotate(u, co, si):
    a = u[0:HD // 2]
    b = u[HD // 2:HD]
    return jnp.concatenate([a * co + b * si, b * co - a * si], axis=0).astype(bf16)


def attend_back(qk, kk, vv, dot, ho, dk, dv, gt, cos, sin, g, gg, qb):
    lo = qb * CH
    hi = lo + CH
    heads = NZ * HQ_OWN * 128
    q = jnp.concatenate([qk[pl.ds(pl.multiple_of((2 * g + h) * 128, 128), 128), lo:hi] for h in range(2)], axis=1)
    parts = []
    for h in range(2):
        do = dot[pl.ds(pl.multiple_of((2 * g + h) * HD, 32), HD), lo:hi]
        o = ho[pl.ds(pl.multiple_of((2 * g + h) * HD, 32), HD), lo:hi]
        delta = jnp.sum(do.astype(f32) * o.astype(f32), axis=0, keepdims=True)
        extra = extra_rows(jnp.zeros((128 - HD, CH), f32), -delta, 0)
        parts.append(jnp.concatenate([do, extra], axis=0))
    do = jnp.concatenate(parts, axis=1)
    do_t = do.T
    q_t = q.T
    dq = jnp.zeros((128, 2 * CH), f32)
    for kb in range(qb + 1):
        ks = slice(kb * CH, (kb + 1) * CH)
        p = jnp.exp2(nn(kk[g, ks, :], q) * C2)
        if kb == qb:
            ki = lax.broadcasted_iota(jnp.int32, (CH, CH), 0)
            qi = lax.broadcasted_iota(jnp.int32, (CH, CH), 1)
            keep = jnp.concatenate([ki <= qi, ki <= qi], axis=1)
            p = jnp.where(keep, p, 0.0)
        ds = (p * nn(vv[g, ks, :], do)).astype(bf16)
        dvb = nn(p.astype(bf16), do_t)
        dkb = nn(ds, q_t)
        if kb == qb:
            dv[ks, :] = dvb
            dk[ks, :] = dkb
        else:
            dv[ks, :] += dvb
            dk[ks, :] += dkb
        dq = dq + nn(qk[pl.ds(pl.multiple_of(heads + g * 128, 128), 128), ks], ds)
    first = (g // KV_OWN) * QKV + gg * 2 * HD
    for h in range(2):
        at = pl.ds(pl.multiple_of(first + h * HD, 32), HD)
        gt[at, lo:hi] = unrotate(dq[0:HD, h * CH:(h + 1) * CH] * SCALE, cos[:, lo:hi], sin[:, lo:hi])


def backward_kernel(groups, lengths, gains, freqs, gain2_i, x, mid, mlp, gm, dot_i, gmlt, hid1t, ho_i, qt_i, kt_i, kk_i, vv_i, w_i, end_i, mid_i,
                    out_o, xg_o, qg_o, kg_o, vg_o, og_o, gains_o,
                    cos, sin, w, gbuf, ho, qk, kk, vv, dk, dv, gt, dot, ga1, own, mb2, ob2, xb, gb, ob,
                    rend, rmid, out, zs, ze, zm, zo,
                    c1, x1, y1, x2, y2, gs, gr, og, oc1, ox1, oy1, ox2, oy2, ogs, ogr, tb, gsend, grecv,
                    lsem, bsem, wsem, psem, osem, isem, tsem, ssem, rsem, asem):
    dp, z, low = places()
    qrows = NZ * HQ_OWN * 128
    loads = [pltpu.make_async_copy(ho_i, ho, lsem.at[1]),
             pltpu.make_async_copy(dot_i, dot, lsem.at[0]),
             pltpu.make_async_copy(kk_i, kk, lsem.at[2]),
             pltpu.make_async_copy(vv_i, vv, lsem.at[3])]
    loads += [pltpu.make_async_copy(qt_i, qk.at[pl.ds(0, qrows)], lsem.at[12]),
              pltpu.make_async_copy(kt_i, qk.at[pl.ds(qrows, NZ * KV_OWN * 128)], lsem.at[13])]
    wloads = [pltpu.make_async_copy(w_i.at[s, pl.ds(0, QKV)], w.at[s], lsem.at[14 + s]) for s in range(NZ)]
    late = [pltpu.make_async_copy(hid1t, qk.at[pl.ds(0, D)], lsem.at[18])]
    nb = ROW // BL3
    nt_blocks = ROW // TB

    def own_load(i):
        s = lax.rem(i, RING3)
        return pltpu.make_async_copy(mlp.at[chunk(i, BL3)], own.at[s], isem.at[s])

    def mid_load(i):
        s = lax.rem(i, 2)
        return pltpu.make_async_copy(mid.at[chunk(i, BL3)], mb2.at[s], osem.at[0, s])

    def out_write(i):
        s = lax.rem(i, 2)
        return pltpu.make_async_copy(ob2.at[s], out_o.at[chunk(i, BL3)], osem.at[1, s])

    def turned_load(k):
        return pltpu.make_async_copy(gmlt.at[pl.ds(k * 192, 192)], tb.at[k % 2], tsem.at[k % 2])

    begun = [pltpu.make_async_copy(src, dst.at[pl.ds(0, AHEAD)], asem.at[i])
             for i, (src, dst) in enumerate(((end_i, rend), (mid_i, rmid)))]
    for c in begun:
        c.start()
    for i in range(2 * LAG3 + 2):
        own_load(i).start()
    mid_load(0).start()
    turned_load(0).start()
    turned_load(1).start()
    for c in loads:
        c.start()
    greet(dp, z, low, range(1, 8))
    angle_tables(lengths, freqs, cos, sin)
    zsum = RowSum(z, lambda i: own.at[lax.rem(i, RING3)], rend, rmid, out, zs, ze, zm, zo, RING3, LAG3, AHEAD)

    def emit(u, lo, hi, v):
        if u == 0:
            qg_o[:, lo:hi] = v
            return
        for ref, first in ((kg_o, 0), (vg_o, KR)):
            a, b = max(lo, first), min(hi, first + KR)
            if a < b:
                ref[:, a - first:b - first] = v[:, a - lo:b - lo]

    def emit_o(u, lo, hi, v):
        og_o[:, lo:hi] = v

    gsum = GradSum(dp, low, WIDTH, CUT, gbuf, c1, x1, y1, x2, y2, gs, gr, emit, True)
    osum = GradSum(dp, low, WIDTH, CUT, og, oc1, ox1, oy1, ox2, oy2, ogs, ogr, emit_o)

    def finish(i):
        mid_load(i).wait()
        s = lax.rem(i, 2)

        @pl.when(i >= 2)
        def _():
            out_write(i - 2).wait()

        ob2[s] = (mb2[s] + out[lax.rem(i, RING3)].astype(f32)).astype(bf16)
        out_write(i).start()

        @pl.when(i + 1 < nb)
        def _():
            mid_load(i + 1).start()

    def tick(beat):
        t = beat + 2 * LAG3
        pl.when((t >= AHEAD) & (t < nb))(lambda: own_load(t).wait())
        zsum.tick(t, nb, finish, begun=AHEAD)
        pl.when(t + 2 < nb)(lambda: own_load(t + 2).start())

    for i in range(AHEAD):
        own_load(i).wait()
    for c in begun:
        c.wait()
    tick(0)
    tick(1)
    loads[0].wait()
    o_rows = ho[pl.ds(pl.multiple_of(z * QR, 128), QR), :]
    for k in range(8):
        turned_load(k).wait()
        osum.put_block(0, k, nt(tb[k % 2], o_rows))
        if k + 2 < 8:
            turned_load(k + 2).start()
    osum.start(0)
    tick(2)
    for c in loads[1:]:
        c.wait()
    for c in wloads:
        c.start()

    def quarter(s, _):
        def one(gg, _):
            g = KV_OWN * s + gg
            for qb in range(ROW // CH):
                attend_back(qk, kk, vv, dot, ho, dk, dv, gt, cos, sin, g, gg, qb)
                done = 10 * g + qb * (qb + 1) // 2
                was, now = (done * BEATS) // 80, ((done + qb + 1) * BEATS) // 80
                pl.when(now > was)(functools.partial(tick, 3 + was))
            first = pl.multiple_of(s * QKV + QR + gg * HD, 32)
            gt[pl.ds(first, HD), :] = unrotate(dk[...].T[0:HD] * SCALE, cos[...], sin[...])
            gt[pl.ds(pl.multiple_of(first + KR, 32), HD), :] = dv[...].T[0:HD].astype(bf16)
            return 0

        lax.fori_loop(0, KV_OWN, one, 0)
        for k in (1, 2, 3):
            pl.when(s == k - 1)(functools.partial(osum.stage, k, 0))
        return 0

    lax.fori_loop(0, NZ, quarter, 0)
    beats = 3 + BEATS
    for c in late:
        c.start()
    for c in wloads + late:
        c.wait()

    for u in range(2):
        rhs = gt[pl.ds(pl.multiple_of(z * QKV + u * WIDTH, 128), WIDTH), :]
        for k in range(8):
            gsum.put_block(u, k, nt(qk[k * 192:(k + 1) * 192, :], rhs))
        gsum.start(u)
        tick(beats + u)
    beats += 2

    def tail_loads(b, slot):
        r = chunk(b, TB)
        return [pltpu.make_async_copy(x.at[r], xb.at[slot], bsem.at[0, slot]),
                pltpu.make_async_copy(gm.at[r], gb.at[slot], bsem.at[1, slot])]

    def out_copy(b, slot):
        return pltpu.make_async_copy(ob.at[slot], xg_o.at[chunk(b, TB)], psem.at[slot])

    for c in tail_loads(0, 0):
        c.start()
    ga1[...] = jnp.zeros_like(ga1)

    def tail(b, _):
        slot = lax.rem(b, 2)

        @pl.when(b + 1 < nt_blocks)
        def _():
            for c in tail_loads(b + 1, 1 - slot):
                c.start()

        r = chunk(b, TB)
        acc = jnp.zeros((TB, D), f32)
        for s in range(NZ):
            acc = acc + tn(gt[QKV * s:QKV * s + QKV, r], w[s])
        for c in tail_loads(b, slot):
            c.wait()

        @pl.when(b >= 2)
        def _():
            out_copy(b - 2, slot).wait()

        xx = xb[slot].astype(f32)
        f = lax.rsqrt(jnp.mean(xx * xx, axis=1, keepdims=True) + eps)
        n = xx * f
        gn = acc * n
        ga1[...] += jnp.sum(gn, axis=0, keepdims=True)
        ga = gains[0:1, :].astype(f32)
        res = gb[slot] + f * (acc * ga - n * jnp.mean(gn * ga, axis=1, keepdims=True))
        ob[slot] = res.astype(bf16)
        out_copy(b, slot).start()
        tick(beats + b)
        pl.when(b == 0)(lambda: (gsum.stage(1, 0), gsum.stage(1, 1)) and None)
        pl.when(b == 1)(lambda: gsum.stage(2, 0))
        pl.when(b == 2)(lambda: gsum.stage(2, 1))
        pl.when(b == 3)(lambda: gsum.stage(3, 0))
        return 0

    lax.fori_loop(0, nt_blocks, tail, 0)
    beats += nt_blocks

    def gains_copy(mask):
        to = flip(low, mask)
        return put(gsend.at[to], grecv.at[low], ssem.at[mask], rsem.at[mask], {"dp": dp - low + to})

    share = D // 8 // groups
    for k in range(8):
        for i, v in enumerate((ga1, gain2_i)):
            gsend[k, i:i + 1, 0:D // 8] = jnp.concatenate(
                [v[:, (g * 8 + k) * share:(g * 8 + k + 1) * share] for g in range(groups)], axis=1)
    for mask in range(1, 8):
        gains_copy(mask).start()

    def rest(t, _):
        tick(t)
        return 0

    ends = nb + 2 * LAG3
    if beats < ends:
        lax.fori_loop(beats, ends, rest, 0)
    gsum.stage(3, 1)
    total = gsend[low]
    for mask in range(1, 8):
        gains_copy(mask).wait_recv()
        total = total + grecv[flip(low, mask)]
    gains_o[...] = total
    for mask in range(1, 8):
        gains_copy(mask).wait_send()
    for u in range(2):
        gsum.drain(u)
    osum.drain(0)
    for b in range(nt_blocks - 2, nt_blocks):
        out_copy(b, b % 2).wait()
    for i in (nb - 2, nb - 1):
        out_write(i).wait()


def backward(groups, lengths, gains, freqs, gain2_sum, x, mid, mlp, gm, dot, gmlt, hid1t, ho, qt, kt, kk, vv, w, ends, mids):
    vm = pltpu.VMEM
    heads = NZ * HQ_OWN
    kv = NZ * KV_OWN
    return pl.pallas_call(
        functools.partial(backward_kernel, groups),
        out_shape=(sds((ROW, D), bf16), sds((ROW, D), bf16), sds((D // 8, QR), f32), sds((D // 8, KR), f32),
                   sds((D // 8, KR), f32), sds((D // 8, QR), f32), sds((8, 256), f32)),
        in_specs=[pl.BlockSpec(memory_space=pltpu.SMEM)] + [VM] * 3 + [ANY] * 15,
        out_specs=(ANY, ANY) + (VM,) * 5,
        scratch_shapes=[
            vm((HD // 2, ROW), f32), vm((HD // 2, ROW), f32), vm((NZ, QKV, D), bf16), vm((2, 2, 2, 192, 2 * WIDTH), bf16), vm((heads * HD, ROW), bf16),
            vm(((heads + kv) * 128, ROW), bf16), vm((kv, ROW, 128), bf16), vm((kv, ROW, 128), bf16),
            vm((ROW, 128), f32), vm((ROW, 128), f32), vm((NZ * QKV, ROW), bf16),
            vm((heads * HD, ROW), bf16), vm((1, D), f32),
            vm((RING3, BL3, D), bf16), vm((2, BL3, D), f32), vm((2, BL3, D), bf16),
            vm((2, TB, D), bf16), vm((2, TB, D), f32), vm((2, TB, D), bf16)]
        + ring_scratch(RING3, BL3) + sum_scratch(2, WIDTH, CUT)[1:] + sum_scratch(1, WIDTH, CUT)
        + [vm((2, 192, ROW), bf16), vm((8, 8, 256), f32), vm((8, 8, 256), f32),
           DMA((19,)), DMA((2, 2)), DMA((2,)), DMA((2,)), DMA((2, 2)), DMA((RING3,)), DMA((2,)), DMA((8,)), DMA((8,)), DMA((2,))],
        compiler_params=pltpu.CompilerParams(
            collective_id=3, has_side_effects=True, vmem_limit_bytes=63 * 2**20),
        name="attention_backward",
    )(lengths, gains, freqs, gain2_sum, x, mid, mlp, gm, dot, gmlt, hid1t, ho, qt, kt, kk, vv, w,
      ends, mids)


def by_block(v, groups):
    if groups == 1:
        return v
    rows, cols = v.shape
    return v.reshape(groups, 8, rows // (8 * groups), cols).transpose(1, 0, 2, 3).reshape(rows, cols)


def body(groups, inputs, lengths, q_weight, k_weight, v_weight, o_weight, gate_weight, up_weight, down_weight,
         attn_gain, mlp_gain, cotangent):
    x = inputs.reshape(ROW, D)
    cot = cotangent.reshape(ROW, D)
    first = lax.broadcasted_iota(jnp.int32, (2, D), 0) == 0
    gains = jnp.where(first, attn_gain[None, :], mlp_gain[None, :])
    freqs = frequencies()
    mid, hid2, ho, qt, kt, kk, vv, w, hid1t, hid2t, cott = forward(
        lengths, x, gains, freqs, q_weight, k_weight.T, v_weight.T, o_weight, cot)
    mlp, gm, dot, gmlt, gain2_sum, gate_g, up_g, down_g, ends, mids = feed(
        gains, hid2, cot, mid, by_block(hid2t, groups), by_block(cott, groups), gate_weight, up_weight, down_weight, w)
    output, input_grad, q_g, k_g, v_g, o_g, gain_sums = backward(
        groups, lengths, gains, freqs, gain2_sum, x, mid, mlp, gm, dot, by_block(gmlt, groups), by_block(hid1t, groups),
        ho, qt.reshape(-1, ROW), kt.reshape(-1, ROW), kk, vv, w, ends.reshape(-1, BL3, D), mids.reshape(-1, BL3, D))
    grads = [q_g, k_g, v_g, o_g, gate_g, up_g, down_g]
    if groups > 1:
        same = [[g * 8 + low for g in range(groups)] for low in range(8)]
        def over(v, dim=0):
            return lax.psum_scatter(v, "dp", scatter_dimension=dim, axis_index_groups=same, tiled=True)

        grads = [over(v) for v in grads]
        gain_sums = over(gain_sums[:, 0:D // 8], 1)
    output, input_grad, *grads = hand_over(gain_sums, output, input_grad, *grads)
    grads[3], grads[6] = grads[3].T, grads[6].T
    return (output.reshape(1, ROW, D), input_grad.reshape(1, ROW, D), *grads)


def hand_over_kernel(n, sums, *refs):
    first, second = refs[2 * n:2 * n + 2]
    refs = refs[:2 * n] + refs[2 * n + 2:]
    held, load, store = refs[2 * n:3 * n], refs[3 * n], refs[3 * n + 1]
    first[...] = sums[0, 0:first.shape[0]]
    second[...] = sums[1, 0:second.shape[0]]
    pieces = []
    for i in range(n):
        rows = held[i].shape[0]
        parts = 4 if rows % 64 == 0 and rows > 512 else 1
        pieces += [(i, pl.ds(p * (rows // parts), rows // parts)) for p in range(parts)]
    come = [pltpu.make_async_copy(refs[i].at[r], held[i].at[r], load.at[k]) for k, (i, r) in enumerate(pieces)]
    go = [pltpu.make_async_copy(held[i].at[r], refs[n + i].at[r], store.at[k]) for k, (i, r) in enumerate(pieces)]
    for c in come:
        c.start()
    for a, b in zip(come, go):
        a.wait()
        b.start()
    for c in go:
        c.wait()


def hand_over(sums, *arrays):
    n = len(arrays)
    keep = arrays[-1].shape[0]
    return pl.pallas_call(
        functools.partial(hand_over_kernel, n),
        out_shape=tuple(sds(v.shape, v.dtype) for v in arrays) + (sds((keep,), f32),) * 2,
        in_specs=[VM] + [ANY] * n,
        out_specs=(ANY,) * n + (VM,) * 2,
        scratch_shapes=[pltpu.VMEM(v.shape, v.dtype) for v in arrays] + [DMA((4 * n,)), DMA((4 * n,))],
        compiler_params=pltpu.CompilerParams(vmem_limit_bytes=63 * 2**20),
        name="hand_over",
    )(sums, *arrays)


def solution(mesh):
    row = P("dp", None, None)
    in_specs = (row, P("dp", None), P(None, "mp"), P(None, "mp"), P(None, "mp"), P("mp", None),
                P(None, "mp"), P(None, "mp"), P("mp", None), P(), P(), row)
    out_specs = (row, row, P("dp", "mp"), P("dp", "mp"), P("dp", "mp"), P("mp", "dp"),
                 P("dp", "mp"), P("dp", "mp"), P("mp", "dp"), P("dp"), P("dp"))
    return jax.shard_map(functools.partial(body, mesh.shape["dp"] // 8), mesh=mesh, in_specs=in_specs,
                         out_specs=out_specs, check_vma=False)
```

```python
import functools

import jax
import jax.numpy as jnp
import numpy as np
from jax import lax
from jax.experimental import pallas as pl
from jax.experimental.pallas import tpu as pltpu
from jax.sharding import PartitionSpec as P

D = 1536
HD = 96
ROW = 1024
SEGS = 4
NZ = 4
CH = 256
TB = 256
BL = 64
LAG = 2
RING = 10
BL3 = 64
AHEAD = 4
HQ_OWN = 4
KV_OWN = 2
QR = HQ_OWN * HD
KR = KV_OWN * HD
QKV = QR + 2 * KR
WR = QKV + QR
SCALE = HD ** -0.5
C2 = SCALE * 1.4426950408889634
NEG = -1e30
eps = 1e-05
rope_base = 100000.0
f32 = jnp.float32
bf16 = jnp.bfloat16
MESH = pl.DeviceIdType.MESH
ANY = pl.BlockSpec(memory_space=pl.ANY)
VM = pl.BlockSpec(memory_space=pltpu.VMEM)
DMA = pltpu.SemaphoreType.DMA
sds = jax.ShapeDtypeStruct


def nt(a, b):
    return lax.dot_general(a, b, (((1,), (1,)), ((), ())), preferred_element_type=f32)


def nn(a, b):
    return lax.dot_general(a, b, (((1,), (0,)), ((), ())), preferred_element_type=f32)


def tn(a, b):
    return lax.dot_general(a, b, (((0,), (0,)), ((), ())), preferred_element_type=f32)


def chunk(c, size=CH):
    return pl.ds(pl.multiple_of(c * size, size), size)


def places():
    dp = lax.axis_index("dp")
    z = lax.axis_index("mp")
    low = lax.rem(dp, 8)
    return dp, z, low


def partner(low, dp, bit):
    on = lax.rem(low // bit, 2)
    return dp + bit - 2 * bit * on


def flip(low, mask):
    for bit in (1, 2, 4):
        if mask & bit:
            low = low + bit - 2 * bit * lax.rem(low // bit, 2)
    return low


def greet(dp, z, low, masks=(1, 2, 4)):
    barrier = pltpu.get_barrier_semaphore()
    for mask in masks:
        pl.semaphore_signal(barrier, inc=1, device_id={"dp": dp - low + flip(low, mask)}, device_id_type=MESH)
    for other in (1, 2, 3):
        pl.semaphore_signal(barrier, inc=1, device_id={"mp": lax.rem(z + other, NZ)}, device_id_type=MESH)
    pl.semaphore_wait(barrier, len(masks) + 3)


def put(src, dst, ssem, rsem, dev):
    return pltpu.make_async_remote_copy(
        src_ref=src, dst_ref=dst, send_sem=ssem, recv_sem=rsem, device_id=dev, device_id_type=MESH)


def split3(v):
    hi = v.astype(bf16).astype(f32)
    rest = v - hi
    mid = rest.astype(bf16).astype(f32)
    return hi, mid, rest - mid


def extra_rows(base, v, first):
    row = lax.broadcasted_iota(jnp.int32, base.shape, 0)
    out = base
    for i, part in enumerate(split3(v)):
        out = jnp.where(row == first + i, part, out)
    return out.astype(bf16)


def project(w, hid, qt, kt, kk, vt, vv, cos, sin, qaug, kaug, s, c):
    cols = chunk(c)
    t = nt(w[s, 0:QKV], hid[cols])
    co = cos[:, cols]
    si = sin[:, cols]

    def rot(u):
        a = u[0:HD // 2]
        b = u[HD // 2:HD]
        return jnp.concatenate([a * co - b * si, b * co + a * si], axis=0).astype(bf16)

    for h in range(HQ_OWN):
        qt[HQ_OWN * s + h, 0:HD, cols] = rot(t[HD * h:HD * h + HD])
        qt[HQ_OWN * s + h, HD:128, cols] = qaug[:, cols]
    for h in range(KV_OWN):
        g = KV_OWN * s + h
        k = jnp.concatenate([rot(t[QR + HD * h:QR + HD * h + HD]), kaug[:, cols]], axis=0)
        kt[g, :, cols] = k
        kk[g, cols, :] = k.T
        v = t[QR + KR + HD * h:QR + KR + HD * h + HD].astype(bf16)
        v = jnp.concatenate([v, jnp.ones((128 - HD, CH), bf16)], axis=0)
        vt[g, :, cols] = v
        vv[g, cols, :] = v.T


def attend(qt, kk, vt, ho, qaug, g, between):
    ki = lax.broadcasted_iota(jnp.int32, (CH, CH), 0)
    qi = lax.broadcasted_iota(jnp.int32, (CH, CH), 1)
    keep = jnp.concatenate([ki <= qi, ki <= qi], axis=1)

    def scores(qb):
        lo = qb * CH
        nk = lo + CH
        q = jnp.concatenate([qt[2 * g, :, lo:nk], qt[2 * g + 1, :, lo:nk]], axis=1)
        return [nn(kk[g, kb * CH:(kb + 1) * CH, :], q) for kb in range(qb + 1)]

    def rest(qb, st):
        lo = qb * CH
        nk = lo + CH
        st[qb] = jnp.where(keep, st[qb], NEG)
        m = jnp.max(st[qb], axis=0, keepdims=True)
        for kb in range(qb):
            m = jnp.maximum(m, jnp.max(st[kb], axis=0, keepdims=True))
        mc = m * C2
        o = jnp.zeros((128, 2 * CH), f32)
        for kb in range(qb + 1):
            o = o + nn(vt[g, :, kb * CH:(kb + 1) * CH], jnp.exp2(st[kb] * C2 - mc).astype(bf16))
        total = o[HD:HD + 1]
        r = (o[0:HD] / total).astype(bf16)
        back = (mc + jnp.log2(total)) * (-1.0 / C2)
        for h in range(2):
            part = slice(h * CH, (h + 1) * CH)
            ho[pl.ds(pl.multiple_of(g * 2 * HD + h * HD, 32), HD), lo:nk] = r[:, part]
            base = qaug[:, lo:nk].astype(f32)
            qt[2 * g + h, HD:128, lo:nk] = extra_rows(base, back[:, part], SEGS)

    st = scores(0)
    for qb in range(ROW // CH):
        following = scores(qb + 1) if qb + 1 < ROW // CH else None
        rest(qb, st)
        st = following
    between(0)
    between(1)


def angle_tables(lengths, freqs, cos, sin):
    place = lax.broadcasted_iota(jnp.int32, (1, ROW), 1)
    start = jnp.zeros((1, ROW), jnp.int32)
    finish = jnp.int32(0)
    for i in range(SEGS - 1):
        finish = finish + lengths[0, i]
        start = jnp.where(place >= finish, finish, start)
    angles = freqs[...] * (place - start).astype(f32)
    cos[...] = jnp.cos(angles)
    sin[...] = jnp.sin(angles)


def order(z, j):
    places_of = (0, 1, 2, 3), (1, 0, 2, 3), (2, 3, 1, 0), (3, 2, 1, 0)
    s = jnp.int32(0)
    for i, of in enumerate(places_of):
        for k, quarter in enumerate(of):
            if quarter:
                s = s + jnp.where((z == i) & (j == k), quarter, 0)
    return s


EVENTS = {
    3: (("f", 0, 1), ("f", 0, 2), (1, 0, 1)),
    6: ((2, 0, 1),),
    7: (("f", 0, 3), ("s", 1, 0), (1, 0, 2)),
    ("before", 1): ((3, 0, 1), (1, 0, 3), (4, 0, 1)),
    8: ((2, 0, 2), ("f", 1, 1), ("f", 1, 2)),
    11: ((2, 0, 3),),
    13: ((1, 1, 1),),
    15: (("f", 1, 3),),
    ("before", 2): ((3, 0, 2), (4, 0, 2)),
    16: ((1, 1, 2),),
    20: ((3, 0, 3),),
    22: ((1, 1, 3), (2, 1, 1)),
    ("before", 3): ((4, 0, 3),),
    26: ((2, 1, 2),),
    27: ((3, 1, 1),),
    29: ((2, 1, 3), (3, 1, 2)),
    ("before", 4): ((3, 1, 3),),
}
QSLICE = QKV // 8
OSLICE = QR // 8


def forward_kernel(lengths, gains, freqs, x_i, qw_i, kw, vw, ow, cot,
                   mid_o, hid2_o, ho_o, qt_o, kt_o, kk_o, vv_o, w_o, hid1t_o, hid2t_o, cott_o,
                   cos, sin, x, qw, w, hid, ho, qt, kt, kk, vt, vv, qaug, kaug, midb, hidb, hidtb, cb, ctb,
                   zsend, zrecv, xsend, xrecv, ysend, yrecv, csend, crecv, osem, wsem, msem, tsem):
    dp, z, low = places()
    pc, px, py = (partner(low, dp, bit) for bit in (1, 2, 4))
    lx = px - dp + low
    ly = py - dp + low
    lxy = ly + lx - low
    c_at, x_at, y_at = lax.rem(low, 2), lax.rem(low // 2, 2), low // 4
    own = [pltpu.make_async_copy(qw_i, qw, wsem.at[0])]
    own += [pltpu.make_async_copy(src, w.at[z, pl.ds(at, n)], wsem.at[i + 1])
            for i, (src, at, n) in enumerate(((kw, QR, KR), (vw, QR + KR, KR), (ow, QKV, QR)))]
    own += [pltpu.make_async_copy(x_i, x, wsem.at[4])]
    for c in own:
        c.start()
    greet(dp, z, low)
    own[0].wait()
    w[z, 0:QR] = qw[...].T
    own[1].wait()
    own[2].wait()

    def qrows(at, lo=0, hi=QSLICE):
        return pl.ds(pl.multiple_of(at * QSLICE + lo, 16), hi - lo)

    def orows(half, at, core):
        return pl.ds(pl.multiple_of(QKV + half * (QR // 2) + (2 * at + core) * OSLICE, 16), OSLICE)

    def zcopies(part, s, side):
        to = jnp.clip(z + 2 * side - 1, 0, NZ - 1)
        if part == 0:
            slices = ((0, qrows(low)),)
        else:
            slices = ((1, orows(0, y_at, c_at)), (2, orows(1, x_at, c_at)))
        return [put(w.at[s, r], w.at[s, r], zsend.at[i, s, side], zrecv.at[i, s], {"mp": to}) for i, r in slices]

    def send_own(part):
        def go(side):
            for c in zcopies(part, z, side):
                c.start()

        for side in (0, 1):
            pl.when((z < NZ - 1) if side else (z > 0))(functools.partial(go, side))

    send_own(0)
    own[3].wait()
    own[4].wait()

    def copies(part, j, kind):
        s = order(z, j)

        def c(r, sems, semr, i, dev):
            return put(w.at[s, r], w.at[s, r], sems.at[part, j - 1, i], semr.at[part, j - 1, i], {"dp": dev})

        if part == 1:
            if kind == 1:
                return [c(orows(0, y_at, c_at), ysend, yrecv, 0, py), c(orows(1, x_at, c_at), xsend, xrecv, 0, px)]
            return [c(orows(half, at, c_at), csend, crecv, 2 * half + at, pc) for half in (0, 1) for at in (0, 1)]
        cut = QSLICE // 2
        if kind == 1:
            return [c(qrows(low, 0, cut), xsend, xrecv, 0, px), c(qrows(low, cut), ysend, yrecv, 0, py)]
        if kind == 2:
            return [c(qrows(low, 0, cut), ysend, yrecv, 1, py), c(qrows(lx, 0, cut), ysend, yrecv, 2, py),
                    c(qrows(low, cut), xsend, xrecv, 1, px), c(qrows(ly, cut), xsend, xrecv, 2, px)]
        return [c(qrows(at), csend, crecv, i, pc) for i, at in enumerate((low, lx, ly, lxy))]

    def kinds(part):
        return range(1, 3 if part else 4)

    inner = (z > 0) & (z < NZ - 1)

    def pass_on(part, j):
        s = order(z, j)
        return s, jnp.where(s < z, 1, 0)

    def do(kind, part, j):
        if kind == "s":
            send_own(part)
        elif kind == "f":
            @pl.when(inner)
            def _():
                s, side = pass_on(part, j)
                for c in zcopies(part, s, side):
                    c.wait_recv()
                    c.start()
        else:
            if kind == 1:
                @pl.when(jnp.logical_not(inner))
                def _():
                    for c in zcopies(part, order(z, j), 0):
                        c.wait_recv()
            else:
                for c in copies(part, j, kind - 1):
                    c.wait_recv()
            if kind in kinds(part):
                for c in copies(part, j, kind):
                    c.start()

    def beat(step):
        for at, events in EVENTS.items():
            if isinstance(at, int):
                @pl.when(step == at)
                def _(events=events):
                    for e in events:
                        do(*e)

    def before(j):
        for e in EVENTS.get(("before", j), ()):
            do(*e)

    angle_tables(lengths, freqs, cos, sin)
    place = lax.broadcasted_iota(jnp.int32, (1, ROW), 1)
    row = lax.broadcasted_iota(jnp.int32, (128 - HD, ROW), 0)
    segment = jnp.zeros((1, ROW), jnp.int32)
    finish = jnp.int32(0)
    for i in range(SEGS):
        finish = finish + lengths[0, i]
        segment = segment + jnp.where(place >= finish, 1, 0)
    same = row == segment
    qaug[...] = jnp.where(same | (row >= SEGS), 0.0, NEG).astype(bf16)
    kaug[...] = jnp.where(same | ((row >= SEGS) & (row < SEGS + 3)), 1.0, 0.0).astype(bf16)

    def norm(c, _):
        r = chunk(c)
        xx = x[r].astype(f32)
        f = lax.rsqrt(jnp.mean(xx * xx, axis=1, keepdims=True) + eps)
        hid[r] = (xx * f * gains[0:1, :].astype(f32)).astype(bf16)
        return 0

    def turn_copy(i):
        s = lax.rem(i, 2)
        n = ROW // CH
        cols = chunk(lax.rem(i, n))
        return (pltpu.make_async_copy(ctb.at[s], hid1t_o.at[:, cols], tsem.at[0, s]),
                pltpu.make_async_copy(ctb.at[s], cott_o.at[:, cols], tsem.at[0, s]))

    def cot_load(c):
        s = lax.rem(c, 2)
        return pltpu.make_async_copy(cot.at[chunk(c)], cb.at[s], tsem.at[1, s])

    def turn_hid(c, _):
        pl.when(c >= 2)(lambda: turn_copy(c - 2)[0].wait())
        ctb[lax.rem(c, 2)] = hid[chunk(c)].T
        turn_copy(c)[0].start()
        return 0

    def turn_cot(c, _):
        cot_load(c).wait()
        turn_copy(c + 2)[0].wait()
        ctb[lax.rem(c, 2)] = cb[lax.rem(c, 2)].T
        turn_copy(c)[1].start()
        pl.when(c + 2 < ROW // CH)(lambda: cot_load(c + 2).start())
        return 0

    cot_load(0).start()
    cot_load(1).start()
    lax.fori_loop(0, ROW // CH, norm, 0)

    def results(j):
        s = order(z, j)
        h = pl.ds(s * HQ_OWN, HQ_OWN)
        g = pl.ds(s * KV_OWN, KV_OWN)
        r = pl.ds(0, QKV)
        pairs = [(w.at[s, r], w_o.at[s, r]), (qt.at[h], qt_o.at[h]), (kt.at[g], kt_o.at[g]),
                 (kk.at[g], kk_o.at[g]), (vv.at[g], vv_o.at[g])]
        return [pltpu.make_async_copy(a, b, osem.at[j, i]) for i, (a, b) in enumerate(pairs)]

    def quarter(j, _):
        s = order(z, j)
        for i in range(1, NZ):
            @pl.when(j == i)
            def _(i=i):
                if i == 1:
                    lax.fori_loop(0, ROW // CH, turn_hid, 0)
                    lax.fori_loop(0, ROW // CH, turn_cot, 0)
                before(i)

        def one(c, _):
            project(w, hid, qt, kt, kk, vt, vv, cos, sin, qaug, kaug, s, c)
            beat(8 * j + c)
            return 0

        lax.fori_loop(0, ROW // CH, one, 0)

        def two(g, _):
            attend(qt, kk, vt, ho, qaug, KV_OWN * s + g, lambda half: beat(8 * j + 4 + 2 * g + half))
            return 0

        lax.fori_loop(0, KV_OWN, two, 0)
        for c in results(j):
            c.start()
        return 0

    lax.fori_loop(0, NZ, quarter, 0)
    before(NZ)
    last = [pltpu.make_async_copy(ho, ho_o, osem.at[NZ, 0])]
    last += [pltpu.make_async_copy(w.at[s, pl.ds(QKV, QR)], w_o.at[s, pl.ds(QKV, QR)], osem.at[NZ, 1 + s])
             for s in range(NZ)]
    for c in last:
        c.start()

    def mid_copies(c, slot):
        return (pltpu.make_async_copy(midb.at[slot], mid_o.at[chunk(c)], msem.at[0, slot]),
                pltpu.make_async_copy(hidb.at[slot], hid2_o.at[chunk(c)], msem.at[1, slot]),
                pltpu.make_async_copy(hidtb.at[slot], hid2t_o.at[:, chunk(c)], msem.at[2, slot]))

    def out_proj(c, _):
        r = chunk(c)
        slot = lax.rem(c, 2)

        @pl.when(c >= 2)
        def _():
            for m in mid_copies(c - 2, slot):
                m.wait()

        acc = x[r].astype(f32)
        for s in range(NZ):
            acc = acc + tn(ho[QR * s:QR * s + QR, r], w[s, QKV:WR])
        midb[slot] = acc
        f = lax.rsqrt(jnp.mean(acc * acc, axis=1, keepdims=True) + eps)
        h = (acc * f * gains[1:2, :].astype(f32)).astype(bf16)
        hidb[slot] = h
        hidtb[slot] = h.T
        for m in mid_copies(c, slot):
            m.start()
        return 0

    n = ROW // CH
    lax.fori_loop(0, n, out_proj, 0)
    for c in range(max(n - 2, 0), n):
        for m in mid_copies(c, c % 2):
            m.wait()
        turn_copy(c)[1].wait()
    for j in range(NZ):
        for c in results(j):
            c.wait()
    for c in last:
        c.wait()
    for part in range(2):
        def sent(s, side, part=part):
            for c in zcopies(part, s, side):
                c.wait_send()

        for side in (0, 1):
            pl.when((z < NZ - 1) if side else (z > 0))(functools.partial(sent, z, side))
        for j in (1, 2, 3):
            pl.when(inner)(functools.partial(lambda j: sent(*pass_on(part, j)), j))
            for kind in kinds(part):
                for c in copies(part, j, kind):
                    c.wait_send()


def forward(lengths, x, gains, freqs, qw, kw, vw, ow, cot):
    heads = NZ * HQ_OWN
    kv = NZ * KV_OWN
    vm = pltpu.VMEM
    return pl.pallas_call(
        forward_kernel,
        out_shape=(sds((ROW, D), f32), sds((ROW, D), bf16), sds((heads * HD, ROW), bf16),
                   sds((heads, 128, ROW), bf16), sds((kv, 128, ROW), bf16), sds((kv, ROW, 128), bf16),
                   sds((kv, ROW, 128), bf16), sds((NZ, WR, D), bf16), sds((D, ROW), bf16), sds((D, ROW), bf16),
                   sds((D, ROW), bf16)),
        in_specs=[pl.BlockSpec(memory_space=pltpu.SMEM)] + [VM] * 2 + [ANY] * 6,
        out_specs=(ANY,) * 11,
        scratch_shapes=[
            vm((HD // 2, ROW), f32), vm((HD // 2, ROW), f32),
            vm((ROW, D), bf16), vm((D, QR), bf16), vm((NZ, WR, D), bf16), vm((ROW, D), bf16), vm((heads * HD, ROW), bf16),
            vm((heads, 128, ROW), bf16), vm((kv, 128, ROW), bf16), vm((kv, ROW, 128), bf16),
            vm((kv, 128, ROW), bf16), vm((kv, ROW, 128), bf16),
            vm((128 - HD, ROW), bf16), vm((128 - HD, ROW), bf16), vm((2, CH, D), f32), vm((2, CH, D), bf16),
            vm((2, D, CH), bf16), vm((2, CH, D), bf16), vm((2, D, CH), bf16),
            DMA((3, NZ, 2)), DMA((3, NZ)), DMA((2, 3, 3)), DMA((2, 3, 3)), DMA((2, 3, 3)), DMA((2, 3, 3)),
            DMA((2, 3, 4)), DMA((2, 3, 4)), DMA((NZ + 1, 5)), DMA((5,)), DMA((3, 2)), DMA((2, 2))],
        compiler_params=pltpu.CompilerParams(
            collective_id=1, has_side_effects=True, vmem_limit_bytes=60 * 2**20),
        name="attention_forward",
    )(lengths, gains, freqs, x, qw, kw, vw, ow, cot)


def frequencies():
    return jnp.asarray(np.power(np.float32(rope_base), -(np.arange(HD // 2, dtype=np.float32) * 2) / np.float32(HD))[:, None])


class RowSum:
    def __init__(self, z, own, rend, rmid, out, ssem, esem, msem, osem, ring, lag, begun=0, turn=1):
        self.z, self.own, self.ring, self.lag, self.begun, self.turn = z, own, ring, lag, begun, turn
        self.rend, self.rmid, self.out = rend, rmid, out
        self.ssem, self.esem, self.msem, self.osem = ssem, esem, msem, osem

    def who(self, i):
        odd = lax.rem(i // self.turn, 2)
        return 3 * odd, 1 + odd, 2 - odd, 3 - 3 * odd

    def copy(self, kind, i, to, sem=0):
        s = lax.rem(i, self.ring)
        src, dst, rsem = {
            "end": (self.own(i), self.rend.at[s], self.esem),
            "mid": (self.rmid.at[s], self.rmid.at[s], self.msem),
            "out": (self.out.at[s], self.out.at[s], self.osem)}[kind]
        return put(src, dst, self.ssem.at[sem, s], rsem.at[s], {"mp": to})

    def on(self, place, f):
        pl.when(self.z == place)(f)

    def step1(self, i):
        e, o, m, f = self.who(i)
        self.on(e, lambda: self.copy("end", i, o).start())
        self.on(f, lambda: self.copy("end", i, m).start())

    def step2(self, i):
        e, o, m, f = self.who(i)
        s = lax.rem(i, self.ring)

        def go():
            self.copy("end", i, o).wait_recv()
            self.rmid[s] = (self.own(i)[...].astype(f32) + self.rend[s].astype(f32)).astype(bf16)
            self.copy("mid", i, o).start()

        self.on(m, go)

    def step3(self, i):
        e, o, m, f = self.who(i)
        s = lax.rem(i, self.ring)

        def go():
            @pl.when(i >= self.begun)
            def _():
                self.copy("end", i, e).wait_recv()
                self.copy("mid", i, e).wait_recv()

            self.out[s] = (self.own(i)[...].astype(f32) + self.rend[s].astype(f32)
                           + self.rmid[s].astype(f32)).astype(bf16)
            self.copy("out", i, m, 1).start()
            self.copy("out", i, e).start()

        self.on(o, go)

    def step4(self, i):
        e, o, m, f = self.who(i)

        def go():
            self.copy("out", i, o).wait_recv()
            self.copy("out", i, f, 1).start()

        self.on(m, go)

    def arrive(self, i):
        e, o, m, f = self.who(i)
        self.on(e, lambda: self.copy("out", i, o).wait_recv())
        self.on(f, lambda: self.copy("out", i, m).wait_recv())

    def drain(self, i):
        e, o, m, f = self.who(i)

        @pl.when(i >= self.begun)
        def _():
            self.on(e, lambda: self.copy("end", i, o).wait_send())
            self.on(f, lambda: self.copy("end", i, m).wait_send())
            self.on(m, lambda: self.copy("mid", i, o).wait_send())

        def middle():
            self.copy("out", i, f, 1).wait_send()

        def owner():
            self.copy("out", i, m, 1).wait_send()
            self.copy("out", i, e).wait_send()

        self.on(m, middle)
        self.on(o, owner)

    def half_done(self, i):
        e, o, m, f = self.who(i)
        self.on(e, lambda: self.copy("end", i, o).wait_send())
        self.on(f, lambda: self.copy("end", i, m).wait_send())
        self.on(m, lambda: self.copy("mid", i, o).wait_send())

        def owner():
            self.copy("end", i, e).wait_recv()
            self.copy("mid", i, e).wait_recv()

        self.on(o, owner)

    def tick(self, t, count, finish, begun=0, ahead=0):
        def last(i):
            self.arrive(i)
            finish(i)
            self.drain(i)

        for lag, step in ((4, last), (3, self.step4), (2, self.step3), (1, self.step2), (0, self.step1)):
            i = t - lag * self.lag
            lo, hi = (begun, count + ahead) if lag < 2 else (0, count)
            pl.when((i >= lo) & (i < hi))(functools.partial(step, i))


class GradSum:
    def __init__(self, dp, low, width, cut, g, c1, x1, y1, x2, y2, ssem, rsem, emit, wide=False):
        self.pc, self.px, self.py = (partner(low, dp, bit) for bit in (1, 2, 4))
        self.c, self.x, self.y = lax.rem(low, 2), lax.rem(low // 2, 2), low // 4
        self.g, self.c1, self.x1, self.y1, self.x2, self.y2 = g, c1, x1, y1, x2, y2
        self.ssem, self.rsem, self.emit = ssem, rsem, emit
        self.width, self.cut, self.wide = width, cut, wide

    def cols(self, u, lo, hi):
        if self.wide:
            return (pl.ds(pl.multiple_of(u * self.width + lo, 128), hi - lo),)
        return (pl.ds(lo, hi - lo),)

    def part(self, u, *at, lo=None, hi=None):
        lo, hi = (0, self.width) if lo is None else (lo, hi)
        return (() if self.wide else (u,)) + at + self.cols(u, lo, hi)

    def put_block(self, u, k, res):
        self.put_part(u, k, 0, self.width, res)

    def put_part(self, u, k, lo, hi, res):
        self.g[self.part(u, k // 4, (k // 2) % 2, k % 2, slice(None), lo=lo, hi=hi)] = res.astype(bf16)

    def copies(self, u, k):
        g, c, x, y = self.g, self.c, self.x, self.y
        every = slice(None)
        a = dict(lo=0, hi=self.cut)
        b = dict(lo=self.cut, hi=self.width)

        def mk(i, src, dst, dev):
            return put(src, dst, self.ssem.at[u, i], self.rsem.at[u, i], {"dp": dev})

        if k == 0:
            return [mk(0, g.at[self.part(u, every, every, 1 - c, every)], self.c1.at[u], self.pc)]
        if k == 1:
            return [mk(1, g.at[self.part(u, every, 1 - x, c, every, **a)], self.x1.at[u], self.px),
                    mk(2, g.at[self.part(u, 1 - y, every, c, every, **b)], self.y1.at[u], self.py)]
        return [mk(3, g.at[self.part(u, 1 - y, x, c, every, **a)], self.y2.at[u], self.py),
                mk(4, g.at[self.part(u, y, 1 - x, c, every, **b)], self.x2.at[u], self.px)]

    def start(self, u):
        for c in self.copies(u, 0):
            c.start()

    def stage(self, k, u):
        width, cut = self.width, self.cut
        g, c, x, y = self.g, self.c, self.x, self.y
        for cp in self.copies(u, k - 1):
            cp.wait_recv()

        def at(i, j, lo, hi):
            return self.part(u, i, j, c, slice(None), lo=lo, hi=hi)

        def add(i, j, lo, hi, other):
            g[at(i, j, lo, hi)] = (g[at(i, j, lo, hi)].astype(f32) + other.astype(f32)).astype(bf16)

        if k == 1:
            for i in range(2):
                for j in range(2):
                    add(i, j, 0, width, self.c1[u, i, j])
        elif k == 2:
            for i in range(2):
                add(i, x, 0, cut, self.x1[u, i])
                add(y, i, cut, width, self.y1[u, i])
        else:
            self.emit(u, 0, cut, g[at(y, x, 0, cut)].astype(f32) + self.y2[u].astype(f32))
            self.emit(u, cut, width, g[at(y, x, cut, width)].astype(f32) + self.x2[u].astype(f32))
        if k < 3:
            for cp in self.copies(u, k):
                cp.start()

    def drain(self, u):
        for k in range(3):
            for cp in self.copies(u, k):
                cp.wait_send()


def sum_scratch(count, width, cut):
    vm = pltpu.VMEM
    rest = width - cut
    return [vm((count, 2, 2, 2, 192, width), bf16), vm((count, 2, 2, 192, width), bf16),
            vm((count, 2, 192, cut), bf16), vm((count, 2, 192, rest), bf16),
            vm((count, 192, rest), bf16), vm((count, 192, cut), bf16), DMA((count, 5)), DMA((count, 5))]


def ring_scratch(ring, rows):
    vm = pltpu.VMEM
    return [vm((ring, rows, D), bf16), vm((ring, rows, D), bf16), vm((ring, rows, D), bf16),
            DMA((2, ring)), DMA((ring,)), DMA((ring,)), DMA((ring,))]


MLP_UNITS = 6
MLP_WIDTH = 512


def feed_kernel(gains, hid2, cot, mid, hid2t_i, cott_i, gw_i, uw_i, dw_i, w_i,
                mlp_o, gm_o, dot_o, gmlt_o, gain2_o, gate_o, up_o, down_o, end_o, mid_o,
                gw, uw, dw, a3, side, own, hb, cb, tb, mb, cb2, gmb, dotb, gmltb,
                rend, rmid, out, zs, ze, zm, zo,
                g, c1, x1, y1, x2, y2, gs, gr,
                lsem, bsem, tsem, msem, wsem, asem, vsem):
    dp, z, low = places()
    loads = [pltpu.make_async_copy(a, b, lsem.at[i]) for i, (a, b) in enumerate(
        ((gw_i, gw), (uw_i, uw), (dw_i, dw), (hid2t_i, side), (cott_i, side)))]
    oloads = []
    for s in range(NZ):
        for ref, lo, hi in ((dw, 0, D - 2 * CH), (hb.at[0], D - 2 * CH, D - CH), (hb.at[1], D - CH, D)):
            a, b = max(lo, s * QR), min(hi, (s + 1) * QR)
            if a < b:
                oloads.append(pltpu.make_async_copy(
                    w_i.at[s, pl.ds(QKV + a - s * QR, b - a)], ref.at[pl.ds(a - lo, b - a)], vsem.at[len(oloads)]))
    nc = ROW // CH
    nb = ROW // BL
    nj = ROW // 128
    pair = 128 // BL
    per = BL3 // BL

    def chunk_loads(c):
        return [pltpu.make_async_copy(src.at[chunk(c)], dst.at[lax.rem(c, 2)], bsem.at[i, lax.rem(c, 2)])
                for i, (src, dst) in enumerate(((hid2, hb), (cot, cb)))]

    for c in chunk_loads(0):
        c.start()
    for c in loads[:4]:
        c.start()
    greet(dp, z, low)
    def emit(u, lo, hi, v):
        half = lax.rem(u, 2) * MLP_WIDTH
        at = pl.ds(pl.multiple_of(half + lo, 128), hi - lo)
        for i, ref in enumerate((gate_o, up_o, down_o)):
            @pl.when(u // 2 == i)
            def _(ref=ref):
                ref[:, at] = v

    zsum = RowSum(z, lambda i: own.at[chunk(lax.rem(i, nb), BL)], rend, rmid, out, zs, ze, zm, zo, RING, LAG, turn=BL3 // BL)
    gsum = GradSum(dp, low, MLP_WIDTH, MLP_WIDTH // 2, g, c1, x1, y1, x2, y2, gs, gr, emit)
    gain2_o[...] = jnp.zeros_like(gain2_o)

    def gm_loads(j):
        r = chunk(j, 128)
        return [pltpu.make_async_copy(mid.at[r], mb, msem.at[0]),
                pltpu.make_async_copy(cot.at[r], cb2, msem.at[1])]

    def gm_writes(j):
        r = chunk(j, 128)
        s = lax.rem(j, 2)
        return [pltpu.make_async_copy(gmb.at[s], gm_o.at[r], wsem.at[0, s]),
                pltpu.make_async_copy(dotb.at[s], dot_o.at[:, r], wsem.at[1, s]),
                pltpu.make_async_copy(gmltb.at[s], gmlt_o.at[:, r], wsem.at[2, s])]

    def finish_pair(j):
        s = lax.rem(j, 2)
        for c in gm_loads(j):
            c.wait()

        @pl.when(j >= 2)
        def _():
            for c in gm_writes(j - 2):
                c.wait()

        gh = jnp.concatenate([out[lax.rem(j * pair + k, RING)] for k in range(pair)], axis=0).astype(f32)
        m = mb[...]
        f = lax.rsqrt(jnp.mean(m * m, axis=1, keepdims=True) + eps)
        n = m * f
        gn = gh * n
        gain2_o[...] += jnp.sum(gn, axis=0, keepdims=True)
        ga = gains[1:2, :].astype(f32)
        gm = cb2[...].astype(f32) + f * (gh * ga - n * jnp.mean(gn * ga, axis=1, keepdims=True))
        gmb[s] = gm
        low_gm = gm.astype(bf16)
        gmltb[s] = low_gm.T

        @pl.when(j == 0)
        def _():
            for c in oloads:
                c.wait()

        dotb[s, 0:D - 2 * CH] = nt(dw[...], low_gm).astype(bf16)
        for k in range(2):
            first = D - (2 - k) * CH
            dotb[s, first:first + CH] = nt(hb[k], low_gm).astype(bf16)
        for c in gm_writes(j):
            c.start()

        @pl.when(j + 1 < nj)
        def _():
            for c in gm_loads(j + 1):
                c.start()

    def finish(i):
        pl.when(lax.rem(i, pair) == pair - 1)(lambda: finish_pair(i // pair))

    for c in gm_loads(0):
        c.start()

    def tick(t):
        for k in range(per):
            zsum.tick(per * t + k, nb, finish, ahead=AHEAD * per)

    again = pltpu.make_async_copy(mlp_o.at[pl.ds(0, AHEAD * BL3)], own.at[pl.ds(0, AHEAD * BL3)], asem)

    def mlp_write(c):
        return pltpu.make_async_copy(tb.at[lax.rem(c, 2)], mlp_o.at[chunk(c)], tsem.at[lax.rem(c, 2)])

    def mlp_chunk(c, _):
        r = chunk(c)
        s = lax.rem(c, 2)
        for cp in chunk_loads(c):
            cp.wait()

        @pl.when(c + 1 < nc)
        def _():
            for cp in chunk_loads(c + 1):
                cp.start()

        @pl.when(c == 0)
        def _():
            loads[0].wait()
            loads[1].wait()
            loads[2].wait()

        gate = nn(hb[s], gw[...])
        upper = nn(hb[s], uw[...])
        ga = nt(cb[s], dw[...])
        sigma = 1.0 / (1.0 + jnp.exp(-gate))
        silu = gate * sigma
        gg = (ga * upper * sigma * (1.0 + gate * (1.0 - sigma))).astype(bf16)
        gu = (ga * silu).astype(bf16)
        act = (silu * upper).astype(bf16)
        a3[0, r] = gg
        a3[1, r] = gu
        a3[2, r] = act
        own[r] = (nt(gg, gw[...]) + nt(gu, uw[...])).astype(bf16)
        tick(2 * c)

        @pl.when(c >= 2)
        def _():
            mlp_write(c - 2).wait()

        tb[s] = nn(act, dw[...]).astype(bf16)
        mlp_write(c).start()
        tick(2 * c + 1)
        return 0

    def unit(u):
        @pl.when(u == 0)
        def _():
            loads[3].wait()

        @pl.when(u == 4)
        def _():
            loads[4].start()
            loads[4].wait()

        which = u // 2
        cols = chunk(lax.rem(u, 2), MLP_WIDTH)
        rhs = a3[which, :, cols]
        for k in range(8):
            gsum.put_block(u, k, nn(side[k * 192:(k + 1) * 192], rhs))
        gsum.start(u)

    def beat(t, _):
        first = 2 * nc
        u = t - first

        @pl.when(t == first)
        def _():
            for c in range(max(nc - 2, 0), nc):
                mlp_write(c).wait()

        @pl.when(t == nb // per)
        def _():
            again.start()
            again.wait()

        pl.when(u < MLP_UNITS)(lambda: unit(u))
        tick(t)
        for k, lag in ((3, 10), (2, 6), (1, 2)):
            v = u - lag
            pl.when((v >= 0) & (v < MLP_UNITS))(functools.partial(gsum.stage, k, v))
        return 0

    lax.fori_loop(0, nc, mlp_chunk, 0)
    for c in oloads:
        c.start()
    lax.fori_loop(2 * nc, (nb + 4 * LAG + per - 1) // per, beat, 0)

    def drains(u, _):
        gsum.drain(u)
        return 0

    lax.fori_loop(0, MLP_UNITS, drains, 0)
    for j in range(nj - 2, nj):
        for c in gm_writes(j):
            c.wait()
    keep = []
    for i in range(AHEAD * per):
        zsum.half_done(nb + i)
        s = (nb + i) % RING
        keep += [pltpu.make_async_copy(rend.at[s], end_o.at[i], zs.at[0, s]),
                 pltpu.make_async_copy(rmid.at[s], mid_o.at[i], zs.at[1, s])]
    for c in keep:
        c.start()
    for c in keep:
        c.wait()


def feed(gains, hid2, cot, mid, hid2t, cott, gw, uw, dw, w):
    vm = pltpu.VMEM
    ff = gw.shape[1]
    return pl.pallas_call(
        feed_kernel,
        out_shape=(sds((ROW, D), bf16), sds((ROW, D), f32), sds((D, ROW), bf16), sds((D, ROW), bf16),
                   sds((1, D), f32), sds((D // 8, ff), f32), sds((D // 8, ff), f32), sds((D // 8, ff), f32),
                   sds((AHEAD * BL3 // BL, BL, D), bf16), sds((AHEAD * BL3 // BL, BL, D), bf16)),
        in_specs=[VM] + [ANY] * 9,
        out_specs=(ANY, ANY, ANY, ANY, VM, VM, VM, VM, ANY, ANY),
        scratch_shapes=[
            vm((D, ff), bf16), vm((D, ff), bf16), vm((ff, D), bf16), vm((3, ROW, ff), bf16),
            vm((D, ROW), bf16), vm((ROW, D), bf16),
            vm((2, CH, D), bf16), vm((2, CH, D), bf16), vm((2, CH, D), bf16),
            vm((128, D), f32), vm((128, D), bf16), vm((2, 128, D), f32), vm((2, D, 128), bf16),
            vm((2, D, 128), bf16)]
        + ring_scratch(RING, BL) + sum_scratch(MLP_UNITS, MLP_WIDTH, MLP_WIDTH // 2)
        + [DMA((5,)), DMA((2, 2)), DMA((2,)), DMA((2,)), DMA((3, 2)), DMA, DMA((6,))],
        compiler_params=pltpu.CompilerParams(
            collective_id=2, has_side_effects=True, vmem_limit_bytes=63 * 2**20),
        name="feed_forward",
    )(gains, hid2, cot, mid, hid2t, cott, gw, uw, dw, w)


RING3 = 10
LAG3 = 2
WIDTH = QR
BEATS = 8
CUT = 128


def unrotate(u, co, si):
    a = u[0:HD // 2]
    b = u[HD // 2:HD]
    return jnp.concatenate([a * co + b * si, b * co - a * si], axis=0).astype(bf16)


def attend_back(qk, kk, vv, dot, ho, dk, dv, gt, cos, sin, g, gg, qb):
    lo = qb * CH
    hi = lo + CH
    heads = NZ * HQ_OWN * 128
    q = jnp.concatenate([qk[pl.ds(pl.multiple_of((2 * g + h) * 128, 128), 128), lo:hi] for h in range(2)], axis=1)
    parts = []
    for h in range(2):
        do = dot[pl.ds(pl.multiple_of((2 * g + h) * HD, 32), HD), lo:hi]
        o = ho[pl.ds(pl.multiple_of((2 * g + h) * HD, 32), HD), lo:hi]
        delta = jnp.sum(do.astype(f32) * o.astype(f32), axis=0, keepdims=True)
        extra = extra_rows(jnp.zeros((128 - HD, CH), f32), -delta, 0)
        parts.append(jnp.concatenate([do, extra], axis=0))
    do = jnp.concatenate(parts, axis=1)
    do_t = do.T
    q_t = q.T
    dq = jnp.zeros((128, 2 * CH), f32)
    for kb in range(qb + 1):
        ks = slice(kb * CH, (kb + 1) * CH)
        p = jnp.exp2(nn(kk[g, ks, :], q) * C2)
        if kb == qb:
            ki = lax.broadcasted_iota(jnp.int32, (CH, CH), 0)
            qi = lax.broadcasted_iota(jnp.int32, (CH, CH), 1)
            keep = jnp.concatenate([ki <= qi, ki <= qi], axis=1)
            p = jnp.where(keep, p, 0.0)
        ds = (p * nn(vv[g, ks, :], do)).astype(bf16)
        dvb = nn(p.astype(bf16), do_t)
        dkb = nn(ds, q_t)
        if kb == qb:
            dv[ks, :] = dvb
            dk[ks, :] = dkb
        else:
            dv[ks, :] += dvb
            dk[ks, :] += dkb
        dq = dq + nn(qk[pl.ds(pl.multiple_of(heads + g * 128, 128), 128), ks], ds)
    first = (g // KV_OWN) * QKV + gg * 2 * HD
    for h in range(2):
        at = pl.ds(pl.multiple_of(first + h * HD, 32), HD)
        gt[at, lo:hi] = unrotate(dq[0:HD, h * CH:(h + 1) * CH] * SCALE, cos[:, lo:hi], sin[:, lo:hi])


def backward_kernel(groups, lengths, gains, freqs, gain2_i, x, mid, mlp, gm, dot_i, gmlt, hid1t, ho_i, qt_i, kt_i, kk_i, vv_i, w_i, end_i, mid_i,
                    out_o, xg_o, qg_o, kg_o, vg_o, og_o, gains_o,
                    cos, sin, w, gbuf, ho, qk, kk, vv, dk, dv, gt, dot, ga1, own, mb2, ob2, xb, gb, ob,
                    rend, rmid, out, zs, ze, zm, zo,
                    c1, x1, y1, x2, y2, gs, gr, og, oc1, ox1, oy1, ox2, oy2, ogs, ogr, tb, gsend, grecv,
                    lsem, bsem, wsem, psem, osem, isem, tsem, ssem, rsem, asem):
    dp, z, low = places()
    qrows = NZ * HQ_OWN * 128
    loads = [pltpu.make_async_copy(ho_i, ho, lsem.at[1]),
             pltpu.make_async_copy(dot_i, dot, lsem.at[0]),
             pltpu.make_async_copy(kk_i, kk, lsem.at[2]),
             pltpu.make_async_copy(vv_i, vv, lsem.at[3])]
    loads += [pltpu.make_async_copy(qt_i, qk.at[pl.ds(0, qrows)], lsem.at[12]),
              pltpu.make_async_copy(kt_i, qk.at[pl.ds(qrows, NZ * KV_OWN * 128)], lsem.at[13])]
    wloads = [pltpu.make_async_copy(w_i.at[s, pl.ds(0, QKV)], w.at[s], lsem.at[14 + s]) for s in range(NZ)]
    late = [pltpu.make_async_copy(hid1t, qk.at[pl.ds(0, D)], lsem.at[18])]
    nb = ROW // BL3
    nt_blocks = ROW // TB

    def own_load(i):
        s = lax.rem(i, RING3)
        return pltpu.make_async_copy(mlp.at[chunk(i, BL3)], own.at[s], isem.at[s])

    def mid_load(i):
        s = lax.rem(i, 2)
        return pltpu.make_async_copy(mid.at[chunk(i, BL3)], mb2.at[s], osem.at[0, s])

    def out_write(i):
        s = lax.rem(i, 2)
        return pltpu.make_async_copy(ob2.at[s], out_o.at[chunk(i, BL3)], osem.at[1, s])

    def turned_load(k):
        return pltpu.make_async_copy(gmlt.at[pl.ds(k * 192, 192)], tb.at[k % 2], tsem.at[k % 2])

    begun = [pltpu.make_async_copy(src, dst.at[pl.ds(0, AHEAD)], asem.at[i])
             for i, (src, dst) in enumerate(((end_i, rend), (mid_i, rmid)))]
    for c in begun:
        c.start()
    for i in range(2 * LAG3 + 2):
        own_load(i).start()
    mid_load(0).start()
    turned_load(0).start()
    turned_load(1).start()
    for c in loads:
        c.start()
    greet(dp, z, low, range(1, 8))
    angle_tables(lengths, freqs, cos, sin)
    zsum = RowSum(z, lambda i: own.at[lax.rem(i, RING3)], rend, rmid, out, zs, ze, zm, zo, RING3, LAG3, AHEAD)

    def emit(u, lo, hi, v):
        if u == 0:
            qg_o[:, lo:hi] = v
            return
        for ref, first in ((kg_o, 0), (vg_o, KR)):
            a, b = max(lo, first), min(hi, first + KR)
            if a < b:
                ref[:, a - first:b - first] = v[:, a - lo:b - lo]

    def emit_o(u, lo, hi, v):
        og_o[:, lo:hi] = v

    gsum = GradSum(dp, low, WIDTH, CUT, gbuf, c1, x1, y1, x2, y2, gs, gr, emit, True)
    osum = GradSum(dp, low, WIDTH, CUT, og, oc1, ox1, oy1, ox2, oy2, ogs, ogr, emit_o)

    def finish(i):
        mid_load(i).wait()
        s = lax.rem(i, 2)

        @pl.when(i >= 2)
        def _():
            out_write(i - 2).wait()

        ob2[s] = (mb2[s] + out[lax.rem(i, RING3)].astype(f32)).astype(bf16)
        out_write(i).start()

        @pl.when(i + 1 < nb)
        def _():
            mid_load(i + 1).start()

    def tick(beat):
        t = beat + 2 * LAG3
        pl.when((t >= AHEAD) & (t < nb))(lambda: own_load(t).wait())
        zsum.tick(t, nb, finish, begun=AHEAD)
        pl.when(t + 2 < nb)(lambda: own_load(t + 2).start())

    for i in range(AHEAD):
        own_load(i).wait()
    for c in begun:
        c.wait()
    tick(0)
    tick(1)
    loads[0].wait()
    o_rows = ho[pl.ds(pl.multiple_of(z * QR, 128), QR), :]
    for k in range(8):
        turned_load(k).wait()
        osum.put_block(0, k, nt(tb[k % 2], o_rows))
        if k + 2 < 8:
            turned_load(k + 2).start()
    osum.start(0)
    tick(2)
    for c in loads[1:]:
        c.wait()
    for c in wloads:
        c.start()

    def quarter(s, _):
        def one(gg, _):
            g = KV_OWN * s + gg
            for qb in range(ROW // CH):
                attend_back(qk, kk, vv, dot, ho, dk, dv, gt, cos, sin, g, gg, qb)
                done = 10 * g + qb * (qb + 1) // 2
                was, now = (done * BEATS) // 80, ((done + qb + 1) * BEATS) // 80
                pl.when(now > was)(functools.partial(tick, 3 + was))
            first = pl.multiple_of(s * QKV + QR + gg * HD, 32)
            gt[pl.ds(first, HD), :] = unrotate(dk[...].T[0:HD] * SCALE, cos[...], sin[...])
            gt[pl.ds(pl.multiple_of(first + KR, 32), HD), :] = dv[...].T[0:HD].astype(bf16)
            return 0

        lax.fori_loop(0, KV_OWN, one, 0)
        for k in (1, 2, 3):
            pl.when(s == k - 1)(functools.partial(osum.stage, k, 0))
        return 0

    lax.fori_loop(0, NZ, quarter, 0)
    beats = 3 + BEATS
    for c in late:
        c.start()
    for c in wloads + late:
        c.wait()

    for u in range(2):
        rhs = gt[pl.ds(pl.multiple_of(z * QKV + u * WIDTH, 128), WIDTH), :]
        for k in range(8):
            gsum.put_block(u, k, nt(qk[k * 192:(k + 1) * 192, :], rhs))
        gsum.start(u)
        tick(beats + u)
    beats += 2

    def tail_loads(b, slot):
        r = chunk(b, TB)
        return [pltpu.make_async_copy(x.at[r], xb.at[slot], bsem.at[0, slot]),
                pltpu.make_async_copy(gm.at[r], gb.at[slot], bsem.at[1, slot])]

    def out_copy(b, slot):
        return pltpu.make_async_copy(ob.at[slot], xg_o.at[chunk(b, TB)], psem.at[slot])

    for c in tail_loads(0, 0):
        c.start()
    ga1[...] = jnp.zeros_like(ga1)

    def tail(b, _):
        slot = lax.rem(b, 2)

        @pl.when(b + 1 < nt_blocks)
        def _():
            for c in tail_loads(b + 1, 1 - slot):
                c.start()

        r = chunk(b, TB)
        acc = jnp.zeros((TB, D), f32)
        for s in range(NZ):
            acc = acc + tn(gt[QKV * s:QKV * s + QKV, r], w[s])
        for c in tail_loads(b, slot):
            c.wait()

        @pl.when(b >= 2)
        def _():
            out_copy(b - 2, slot).wait()

        xx = xb[slot].astype(f32)
        f = lax.rsqrt(jnp.mean(xx * xx, axis=1, keepdims=True) + eps)
        n = xx * f
        gn = acc * n
        ga1[...] += jnp.sum(gn, axis=0, keepdims=True)
        ga = gains[0:1, :].astype(f32)
        res = gb[slot] + f * (acc * ga - n * jnp.mean(gn * ga, axis=1, keepdims=True))
        ob[slot] = res.astype(bf16)
        out_copy(b, slot).start()
        tick(beats + b)
        pl.when(b == 0)(lambda: (gsum.stage(1, 0), gsum.stage(1, 1)) and None)
        pl.when(b == 1)(lambda: gsum.stage(2, 0))
        pl.when(b == 2)(lambda: gsum.stage(2, 1))
        pl.when(b == 3)(lambda: gsum.stage(3, 0))
        return 0

    lax.fori_loop(0, nt_blocks, tail, 0)
    beats += nt_blocks

    def gains_copy(mask):
        to = flip(low, mask)
        return put(gsend.at[to], grecv.at[low], ssem.at[mask], rsem.at[mask], {"dp": dp - low + to})

    share = D // 8 // groups
    for k in range(8):
        for i, v in enumerate((ga1, gain2_i)):
            gsend[k, i:i + 1, 0:D // 8] = jnp.concatenate(
                [v[:, (g * 8 + k) * share:(g * 8 + k + 1) * share] for g in range(groups)], axis=1)
    for mask in range(1, 8):
        gains_copy(mask).start()

    def rest(t, _):
        tick(t)
        return 0

    ends = nb + 2 * LAG3
    if beats < ends:
        lax.fori_loop(beats, ends, rest, 0)
    gsum.stage(3, 1)
    total = gsend[low]
    for mask in range(1, 8):
        gains_copy(mask).wait_recv()
        total = total + grecv[flip(low, mask)]
    gains_o[...] = total
    for mask in range(1, 8):
        gains_copy(mask).wait_send()
    for u in range(2):
        gsum.drain(u)
    osum.drain(0)
    for b in range(nt_blocks - 2, nt_blocks):
        out_copy(b, b % 2).wait()
    for i in (nb - 2, nb - 1):
        out_write(i).wait()


def backward(groups, lengths, gains, freqs, gain2_sum, x, mid, mlp, gm, dot, gmlt, hid1t, ho, qt, kt, kk, vv, w, ends, mids):
    vm = pltpu.VMEM
    heads = NZ * HQ_OWN
    kv = NZ * KV_OWN
    return pl.pallas_call(
        functools.partial(backward_kernel, groups),
        out_shape=(sds((ROW, D), bf16), sds((ROW, D), bf16), sds((D // 8, QR), f32), sds((D // 8, KR), f32),
                   sds((D // 8, KR), f32), sds((D // 8, QR), f32), sds((8, 256), f32)),
        in_specs=[pl.BlockSpec(memory_space=pltpu.SMEM)] + [VM] * 3 + [ANY] * 15,
        out_specs=(ANY, ANY) + (VM,) * 5,
        scratch_shapes=[
            vm((HD // 2, ROW), f32), vm((HD // 2, ROW), f32), vm((NZ, QKV, D), bf16), vm((2, 2, 2, 192, 2 * WIDTH), bf16), vm((heads * HD, ROW), bf16),
            vm(((heads + kv) * 128, ROW), bf16), vm((kv, ROW, 128), bf16), vm((kv, ROW, 128), bf16),
            vm((ROW, 128), f32), vm((ROW, 128), f32), vm((NZ * QKV, ROW), bf16),
            vm((heads * HD, ROW), bf16), vm((1, D), f32),
            vm((RING3, BL3, D), bf16), vm((2, BL3, D), f32), vm((2, BL3, D), bf16),
            vm((2, TB, D), bf16), vm((2, TB, D), f32), vm((2, TB, D), bf16)]
        + ring_scratch(RING3, BL3) + sum_scratch(2, WIDTH, CUT)[1:] + sum_scratch(1, WIDTH, CUT)
        + [vm((2, 192, ROW), bf16), vm((8, 8, 256), f32), vm((8, 8, 256), f32),
           DMA((19,)), DMA((2, 2)), DMA((2,)), DMA((2,)), DMA((2, 2)), DMA((RING3,)), DMA((2,)), DMA((8,)), DMA((8,)), DMA((2,))],
        compiler_params=pltpu.CompilerParams(
            collective_id=3, has_side_effects=True, vmem_limit_bytes=63 * 2**20),
        name="attention_backward",
    )(lengths, gains, freqs, gain2_sum, x, mid, mlp, gm, dot, gmlt, hid1t, ho, qt, kt, kk, vv, w,
      ends, mids)


def by_block(v, groups):
    if groups == 1:
        return v
    rows, cols = v.shape
    return v.reshape(groups, 8, rows // (8 * groups), cols).transpose(1, 0, 2, 3).reshape(rows, cols)


def body(groups, inputs, lengths, q_weight, k_weight, v_weight, o_weight, gate_weight, up_weight, down_weight,
         attn_gain, mlp_gain, cotangent):
    x = inputs.reshape(ROW, D)
    cot = cotangent.reshape(ROW, D)
    first = lax.broadcasted_iota(jnp.int32, (2, D), 0) == 0
    gains = jnp.where(first, attn_gain[None, :], mlp_gain[None, :])
    freqs = frequencies()
    mid, hid2, ho, qt, kt, kk, vv, w, hid1t, hid2t, cott = forward(
        lengths, x, gains, freqs, q_weight, k_weight.T, v_weight.T, o_weight, cot)
    mlp, gm, dot, gmlt, gain2_sum, gate_g, up_g, down_g, ends, mids = feed(
        gains, hid2, cot, mid, by_block(hid2t, groups), by_block(cott, groups), gate_weight, up_weight, down_weight, w)
    output, input_grad, q_g, k_g, v_g, o_g, gain_sums = backward(
        groups, lengths, gains, freqs, gain2_sum, x, mid, mlp, gm, dot, by_block(gmlt, groups), by_block(hid1t, groups),
        ho, qt.reshape(-1, ROW), kt.reshape(-1, ROW), kk, vv, w, ends.reshape(-1, BL3, D), mids.reshape(-1, BL3, D))
    grads = [q_g, k_g, v_g, o_g, gate_g, up_g, down_g]
    if groups > 1:
        same = [[g * 8 + low for g in range(groups)] for low in range(8)]
        def over(v, dim=0):
            return lax.psum_scatter(v, "dp", scatter_dimension=dim, axis_index_groups=same, tiled=True)

        grads = [over(v) for v in grads]
        gain_sums = over(gain_sums[:, 0:D // 8], 1)
    output, input_grad, *grads = hand_over(gain_sums, output, input_grad, *grads)
    grads[3], grads[6] = grads[3].T, grads[6].T
    return (output.reshape(1, ROW, D), input_grad.reshape(1, ROW, D), *grads)


def hand_over_kernel(n, sums, *refs):
    first, second = refs[2 * n:2 * n + 2]
    refs = refs[:2 * n] + refs[2 * n + 2:]
    held, load, store = refs[2 * n:3 * n], refs[3 * n], refs[3 * n + 1]
    first[...] = sums[0, 0:first.shape[0]]
    second[...] = sums[1, 0:second.shape[0]]
    pieces = []
    for i in range(n):
        rows = held[i].shape[0]
        parts = 4 if rows % 64 == 0 and rows > 512 else 1
        pieces += [(i, pl.ds(p * (rows // parts), rows // parts)) for p in range(parts)]
    come = [pltpu.make_async_copy(refs[i].at[r], held[i].at[r], load.at[k]) for k, (i, r) in enumerate(pieces)]
    go = [pltpu.make_async_copy(held[i].at[r], refs[n + i].at[r], store.at[k]) for k, (i, r) in enumerate(pieces)]
    for c in come:
        c.start()
    for a, b in zip(come, go):
        a.wait()
        b.start()
    for c in go:
        c.wait()


def hand_over(sums, *arrays):
    n = len(arrays)
    keep = arrays[-1].shape[0]
    return pl.pallas_call(
        functools.partial(hand_over_kernel, n),
        out_shape=tuple(sds(v.shape, v.dtype) for v in arrays) + (sds((keep,), f32),) * 2,
        in_specs=[VM] + [ANY] * n,
        out_specs=(ANY,) * n + (VM,) * 2,
        scratch_shapes=[pltpu.VMEM(v.shape, v.dtype) for v in arrays] + [DMA((4 * n,)), DMA((4 * n,))],
        compiler_params=pltpu.CompilerParams(vmem_limit_bytes=63 * 2**20),
        name="hand_over",
    )(sums, *arrays)


def solution(mesh):
    row = P("dp", None, None)
    in_specs = (row, P("dp", None), P(None, "mp"), P(None, "mp"), P(None, "mp"), P("mp", None),
                P(None, "mp"), P(None, "mp"), P("mp", None), P(), P(), row)
    out_specs = (row, row, P("dp", "mp"), P("dp", "mp"), P("dp", "mp"), P("mp", "dp"),
                 P("dp", "mp"), P("dp", "mp"), P("mp", "dp"), P("dp"), P("dp"))
    return jax.shard_map(functools.partial(body, mesh.shape["dp"] // 8), mesh=mesh, in_specs=in_specs,
                         out_specs=out_specs, check_vma=False)
```
